32 devices in a mesh: lat: 8 (over y, x, core), lon: 4 (over z).
Axes of the slice: x: 2, y: 2, z: 4, core: 2. Of those that a mesh axis runs over, the one named last changes fastest.
Arguments:
- tracers: float32 [5, 1, 768, 512], P(None, None, 'lat', 'lon'), may hold values from 0.2 to 2
- offsets: int32 [768, 512], P('lat', 'lon'), may hold values from 0 to 255, as said below
- fraction: float32 [768, 512], P('lat', 'lon'), may hold values from 0 to 0.95
- courant_north: float32 [768, 512], P('lat', 'lon'), may hold values from 0 to 0.9
Outputs:
- advected: float32 [5, 1, 768, 512], P(None, None, 'lat', 'lon')
The draws below stay inside these ranges and needn't reach their ends.
Inputs may be any that keep to these rules, and one draw needn't show every extreme that they name: Let k = min(r, 767 - r) for row r. Rows with k < 24 have offsets from 128 to 255, the largest reached in row 0; rows with 24 <= k < 48 have offsets at most 64, reached in row 24; all other rows have offsets at most 8, reached in row 48. Offsets of adjacent faces g and g + 1 of a row differ by at most one.
All inputs are finite; a program needn't handle non-finite values.
Results may differ from the reference program's by a relative error of at most 0.0003.
Values sent between devices are 32-bit elements; how exact they have to be, the bound alone decides.
No kernel may reach another device: no remote copies, remote signals or barrier semaphores. Data moves between devices by JAX's collectives and lax.ppermute only.
A program may use at most 64 MiB of HBM per device.

```python
import jax
import jax.numpy as jnp
from jax import lax

NTR = 5
LEV = 1
LON_DEV = 128
MID = 8
REACH = 64
POLAR = 24
NLAT = 768
NLON = 512


def draw_offsets(key, part):
    key_start = jax.random.fold_in(key, 21)
    key_step = jax.random.fold_in(key, 22)
    row_index = jnp.arange(NLAT, dtype=jnp.int32)
    pole_distance = jnp.minimum(row_index, NLAT - 1 - row_index)
    polar_rows = pole_distance < POLAR
    band_rows = (pole_distance >= POLAR) & (pole_distance < 2 * POLAR)
    lowest = jnp.where(polar_rows, LON_DEV, 0).astype(jnp.int32)
    highest = jnp.where(polar_rows, 2 * LON_DEV - 1, jnp.where(band_rows, REACH, MID)).astype(jnp.int32)
    raw_start = jax.random.randint(key_start, (NLAT,), 0, 1 << 20, dtype=jnp.int32)
    row_start = (lowest + raw_start % (highest - lowest + 1)).astype(jnp.int32)
    row_start = jnp.where(row_index == 0, 2 * LON_DEV - 1, row_start)
    row_start = jnp.where(row_index == POLAR, REACH, row_start)
    row_start = jnp.where(row_index == 2 * POLAR, MID, row_start).astype(jnp.int32)
    steps_taken = jax.random.randint(key_step, (NLAT, NLON), -1, 2, dtype=jnp.int32)
    walk_value = (row_start[:, None] + jnp.cumsum(steps_taken, axis=1) - steps_taken[:, 0:1]).astype(jnp.int32)
    return jnp.clip(walk_value, lowest[:, None], highest[:, None]).astype(jnp.int32)


def level_of(rng, dims, cuts, least, top_value):
    level = 1.0
    for position, shards_of in cuts:
        steps = jax.random.uniform(jax.random.fold_in(jax.random.fold_in(rng, 6), position), (shards_of,), jnp.float32, least / len(cuts), top_value / len(cuts))
        level = level * jnp.repeat(jnp.exp(steps), dims[position] // shards_of).reshape((-1,) + (1,) * (len(dims) - 1 - position))
    return level


def setup_inputs(seed: int = 0) -> dict:
    splits = jax.random.split(jax.random.key(seed), 5)
    return {
        "tracers": jnp.clip(0.2 + 1.8 * jax.random.uniform(splits[0], (NTR, LEV, NLAT, NLON), jnp.float32) ** level_of(splits[0], (NTR, LEV, NLAT, NLON), ((2, 8), (3, 4)), -0.2, 0.2), 0.2, 2.0),
        "offsets": draw_offsets(jax.random.fold_in(splits[4], 71), 0),
        "fraction": jnp.clip(0.95 * jax.random.uniform(splits[2], (NLAT, NLON), jnp.float32) ** level_of(splits[2], (NLAT, NLON), ((0, 8), (1, 4)), -0.2, 0.2), 0.0, 0.95),
        "courant_north": jnp.clip(0.9 * jax.random.uniform(splits[3], (NLAT, NLON), jnp.float32) ** level_of(splits[3], (NLAT, NLON), ((0, 8), (1, 4)), -0.2, 0.2), 0.0, 0.9),
    }


wide_weight = 7.0 / 12.0
narrow_weight = 1.0 / 12.0


def frac_flux(courant, right_edge, edge_jump, curvature):
    return courant * (right_edge - 0.5 * courant * (edge_jump - (1.0 - (2.0 / 3.0) * courant) * curvature))


def reference(tracers, offsets, fraction, courant_north):
    blocks = NLON // LON_DEV
    face_index = jnp.arange(NLON, dtype=jnp.int32)
    block_own = face_index // LON_DEV
    start_cell = face_index[None, :] - offsets
    block_src = jnp.floor_divide(start_cell, LON_DEV)
    distance = block_own[None, :] - block_src
    first_mask = (distance >= 1).astype(jnp.float32)
    second_mask = (distance >= 2).astype(jnp.float32)
    start_wrapped = jnp.mod(start_cell, NLON).astype(jnp.int32)
    depart_cell = jnp.mod(start_cell - 1, NLON).astype(jnp.int32)
    prev_one = jnp.mod(block_own - 1, blocks).astype(jnp.int32)
    prev_two = jnp.mod(block_own - 2, blocks).astype(jnp.int32)
    later = lax.broadcasted_iota(jnp.int32, (LON_DEV, LON_DEV), 1)
    earlier = lax.broadcasted_iota(jnp.int32, (LON_DEV, LON_DEV), 0)
    strictly_before = (earlier < later).astype(jnp.float32)
    courant = jnp.concatenate([jnp.zeros((1, NLON), jnp.float32), courant_north[1:], jnp.zeros((1, NLON), jnp.float32)], axis=0)

    def one_slice(field):
        left_edge = wide_weight * (jnp.roll(field, 1, 1) + field) - narrow_weight * (jnp.roll(field, 2, 1) + jnp.roll(field, -1, 1))
        right_edge = wide_weight * (field + jnp.roll(field, -1, 1)) - narrow_weight * (jnp.roll(field, 1, 1) + jnp.roll(field, -2, 1))
        edge_jump = right_edge - left_edge
        curvature = 6.0 * (field - 0.5 * (left_edge + right_edge))
        grouped = field.reshape(NLAT, blocks, LON_DEV)
        prefix = jnp.dot(grouped, strictly_before, precision=lax.Precision.HIGHEST).reshape(NLAT, NLON)
        block_total = jnp.sum(grouped, axis=2)
        total_one = jnp.take(block_total, prev_one, axis=1)
        total_two = jnp.take(block_total, prev_two, axis=1)
        base_value = jnp.take_along_axis(prefix, start_wrapped, axis=1) - (total_one * first_mask + total_two * second_mask)
        part_right = jnp.take_along_axis(right_edge, depart_cell, axis=1)
        part_jump = jnp.take_along_axis(edge_jump, depart_cell, axis=1)
        part_curve = jnp.take_along_axis(curvature, depart_cell, axis=1)
        zonal_flux = (prefix - base_value) + frac_flux(fraction, part_right, part_jump, part_curve)
        after_zonal = field - (jnp.roll(zonal_flux, -1, 1) - zonal_flux)
        padded = jnp.pad(after_zonal, ((3, 3), (0, 0)))

        def row_window(shift_by):
            return padded[2 + shift_by:3 + shift_by + NLAT]

        merid_left = wide_weight * (row_window(-1) + row_window(0)) - narrow_weight * (row_window(-2) + row_window(1))
        merid_right = wide_weight * (row_window(0) + row_window(1)) - narrow_weight * (row_window(-1) + row_window(2))
        merid_jump = merid_right - merid_left
        merid_curve = 6.0 * (row_window(0) - 0.5 * (merid_left + merid_right))
        merid_flux = frac_flux(courant, merid_right, merid_jump, merid_curve)
        return after_zonal - (merid_flux[1:] - merid_flux[:-1])

    stacked = tracers.reshape(NTR * LEV, NLAT, NLON)
    result = lax.map(one_slice, stacked)
    return result.reshape(NTR, LEV, NLAT, NLON)
```

```python
import functools

import jax
import jax.numpy as jnp
from jax import lax
from jax.experimental import pallas as pl
from jax.experimental.pallas import tpu as pltpu
from jax.sharding import PartitionSpec as P

WIDE = 7.0 / 12.0
NARROW = 1.0 / 12.0
POLAR = 24
BAND = 24
SEG = 24
WEST = 11
EAST0 = 12
FAR0 = 14
OFF_LANE = 120
FRAC_LANE = 121

f32 = jnp.float32
i32 = jnp.int32
VMEM = pltpu.VMEM


def lanes(shape):
    return lax.broadcasted_iota(i32, shape, 1)


def rolled(value, steps):
    steps = steps % value.shape[1]
    return pltpu.roll(value, steps, 1) if steps else value


def pick(table, index):
    return jnp.take_along_axis(table, index, axis=1, mode="promise_in_bounds")


def parabola(c, right, left, centre):
    jump = right - left
    curve = 6.0 * centre - 3.0 * (left + right)
    return c * (right - 0.5 * c * (jump - (1.0 - (2.0 / 3.0) * c) * curve))


def running_sum(value):
    count = value.shape[1]
    shape = (count, count)
    upto = lax.broadcasted_iota(i32, shape, 0) <= lax.broadcasted_iota(i32, shape, 1)
    ones = upto.astype(jnp.bfloat16)
    high = value.astype(jnp.bfloat16)
    low = (value - high.astype(f32)).astype(jnp.bfloat16)
    return jnp.dot(high, ones, preferred_element_type=f32) + jnp.dot(
        low, ones, preferred_element_type=f32
    )


def edges(value):
    right = WIDE * (value + rolled(value, -1)) - NARROW * (rolled(value, 1) + rolled(value, -2))
    return right, rolled(right, 1)


def edges_between(value, west, east):
    lane = lanes(value.shape)
    last = value.shape[1] - 1
    back_one = jnp.where(lane < 1, rolled(west, 1), rolled(value, 1))
    back_two = jnp.where(lane < 2, rolled(west, 2), rolled(value, 2))
    on_one = jnp.where(lane > last - 1, rolled(east, -1), rolled(value, -1))
    on_two = jnp.where(lane > last - 2, rolled(east, -2), rolled(value, -2))
    right = WIDE * (value + on_one) - NARROW * (back_one + on_two)
    left = WIDE * (back_one + value) - NARROW * (back_two + on_one)
    return right, left


def pack_kernel(tracers, offsets, fraction, to_east, to_west, pole_one, pole_two):
    depth, row_count, cells = tracers.shape
    shape = (row_count, cells)
    lane = lanes(shape)
    place, tracer = lane % SEG, lane // SEG
    east_message = jnp.zeros(shape, f32)
    west_message = jnp.where(
        lane == OFF_LANE,
        rolled(offsets[...].astype(f32), OFF_LANE),
        jnp.where(lane == FRAC_LANE, rolled(fraction[...], FRAC_LANE), 0.0),
    )
    for t in range(depth):
        field = tracers[t]
        mine = tracer == t
        east_message = jnp.where(
            mine & (place < WEST), rolled(field, t * SEG + WEST - cells), east_message
        )
        near = mine & (place >= EAST0) & (place < FAR0)
        far = mine & (place >= FAR0) & (place < FAR0 + 2)
        west_message = jnp.where(near, rolled(field, t * SEG + EAST0), west_message)
        west_message = jnp.where(far, rolled(field, t * SEG + FAR0 + 2 - cells), west_message)
    to_east[...] = east_message
    to_west[...] = west_message
    south = lax.axis_index("lat") == 0
    start = pl.multiple_of(jnp.where(south, 0, row_count - POLAR - BAND), 8)
    inner = pl.multiple_of(jnp.where(south, 0, row_count - POLAR), 8)
    pole_one[...] = tracers[:, pl.ds(start, POLAR + BAND), :]
    pole_two[...] = tracers[:, pl.ds(inner, POLAR), :]


def own_kernel(tracers, offsets, fraction, flux, seam_west, seam_east, seam_offsets, seam_fraction):
    depth, row_count, cells = tracers.shape
    shape = (row_count, cells)
    lane = lanes(shape)
    place, tracer = lane % SEG, lane // SEG
    offset = offsets[...]
    courant = fraction[...]
    index = (lane - offset - 1) & (cells - 1)
    west_rows = jnp.zeros(shape, f32)
    east_rows = jnp.zeros(shape, f32)
    for t in range(depth):
        field = tracers[t]
        right, left = edges(field)
        sums = running_sum(field)
        flux[t] = (
            sums
            - field
            - pick(sums, index)
            + parabola(courant, pick(right, index), pick(left, index), pick(field, index))
        )
        mine = tracer == t
        west_rows = jnp.where(
            mine & (place >= WEST) & (place < 2 * WEST + 1), rolled(field, t * SEG + WEST), west_rows
        )
        east_rows = jnp.where(
            mine & (place < EAST0), rolled(field, t * SEG + EAST0 - cells), east_rows
        )
    seam_west[...] = west_rows
    seam_east[...] = east_rows
    first = (place - WEST) & (cells - 1)
    final = jnp.full(shape, cells - 1, i32)
    seam_offsets[0] = pick(offset, first)
    seam_offsets[1] = pick(offset, final)
    seam_fraction[0] = pick(courant, first)
    seam_fraction[1] = pick(courant, final)


def seam_flux(rows, offset, courant, place):
    cells = rows.shape[1]
    right, left = edges(rows)
    sums = rows
    for step in (1, 2, 4, 8, 16):
        sums = sums + jnp.where(place >= step, rolled(sums, step), 0.0)
    index = (lanes(rows.shape) - offset - 1) & (cells - 1)
    return (
        sums
        - rows
        - pick(sums, index)
        + parabola(courant, pick(right, index), pick(left, index), pick(rows, index))
    )


def seam_kernel(
    tracers, flux, seam_west, seam_east, seam_offsets, seam_fraction, courant_north,
    from_west, from_east, after, message_a, message_b,
):
    depth, row_count, cells = tracers.shape
    shape = (row_count, cells)
    lane = lanes(shape)
    place = lane % SEG
    west_rows = jnp.where(place < WEST, from_west[...], seam_west[...])
    west_flux = seam_flux(west_rows, seam_offsets[0], seam_fraction[0], place)
    received = from_east[...]
    east_rows = jnp.where(place < EAST0, seam_east[...], received)
    next_face = place == EAST0
    next_offset = pick(received, jnp.full(shape, OFF_LANE, i32)).astype(i32)
    next_fraction = pick(received, jnp.full(shape, FRAC_LANE, i32))
    east_flux = seam_flux(
        east_rows,
        jnp.where(next_face, next_offset, seam_offsets[1]),
        jnp.where(next_face, next_fraction, seam_fraction[1]),
        place,
    )
    even = lax.axis_index("lat") % 2 == 0
    for t in range(depth):
        west_faces = rolled(west_flux, -(t * SEG + WEST))
        east_faces = rolled(east_flux, cells - 1 - (t * SEG + EAST0 - 1))
        face = jnp.where(
            lane < WEST, west_faces, jnp.where(lane == cells - 1, east_faces, flux[t])
        )
        following = rolled(jnp.where(lane == 0, east_faces, face), -1)
        after[t] = tracers[t] - (following - face)
        top = after[t, row_count - 3 :]
        bottom = after[t, :3]
        message_a[3 * t : 3 * t + 3] = jnp.where(even, top, bottom)
        message_b[3 * t : 3 * t + 3] = jnp.where(even, bottom, top)
    message_a[3 * depth : 3 * depth + 1] = courant_north[:1]
    message_b[3 * depth : 3 * depth + 1] = courant_north[:1]


def polar_rows(own, west, west_two, near, far, offset, courant, next_offset, next_courant):
    cells = own.shape[1]
    lane = lanes(own.shape)
    right_one, left_one = edges_between(west, west_two, own)
    right_two, left_two = edges_between(west_two, far, west)
    sums = running_sum(own)
    sums_one = running_sum(west)
    sums_two = running_sum(west_two)
    total, total_one, total_two = (s[:, cells - 1 :] for s in (sums, sums_one, sums_two))
    source = lane - offset - 1
    index = source & (cells - 1)
    near_block = source >= -cells

    def both(one, two):
        return jnp.where(near_block, pick(one, index), pick(two, index))

    face = (
        sums
        - own
        + total_one
        - jnp.where(near_block, pick(sums_one, index), pick(sums_two, index) - total_two)
        + parabola(courant, both(right_one, right_two), both(left_one, left_two), both(west, west_two))
    )
    index = (cells - 1 - next_offset) & (cells - 1)
    last = (
        total
        + total_one
        - pick(sums_one, index)
        + parabola(next_courant, pick(right_one, index), pick(left_one, index), pick(west, index))
    )
    following = rolled(jnp.where(lane == 0, last, face), -1)
    return own - (following - face)


def band_rows(own, west, near, offset, courant, next_offset, next_courant):
    cells = own.shape[1]
    lane = lanes(own.shape)
    right, left = edges_between(own, west, near)
    right_one, left_one = edges_between(west, west, own)
    sums = running_sum(own)
    sums_one = running_sum(west)
    total, total_one = sums[:, cells - 1 :], sums_one[:, cells - 1 :]
    source = lane - offset - 1
    index = source & (cells - 1)
    inside = source >= 0

    def both(here, there):
        return jnp.where(inside, pick(here, index), pick(there, index))

    face = (
        sums
        - own
        - both(sums, sums_one - total_one)
        + parabola(courant, both(right, right_one), both(left, left_one), both(own, west))
    )
    index = (cells - 1 - next_offset) & (cells - 1)
    last = (
        total
        - pick(sums, index)
        + parabola(next_courant, pick(right, index), pick(left, index), pick(own, index))
    )
    following = rolled(jnp.where(lane == 0, last, face), -1)
    return own - (following - face)


def merid_kernel(
    lat_count, tracers, offsets, fraction, courant_north, after, from_east, from_far, pole_one, pole_two,
    message_a, message_b, out, wide, courant_rows,
):
    depth, row_count, cells = tracers.shape
    lat = lax.axis_index("lat")
    south, north = lat == 0, lat == lat_count - 1
    even = lat % 2 == 0
    for t in range(depth):
        wide[t, 8 : 8 + row_count] = after[t]
        below = jnp.where(even, message_b[3 * t : 3 * t + 3], message_a[3 * t : 3 * t + 3])
        above = jnp.where(even, message_a[3 * t : 3 * t + 3], message_b[3 * t : 3 * t + 3])
        wide[t, 5:8] = below
        wide[t, 8 + row_count : 11 + row_count] = above
    last = 3 * depth
    courant_rows[7 : 7 + row_count] = courant_north[...]
    courant_rows[7 + row_count : 8 + row_count] = jnp.where(
        even, message_a[last : last + 1], message_b[last : last + 1]
    )

    @pl.when(south)
    def _():
        courant_rows[7:8] = jnp.zeros((1, cells), f32)

    @pl.when(south | north)
    def _():
        def part(first, in_window, count, polar):
            rows = pl.ds(pl.multiple_of(first, 8), count)
            window = pl.ds(pl.multiple_of(in_window, 8), count)
            offset, courant = offsets[rows], fraction[rows]
            east, far_cells = from_east[rows], from_far[rows]
            shape = east.shape
            next_offset = pick(east, jnp.full(shape, OFF_LANE, i32)).astype(i32)
            next_courant = pick(east, jnp.full(shape, FRAC_LANE, i32))
            for t in range(depth):
                own = tracers[t, rows]
                near = rolled(east, -(t * SEG + EAST0))
                common = (offset, courant, next_offset, next_courant)
                if polar:
                    far = rolled(far_cells, cells - 2 - (t * SEG + FAR0))
                    result = polar_rows(own, pole_one[t, window], pole_two[t], near, far, *common)
                else:
                    result = band_rows(own, pole_one[t, window], near, *common)
                wide[t, pl.ds(pl.multiple_of(first + 8, 8), count)] = result

        base = row_count - POLAR - BAND
        part(jnp.where(south, 0, base + BAND), jnp.where(south, 0, BAND), POLAR, True)
        part(jnp.where(south, POLAR, base), jnp.where(south, POLAR, 0), BAND, False)

    courant = courant_rows[...]
    for t in range(depth):
        value = wide[t]
        size = row_count + 16
        right = WIDE * (value + pltpu.roll(value, size - 1, 0)) - NARROW * (
            pltpu.roll(value, 1, 0) + pltpu.roll(value, size - 2, 0)
        )
        left = pltpu.roll(right, 1, 0)
        face = parabola(courant, right, left, value)
        result = value - (face - pltpu.roll(face, 1, 0))
        out[t] = result[8 : 8 + row_count]


def in_vmem(*values):
    return [pltpu.with_memory_space_constraint(value, VMEM) for value in values]


def whole(count):
    return [pl.BlockSpec(memory_space=VMEM)] * count


def on_device(lat_count, lon_count, tracers, offsets, fraction, courant_north):
    tracer_count, level_count, row_count, cells = tracers.shape
    depth = tracer_count * level_count
    shape = (row_count, cells)
    field = tracers.reshape(depth, row_count, cells)
    field, offsets, fraction, courant_north = in_vmem(field, offsets, fraction, courant_north)

    def along_lon(value, steps, lats=range(lat_count)):
        pairs = [
            (l * lon_count + o, l * lon_count + (o + steps) % lon_count)
            for l in lats
            for o in range(lon_count)
        ]
        return lax.ppermute(value, ("lat", "lon"), pairs)

    def along_lat(value, first):
        pairs = []
        for l in range(first, lat_count - 1, 2):
            for o in range(lon_count):
                low, high = l * lon_count + o, (l + 1) * lon_count + o
                pairs += [(low, high), (high, low)]
        return lax.ppermute(value, ("lat", "lon"), pairs)

    to_east, to_west, pole_one, pole_two = pl.pallas_call(
        pack_kernel,
        out_shape=[
            VMEM(shape, f32),
            VMEM(shape, f32),
            VMEM((depth, POLAR + BAND, cells), f32),
            VMEM((depth, POLAR, cells), f32),
        ],
        in_specs=whole(3),
        out_specs=whole(4),
        name="pack",
    )(field, offsets, fraction)
    from_west = along_lon(to_east, 1)
    from_east = along_lon(to_west, -1)
    poles = (0, lat_count - 1)
    from_far = from_east if lon_count == 4 else along_lon(to_west, 3)
    pole_one = along_lon(pole_one, 1, poles)
    pole_two = along_lon(pole_two, 2, poles)

    own = pl.pallas_call(
        own_kernel,
        out_shape=[
            VMEM((depth, row_count, cells), f32),
            VMEM(shape, f32),
            VMEM(shape, f32),
            VMEM((2, row_count, cells), i32),
            VMEM((2, row_count, cells), f32),
        ],
        in_specs=whole(3),
        out_specs=whole(5),
        name="own",
    )(field, offsets, fraction)

    after, message_a, message_b = pl.pallas_call(
        seam_kernel,
        out_shape=[
            VMEM((depth, row_count, cells), f32),
            VMEM((3 * depth + 1, cells), f32),
            VMEM((3 * depth + 1, cells), f32),
        ],
        in_specs=whole(9),
        out_specs=whole(3),
        name="seam",
    )(field, *in_vmem(*own), courant_north, *in_vmem(from_west, from_east))
    message_b = along_lat(message_b, 1)
    message_a = along_lat(message_a, 0)

    out = pl.pallas_call(
        functools.partial(merid_kernel, lat_count),
        out_shape=jax.ShapeDtypeStruct((depth, row_count, cells), f32),
        in_specs=whole(11),
        out_specs=pl.BlockSpec(memory_space=VMEM),
        scratch_shapes=[
            VMEM((depth, row_count + 16, cells), f32),
            VMEM((row_count + 16, cells), f32),
        ],
        name="merid",
    )(
        field, offsets, fraction, courant_north,
        *in_vmem(after, from_east, from_far, pole_one, pole_two, message_a, message_b),
    )
    return out.reshape(tracers.shape)


def solution(mesh):
    placed = (P(None, None, "lat", "lon"), P("lat", "lon"), P("lat", "lon"), P("lat", "lon"))
    return jax.shard_map(
        functools.partial(on_device, mesh.shape["lat"], mesh.shape["lon"]),
        mesh=mesh,
        in_specs=placed,
        out_specs=P(None, None, "lat", "lon"),
        check_vma=False,
    )
```

```python
import functools

import jax
import jax.numpy as jnp
from jax import lax
from jax.experimental import pallas as pl
from jax.experimental.pallas import tpu as pltpu
from jax.sharding import PartitionSpec as P

POLAR = 24
BAND = 24
POLE = POLAR + BAND
WEST = 12
SEG = 24
FACES = 11
OFF_LANE = 120
FRAC_LANE = 121
EDGE = 8

f32 = jnp.float32
bf16 = jnp.bfloat16
i32 = jnp.int32
VMEM = pltpu.VMEM


def lanes(shape):
    return lax.broadcasted_iota(i32, shape, 1)


def rolled(value, steps):
    steps = steps % value.shape[1]
    return pltpu.roll(value, steps, 1) if steps else value


def pick(table, index):
    return jnp.take_along_axis(table, index, axis=1, mode="promise_in_bounds")


def parabola(c, right, left, centre):
    jump = right - left
    curve = 6.0 * centre - 3.0 * (left + right)
    return c * (right - 0.5 * c * (jump - (1.0 - (2.0 / 3.0) * c) * curve))


def times(value, matrix):
    high = value.astype(bf16)
    low = (value - high.astype(f32)).astype(bf16)
    return jnp.dot(high, matrix, preferred_element_type=f32) + jnp.dot(
        low, matrix, preferred_element_type=f32
    )


def edge_weights(gap):
    def weight(gap):
        inner = (gap == 0) | (gap == 1)
        outer = (gap == -1) | (gap == 2)
        return jnp.where(inner, 7.0, jnp.where(outer, -1.0, 0.0))

    return weight(gap), weight(gap + 1)


def split(table, cells):
    return [table[:, i : i + cells] for i in range(0, table.shape[1], cells)]


def pack_kernel(
    tracers, offsets, fraction, courant, field, offset, part, north, packed, pole_one, pole_two, sems
):
    depth, row_count, cells = field.shape
    copies = [
        pltpu.make_async_copy(source, target, sems.at[i])
        for i, (source, target) in enumerate(
            ((tracers, field), (offsets, offset), (fraction, part), (courant, north))
        )
    ]
    for copy in copies:
        copy.start()
    for copy in copies[:3]:
        copy.wait()
    shape = (row_count, cells)
    lane = lanes(shape)
    message = jnp.where(
        lane == OFF_LANE,
        rolled(offset[...].astype(f32), OFF_LANE),
        jnp.where(lane == FRAC_LANE, rolled(part[...], FRAC_LANE), 0.0),
    )
    for t in range(depth):
        mine = (lane >= t * SEG) & (lane < (t + 1) * SEG)
        message = jnp.where(mine, rolled(field[t], t * SEG + WEST), message)
    packed[...] = message
    south = lax.axis_index("lat") == 0
    outer = pl.multiple_of(jnp.where(south, 0, row_count - POLE), 8)
    inner = pl.multiple_of(jnp.where(south, 0, row_count - POLAR), 8)
    pole_one[...] = field[:, pl.ds(outer, POLE), :]
    pole_two[...] = field[:, pl.ds(inner, POLAR), :]
    copies[3].wait()


def own_kernel(
    field, offset, part, flux, seam_index, seam_part, block_matrix, seam_matrix
):
    depth, row_count, cells = field.shape
    shape = (cells, cells)
    source = lax.broadcasted_iota(i32, shape, 0)
    target = lax.broadcasted_iota(i32, shape, 1)
    gap = source - target
    upto = jnp.where(gap <= 0, 1.0, 0.0)
    right, left = edge_weights(gap)
    block_matrix[cells : 2 * cells] = jnp.concatenate(
        [upto, right, left, jnp.ones(shape, f32)], axis=1
    ).astype(bf16)
    zeros = jnp.zeros(shape, f32)
    for first, away in ((0, -cells), (2 * cells, cells)):
        block_matrix[first : first + cells] = jnp.concatenate(
            [zeros, *edge_weights(gap + away), zeros], axis=1
        ).astype(bf16)
    together = source // SEG == target // SEG
    seam_matrix[...] = jnp.concatenate([jnp.where(together, upto, 0.0), right, left], axis=1).astype(bf16)

    shape = (row_count, cells)
    lane = lanes(shape)
    place = lane % SEG
    offsets = offset[...]
    courant = part[...]
    index = (lane - offsets - 1) & (cells - 1)
    own = field[...].reshape(depth * row_count, cells)
    tables = times(own, block_matrix[cells : 2 * cells, : 3 * cells])
    for t in range(depth):
        rows = slice(t * row_count, (t + 1) * row_count)
        sums, right, left = split(tables[rows], cells)
        value = field[t]
        flux[t] = (
            sums
            - value
            - pick(sums, index)
            + parabola(
                courant, pick(right, index) * (1 / 12), pick(left, index) * (1 / 12), pick(value, index)
            )
        )
    first = (place - WEST) & (cells - 1)
    final = jnp.full(shape, cells - 1, i32)
    seam_index[0] = (lane - pick(offsets, first) - 1) & (cells - 1)
    seam_index[1] = (lane - pick(offsets, final) - 1) & (cells - 1)
    seam_part[0] = pick(courant, first)
    seam_part[1] = pick(courant, final)


def rows_after(field, flux, packed, seam_index, seam_part, from_west, from_east, seam_matrix, parts):
    def take(ref, *lead):
        return jnp.concatenate([ref[(*lead, part)] for part in parts], axis=0)

    mine, west, east = take(packed), take(from_west), take(from_east)
    count, cells = mine.shape
    shape = mine.shape
    lane = lanes(shape)
    place = lane % SEG
    near = place < WEST
    rows = jnp.concatenate([jnp.where(near, west, mine), jnp.where(near, mine, east)], axis=0)
    next_face = place == WEST
    next_offset = pick(east, jnp.full(shape, OFF_LANE, i32)).astype(i32)
    next_part = pick(east, jnp.full(shape, FRAC_LANE, i32))
    next_index = (lane - next_offset - 1) & (cells - 1)
    index = jnp.concatenate(
        [take(seam_index, 0), jnp.where(next_face, next_index, take(seam_index, 1))], axis=0
    )
    courant = jnp.concatenate(
        [take(seam_part, 0), jnp.where(next_face, next_part, take(seam_part, 1))], axis=0
    )
    sums, right, left = split(times(rows, seam_matrix[...]), cells)
    faces = (
        sums
        - rows
        - pick(sums, index)
        + parabola(
            courant, pick(right, index) * (1 / 12), pick(left, index) * (1 / 12), pick(rows, index)
        )
    )
    east_faces = faces[count:]
    both = jnp.where(place == WEST - 1, east_faces, faces[:count])
    outside = (lane < FACES) | (lane == cells - 1)
    results = []
    for t in range(field.shape[0]):
        steps = -(t * SEG + WEST)
        face = jnp.where(outside, rolled(both, steps), take(flux, t))
        following = jnp.where(lane == cells - 1, rolled(east_faces, steps - 1), rolled(face, -1))
        results.append(take(field, t) - (following - face))
    return results


def edge_kernel(
    field, flux, packed, seam_index, seam_part, seam_matrix, north, from_east, from_west,
    message_a, message_b,
):
    depth, row_count, _ = field.shape
    parts = (pl.ds(0, EDGE), pl.ds(row_count - EDGE, EDGE))
    after = rows_after(
        field, flux, packed, seam_index, seam_part, from_west, from_east, seam_matrix, parts
    )
    even = lax.axis_index("lat") % 2 == 0
    for t in range(depth):
        bottom, top = after[t][:3], after[t][2 * EDGE - 3 :]
        message_a[3 * t : 3 * t + 3] = jnp.where(even, top, bottom)
        message_b[3 * t : 3 * t + 3] = jnp.where(even, bottom, top)
    message_a[3 * depth : 3 * depth + 1] = north[:1]
    message_b[3 * depth : 3 * depth + 1] = north[:1]


def polar_rows(tables, own, west, west_two, offset, courant, next_offset, next_courant):
    cells = own.shape[1]
    lane = lanes(own.shape)
    (sums, _, _, total), one, two = tables
    source = lane - offset - 1
    index = source & (cells - 1)
    close = source >= -cells

    def both(here, there):
        return jnp.where(close, pick(here, index), pick(there, index))

    face = (
        sums
        - own
        + one[3]
        - both(one[0], two[0] - two[3])
        + parabola(
            courant, both(one[1], two[1]) * (1 / 12), both(one[2], two[2]) * (1 / 12), both(west, west_two)
        )
    )
    index = (cells - 1 - next_offset) & (cells - 1)
    last = parabola(next_courant, one[1] * (1 / 12), one[2] * (1 / 12), west) - one[0]
    last = total + one[3] + pick(last, index)
    following = rolled(jnp.where(lane == 0, last, face), -1)
    return own - (following - face)


def band_rows(tables, own, west, offset, courant, next_offset, next_courant):
    cells = own.shape[1]
    lane = lanes(own.shape)
    here, one = tables
    source = lane - offset - 1
    index = source & (cells - 1)
    inside = source >= 0

    def both(inner, outer):
        return jnp.where(inside, pick(inner, index), pick(outer, index))

    face = (
        here[0]
        - own
        - both(here[0], one[0] - one[3])
        + parabola(
            courant, both(here[1], one[1]) * (1 / 12), both(here[2], one[2]) * (1 / 12), both(own, west)
        )
    )
    index = (cells - 1 - next_offset) & (cells - 1)
    last = parabola(next_courant, here[1] * (1 / 12), here[2] * (1 / 12), own) - here[0]
    last = here[3] + pick(last, index)
    following = rolled(jnp.where(lane == 0, last, face), -1)
    return own - (following - face)


def merid_flux(wide, t, courant, first, count):
    cell = [wide[t, first + k : first + k + count] for k in (-3, -2, -1, 0, 1)]
    left = (7.0 * (cell[1] + cell[2]) - (cell[0] + cell[3])) * (1 / 12)
    right = (7.0 * (cell[2] + cell[3]) - (cell[1] + cell[4])) * (1 / 12)
    return parabola(courant, right, left, cell[2])


def middle_kernel(
    lat_count, field, offset, part, north, flux, packed, seam_index, seam_part, seam_matrix, block_matrix,
    from_east, from_far, from_west, pole_one, pole_two, wide, out, result, faces, sems,
):
    depth, row_count, cells = field.shape
    lat = lax.axis_index("lat")
    south = lat == 0
    after = rows_after(
        field, flux, packed, seam_index, seam_part, from_west, from_east, seam_matrix, (pl.ds(0, row_count),)
    )
    for t in range(depth):
        wide[t] = after[t]

    @pl.when(south | (lat == lat_count - 1))
    def _():
        base = pl.multiple_of(jnp.where(south, 0, row_count - POLE), 8)
        polar = pl.multiple_of(jnp.where(south, 0, BAND), 8)
        band = pl.multiple_of(jnp.where(south, POLAR, 0), 8)
        polar_at = pl.ds(pl.multiple_of(base + polar, 8), POLAR)
        band_at = pl.ds(pl.multiple_of(base + band, 8), BAND)

        def stacked(ref, rows):
            return ref[:, rows, :].reshape(-1, cells)

        def unpacked(ref, rows, lane):
            value = ref[rows]
            return jnp.concatenate([rolled(value, lane - t * SEG) for t in range(depth)], axis=0)

        own_polar, own_band = stacked(field, polar_at), stacked(field, band_at)
        west_polar = stacked(pole_one, pl.ds(polar, POLAR))
        west_band = stacked(pole_one, pl.ds(band, BAND))
        west_two = pole_two[...].reshape(-1, cells)
        far = unpacked(from_far, polar_at, cells - WEST)
        east = unpacked(from_east, band_at, -WEST)
        rows = jnp.concatenate(
            [
                jnp.concatenate(three, axis=1)
                for three in (
                    (west_polar, own_polar, own_polar),
                    (west_two, west_polar, own_polar),
                    (far, west_two, west_polar),
                    (west_band, own_band, east),
                    (west_band, west_band, own_band),
                )
            ],
            axis=0,
        )
        tables = times(rows, block_matrix[...])

        def table(which, t):
            first = (which * depth + t) * POLAR
            return split(tables[first : first + POLAR], cells)

        for rows_at, is_polar in ((polar_at, True), (band_at, False)):
            shape = (POLAR, cells)
            beyond = from_east[rows_at]
            common = (
                offset[rows_at],
                part[rows_at],
                pick(beyond, jnp.full(shape, OFF_LANE, i32)).astype(i32),
                pick(beyond, jnp.full(shape, FRAC_LANE, i32)),
            )
            for t in range(depth):
                at = slice(t * POLAR, (t + 1) * POLAR)
                if is_polar:
                    wide[t, rows_at] = polar_rows(
                        (table(0, t), table(1, t), table(2, t)),
                        own_polar[at], west_polar[at], west_two[at], *common,
                    )
                else:
                    wide[t, rows_at] = band_rows(
                        (table(3, t), table(4, t)), own_band[at], west_band[at], *common
                    )

    count = row_count - 2 * EDGE
    copies = []
    for t in range(depth):
        faces[t, :count] = merid_flux(wide, t, north[EDGE : EDGE + count], EDGE, count)
        last = merid_flux(wide, t, north[EDGE + count : EDGE + count + 1], EDGE + count, 1)
        faces[t, count : count + 1] = last
        result[t] = wide[t, EDGE : EDGE + count] - (faces[t, 1 : 1 + count] - faces[t, :count])
        copies.append(
            pltpu.make_async_copy(result.at[t], out.at[t, pl.ds(EDGE, count)], sems.at[t])
        )
        copies[-1].start()
    for copy in copies:
        copy.wait()


def last_kernel(lat_count, wide, north, message_b, message_a, partial, out, low, high, result, sems):
    del partial
    depth, row_count, cells = wide.shape
    lat = lax.axis_index("lat")
    even = lat % 2 == 0
    south, top = lat == 0, lat == lat_count - 1
    end = 3 * depth
    north_courant = jnp.where(even, message_a[end : end + 1], message_b[end : end + 1])
    north_courant = jnp.where(top, 0.0, north_courant)
    first_row = lax.broadcasted_iota(i32, (EDGE, cells), 0)
    low_courant = jnp.where(south & (first_row == 0), 0.0, north[:EDGE])
    high_next = jnp.concatenate([north[row_count - EDGE + 1 :], north_courant], axis=0)
    for t in range(depth):
        rows = slice(3 * t, 3 * t + 3)
        from_a, from_b = message_a[rows], message_b[rows]
        low[t, EDGE - 3 : EDGE] = jnp.where(south, 0.0, jnp.where(even, from_b, from_a))
        low[t, EDGE : 3 * EDGE] = wide[t, : 2 * EDGE]
        high[t, : 2 * EDGE] = wide[t, row_count - 2 * EDGE :]
        high[t, 2 * EDGE : 2 * EDGE + 3] = jnp.where(top, 0.0, jnp.where(even, from_a, from_b))
    for t in range(depth):
        south_face = merid_flux(low, t, low_courant, EDGE, EDGE)
        north_face = merid_flux(low, t, north[1 : EDGE + 1], EDGE + 1, EDGE)
        result[0, t] = low[t, EDGE : 2 * EDGE] - (north_face - south_face)
        south_face = merid_flux(high, t, north[row_count - EDGE :], EDGE, EDGE)
        north_face = merid_flux(high, t, high_next, EDGE + 1, EDGE)
        result[1, t] = high[t, EDGE : 2 * EDGE] - (north_face - south_face)
    copies = [
        pltpu.make_async_copy(result.at[i], out.at[:, pl.ds(first, EDGE)], sems.at[i])
        for i, first in enumerate((0, row_count - EDGE))
    ]
    for copy in copies:
        copy.start()
    for copy in copies:
        copy.wait()


def cost(microseconds):
    return pl.CostEstimate(
        flops=int(microseconds * 1e8), bytes_accessed=int(microseconds * 3e6), transcendentals=0
    )


def in_vmem(*values):
    return [pltpu.with_memory_space_constraint(value, VMEM) for value in values]


def whole(count):
    return [pl.BlockSpec(memory_space=VMEM)] * count


def anywhere(count):
    return [pl.BlockSpec(memory_space=pl.ANY)] * count


def on_device(lat_count, lon_count, tracers, offsets, fraction, courant_north):
    tracer_count, level_count, row_count, cells = tracers.shape
    depth = tracer_count * level_count
    shape = (row_count, cells)
    stack = (depth, row_count, cells)
    dma = pltpu.SemaphoreType.DMA

    def along_lon(value, steps, everywhere=True):
        pairs = []
        for l in range(lat_count):
            from_pole = min(l, lat_count - 1 - l)
            for o in range(lon_count):
                if everywhere or from_pole == 0 or lat_count % 2 or lon_count % 2:
                    target = (l, (o + steps) % lon_count)
                else:
                    target = (l, o ^ 1) if from_pole == 1 else (l ^ 1, o)
                pairs.append((l * lon_count + o, target[0] * lon_count + target[1]))
        return lax.ppermute(value, ("lat", "lon"), pairs)

    def along_lat(value, first):
        pairs = []
        for l in range(first, lat_count if lat_count % 2 == 0 else lat_count - 1, 2):
            for o in range(lon_count):
                low, high = l * lon_count + o, (l + 1) % lat_count * lon_count + o
                pairs += [(low, high), (high, low)]
        return lax.ppermute(value, ("lat", "lon"), pairs)

    field, offset, part, north, packed, pole_one, pole_two = in_vmem(
        *pl.pallas_call(
            pack_kernel,
            out_shape=[
                VMEM(stack, f32),
                VMEM(shape, i32),
                VMEM(shape, f32),
                VMEM(shape, f32),
                VMEM(shape, f32),
                VMEM((depth, POLE, cells), f32),
                VMEM((depth, POLAR, cells), f32),
            ],
            in_specs=anywhere(4),
            out_specs=whole(7),
            scratch_shapes=[dma((4,))],
            cost_estimate=cost(1.0),
            name="pack",
        )(tracers.reshape(stack), offsets, fraction, courant_north)
    )
    from_west = along_lon(packed, 1)
    from_east = along_lon(packed, -1)
    from_far = from_east if lon_count == 4 else along_lon(packed, 3)

    flux, seam_index, seam_part, block_matrix, seam_matrix = in_vmem(
        *pl.pallas_call(
            own_kernel,
            out_shape=[
                VMEM(stack, f32),
                VMEM((2, *shape), i32),
                VMEM((2, *shape), f32),
                VMEM((3 * cells, 4 * cells), bf16),
                VMEM((cells, 3 * cells), bf16),
            ],
            in_specs=whole(3),
            out_specs=whole(5),
            cost_estimate=cost(2.0),
            name="own",
        )(field, offset, part)
    )
    pole_one = along_lon(pole_one, 1, False)
    pole_two = along_lon(pole_two, 2, False)
    from_west, from_east, from_far = in_vmem(from_west, from_east, from_far)

    message = (3 * depth + 1, cells)
    message_a, message_b = pl.pallas_call(
        edge_kernel,
        out_shape=[VMEM(message, f32), VMEM(message, f32)],
        in_specs=whole(9),
        out_specs=whole(2),
        cost_estimate=cost(8.0),
        name="edge",
    )(field, flux, packed, seam_index, seam_part, seam_matrix, north, from_east, from_west)
    message_a = along_lat(message_a, 0)
    message_b = along_lat(message_b, 1)

    wide, partial = pl.pallas_call(
        functools.partial(middle_kernel, lat_count),
        out_shape=[VMEM(stack, f32), jax.ShapeDtypeStruct(stack, f32)],
        in_specs=whole(15),
        out_specs=whole(1) + anywhere(1),
        scratch_shapes=[
            VMEM((depth, row_count - 2 * EDGE, cells), f32),
            VMEM((depth, row_count - EDGE, cells), f32),
            dma((depth,)),
        ],
        cost_estimate=cost(3.0),
        name="middle",
    )(
        field, offset, part, north, flux, packed, seam_index, seam_part, seam_matrix, block_matrix,
        from_east, from_far, from_west, *in_vmem(pole_one, pole_two),
    )

    out = pl.pallas_call(
        functools.partial(last_kernel, lat_count),
        out_shape=jax.ShapeDtypeStruct(stack, f32),
        in_specs=whole(4) + anywhere(1),
        out_specs=pl.BlockSpec(memory_space=pl.ANY),
        scratch_shapes=[
            VMEM((depth, 3 * EDGE, cells), f32),
            VMEM((depth, 3 * EDGE, cells), f32),
            VMEM((2, depth, EDGE, cells), f32),
            dma((2,)),
        ],
        input_output_aliases={4: 0},
        cost_estimate=cost(0.7),
        name="last",
    )(*in_vmem(wide), north, *in_vmem(message_b, message_a), partial)
    return out.reshape(tracers.shape)


def solution(mesh):
    placed = (P(None, None, "lat", "lon"), P("lat", "lon"), P("lat", "lon"), P("lat", "lon"))
    return jax.shard_map(
        functools.partial(on_device, mesh.shape["lat"], mesh.shape["lon"]),
        mesh=mesh,
        in_specs=placed,
        out_specs=P(None, None, "lat", "lon"),
        check_vma=False,
    )
```

```python
import functools

import jax
import jax.numpy as jnp
from jax import lax
from jax.experimental import pallas as pl
from jax.experimental.pallas import tpu as pltpu
from jax.sharding import PartitionSpec as P

POLAR = 24
BAND = 24
POLE = POLAR + BAND
WEST = 12
SEG = 24
FACES = 11
OFF_LANE = 120
FRAC_LANE = 121
EDGE = 8

f32 = jnp.float32
bf16 = jnp.bfloat16
i32 = jnp.int32
VMEM = pltpu.VMEM


def lanes(shape):
    return lax.broadcasted_iota(i32, shape, 1)


def rolled(value, steps):
    steps = steps % value.shape[1]
    return pltpu.roll(value, steps, 1) if steps else value


def pick(table, index):
    return jnp.take_along_axis(table, index, axis=1, mode="promise_in_bounds")


def parabola(c, right, left, centre):
    jump = right - left
    curve = 6.0 * centre - 3.0 * (left + right)
    return c * (right - 0.5 * c * (jump - (1.0 - (2.0 / 3.0) * c) * curve))


def times(value, matrix):
    high = value.astype(bf16)
    low = (value - high.astype(f32)).astype(bf16)
    return jnp.dot(high, matrix, preferred_element_type=f32) + jnp.dot(
        low, matrix, preferred_element_type=f32
    )


def edge_weights(gap):
    def weight(gap):
        inner = (gap == 0) | (gap == 1)
        outer = (gap == -1) | (gap == 2)
        return jnp.where(inner, 7.0, jnp.where(outer, -1.0, 0.0))

    return weight(gap), weight(gap + 1)


def split(table, cells):
    return [table[:, i : i + cells] for i in range(0, table.shape[1], cells)]


def pack_kernel(
    lat_count, tracers, offsets, fraction, courant,
    field, offset, part, north, packed, to_east, pole_one, pole_two, sems,
):
    depth, row_count, cells = field.shape
    copies = [
        pltpu.make_async_copy(source, target, sems.at[i])
        for i, (source, target) in enumerate(
            ((tracers, field), (offsets, offset), (fraction, part), (courant, north))
        )
    ]
    for copy in copies:
        copy.start()
    for copy in copies[:3]:
        copy.wait()
    shape = (row_count, cells)
    lane = lanes(shape)
    message = jnp.where(
        lane == OFF_LANE,
        rolled(offset[...].astype(f32), OFF_LANE),
        jnp.where(lane == FRAC_LANE, rolled(part[...], FRAC_LANE), 0.0),
    )
    for t in range(depth):
        mine = (lane >= t * SEG) & (lane < (t + 1) * SEG)
        message = jnp.where(mine, rolled(field[t], t * SEG + WEST), message)
    packed[...] = message
    to_east[...] = message
    lat = lax.axis_index("lat")
    south = lat == 0

    @pl.when(south | (lat == lat_count - 1))
    def _():
        base = pl.multiple_of(jnp.where(south, 0, row_count - POLE), 8)
        band = pl.multiple_of(jnp.where(south, POLAR, row_count - POLE), 8)
        polar = pl.multiple_of(jnp.where(south, 0, row_count - POLAR), 8)
        rows = [field[t, pl.ds(band, BAND)] for t in range(depth)]
        lane = lanes(rows[0].shape)
        half = cells // 2
        halves = []
        for t in range(0, depth, 2):
            other = rolled(rows[t + 1], half) if t + 1 < depth else jnp.zeros(lane.shape, f32)
            halves.append(jnp.where(lane >= half, rows[t], other))
        rest = halves.pop()
        for t in range(depth):
            mine = (lane >= 3 * t) & (lane < 3 * t + 3)
            rest = jnp.where(mine, rolled(rows[t], 3 * t + 3 - half), rest)
        for i, value in enumerate(halves):
            to_east[pl.ds(pl.multiple_of(base + i * BAND, 8), BAND)] = value
        pole_one[:BAND] = rest
        for t in range(depth):
            value = field[t, pl.ds(polar, POLAR)]
            pole_one[BAND + t * POLAR : BAND + (t + 1) * POLAR] = value
            pole_two[t * POLAR : (t + 1) * POLAR] = value

    copies[3].wait()


def pieces(row_count):
    return [(0, POLE), (POLE, row_count - 2 * POLE), (row_count - POLE, POLE)]


def each_mid_piece(lat_count, row_count, body):
    lat = lax.axis_index("lat")
    conditions = (lat > 0, None, lat < lat_count - 1)
    for (first, count), condition in zip(pieces(row_count), conditions):
        if count and condition is None:
            body(first, count)
        elif count:
            pl.when(condition)(functools.partial(body, first, count))


def own_kernel(
    lat_count, field, offset, part, flux, seam_index, seam_part, block_matrix, seam_matrix
):
    depth, row_count, cells = field.shape
    shape = (cells, cells)
    source = lax.broadcasted_iota(i32, shape, 0)
    target = lax.broadcasted_iota(i32, shape, 1)
    gap = source - target
    upto = jnp.where(gap <= 0, 1.0, 0.0)
    right, left = edge_weights(gap)
    block_matrix[:cells] = jnp.concatenate([upto, right, left, jnp.ones(shape, f32)], axis=1).astype(bf16)
    zeros = jnp.zeros(shape, f32)
    beyond = gap + jnp.where(source < cells // 2, cells, -cells)
    block_matrix[cells:] = jnp.concatenate([zeros, *edge_weights(beyond), zeros], axis=1).astype(bf16)
    together = source // SEG == target // SEG
    seam_matrix[...] = jnp.concatenate([jnp.where(together, upto, 0.0), right, left], axis=1).astype(bf16)

    def step(first_row, count):
        at = pl.ds(first_row, count)
        shape = (count, cells)
        lane = lanes(shape)
        place = lane % SEG
        offsets = offset[at]
        courant = part[at]
        index = (lane - offsets - 1) & (cells - 1)
        own = field[:, at].reshape(depth * count, cells)
        tables = times(own, block_matrix[:cells, : 3 * cells])
        for t in range(depth):
            sums, right, left = split(tables[t * count : (t + 1) * count], cells)
            value = field[t, at]
            flux[t, at] = (
                sums
                - value
                - pick(sums, index)
                + parabola(
                    courant, pick(right, index) * (1 / 12), pick(left, index) * (1 / 12), pick(value, index)
                )
            )
        first = (place - WEST) & (cells - 1)
        final = jnp.full(shape, cells - 1, i32)
        seam_index[0, at] = (lane - pick(offsets, first) - 1) & (cells - 1)
        seam_index[1, at] = (lane - pick(offsets, final) - 1) & (cells - 1)
        seam_part[0, at] = pick(courant, first)
        seam_part[1, at] = pick(courant, final)

    each_mid_piece(lat_count, row_count, step)


def rows_after(field, flux, packed, seam_index, seam_part, from_west, from_east, seam_matrix, parts):
    def take(ref, *lead):
        return jnp.concatenate([ref[(*lead, part)] for part in parts], axis=0)

    mine, west, east = take(packed), take(from_west), take(from_east)
    count, cells = mine.shape
    shape = mine.shape
    lane = lanes(shape)
    place = lane % SEG
    near = place < WEST
    rows = jnp.concatenate([jnp.where(near, west, mine), jnp.where(near, mine, east)], axis=0)
    next_face = place == WEST
    next_offset = pick(east, jnp.full(shape, OFF_LANE, i32)).astype(i32)
    next_part = pick(east, jnp.full(shape, FRAC_LANE, i32))
    next_index = (lane - next_offset - 1) & (cells - 1)
    index = jnp.concatenate(
        [take(seam_index, 0), jnp.where(next_face, next_index, take(seam_index, 1))], axis=0
    )
    courant = jnp.concatenate(
        [take(seam_part, 0), jnp.where(next_face, next_part, take(seam_part, 1))], axis=0
    )
    sums, right, left = split(times(rows, seam_matrix[...]), cells)
    faces = (
        sums
        - rows
        - pick(sums, index)
        + parabola(
            courant, pick(right, index) * (1 / 12), pick(left, index) * (1 / 12), pick(rows, index)
        )
    )
    east_faces = faces[count:]
    both = jnp.where(place == WEST - 1, east_faces, faces[:count])
    outside = (lane < FACES) | (lane == cells - 1)
    results = []
    for t in range(field.shape[0]):
        steps = -(t * SEG + WEST)
        face = jnp.where(outside, rolled(both, steps), take(flux, t))
        following = jnp.where(lane == cells - 1, rolled(east_faces, steps - 1), rolled(face, -1))
        results.append(take(field, t) - (following - face))
    return results


def edge_kernel(
    field, flux, packed, seam_index, seam_part, seam_matrix, north, from_east, from_west,
    message_a, message_b,
):
    depth, row_count, _ = field.shape
    parts = (pl.ds(0, EDGE), pl.ds(row_count - EDGE, EDGE))
    after = rows_after(
        field, flux, packed, seam_index, seam_part, from_west, from_east, seam_matrix, parts
    )
    even = lax.axis_index("lat") % 2 == 0
    for t in range(depth):
        bottom, top = after[t][:3], after[t][2 * EDGE - 3 :]
        message_a[3 * t : 3 * t + 3] = jnp.where(even, top, bottom)
        message_b[3 * t : 3 * t + 3] = jnp.where(even, bottom, top)
    message_a[3 * depth : 3 * depth + 1] = north[:1]
    message_b[3 * depth : 3 * depth + 1] = north[:1]


def polar_rows(tables, own, west, west_two, offset, courant, next_offset, next_courant):
    cells = own.shape[1]
    lane = lanes(own.shape)
    (sums, _, _, total), one, two = tables
    source = lane - offset - 1
    index = source & (cells - 1)
    close = source >= -cells

    def both(here, there):
        return jnp.where(close, pick(here, index), pick(there, index))

    face = (
        sums
        - own
        + one[3]
        - both(one[0], two[0] - two[3])
        + parabola(
            courant, both(one[1], two[1]) * (1 / 12), both(one[2], two[2]) * (1 / 12), both(west, west_two)
        )
    )
    index = (cells - 1 - next_offset) & (cells - 1)
    last = parabola(next_courant, one[1] * (1 / 12), one[2] * (1 / 12), west) - one[0]
    last = total + one[3] + pick(last, index)
    following = rolled(jnp.where(lane == 0, last, face), -1)
    return own - (following - face)


def band_rows(tables, own, west, offset, courant, next_offset, next_courant):
    cells = own.shape[1]
    lane = lanes(own.shape)
    here, one = tables
    source = lane - offset - 1
    index = source & (cells - 1)
    inside = source >= 0

    def both(inner, outer):
        return jnp.where(inside, pick(inner, index), pick(outer, index))

    face = (
        here[0]
        - own
        - both(here[0], one[0] - one[3])
        + parabola(
            courant, both(here[1], one[1]) * (1 / 12), both(here[2], one[2]) * (1 / 12), both(own, west)
        )
    )
    index = (cells - 1 - next_offset) & (cells - 1)
    last = parabola(next_courant, here[1] * (1 / 12), here[2] * (1 / 12), own) - here[0]
    last = here[3] + pick(last, index)
    following = rolled(jnp.where(lane == 0, last, face), -1)
    return own - (following - face)


def merid_flux(wide, t, courant, first, count):
    cell = [wide[t, first + k : first + k + count] for k in (-3, -2, -1, 0, 1)]
    left = (7.0 * (cell[1] + cell[2]) - (cell[0] + cell[3])) * (1 / 12)
    right = (7.0 * (cell[2] + cell[3]) - (cell[1] + cell[4])) * (1 / 12)
    return parabola(courant, right, left, cell[2])


def middle_kernel(
    lat_count, field, north, flux, packed, seam_index, seam_part, seam_matrix, from_east, from_west,
    wide, out, result, faces, sems,
):
    depth, row_count, cells = field.shape

    def step(first, count):
        after = rows_after(
            field, flux, packed, seam_index, seam_part, from_west, from_east, seam_matrix,
            (pl.ds(first, count),),
        )
        for t in range(depth):
            wide[t, first : first + count] = after[t]

    each_mid_piece(lat_count, row_count, step)
    lat = lax.axis_index("lat")

    @pl.when((lat > 0) & (lat < lat_count - 1))
    def _():
        copies = [
            pltpu.make_async_copy(result.at[t], out.at[t, pl.ds(EDGE, result.shape[1])], sems.at[t])
            for t in range(depth)
        ]
        inner_rows(wide, north, faces, result, copies)
        for copy in copies:
            copy.wait()


def inner_rows(wide, north, faces, result, copies=()):
    depth, count, _ = result.shape
    for t in range(depth):
        faces[t, :count] = merid_flux(wide, t, north[EDGE : EDGE + count], EDGE, count)
        last = merid_flux(wide, t, north[EDGE + count : EDGE + count + 1], EDGE + count, 1)
        faces[t, count : count + 1] = last
        result[t] = wide[t, EDGE : EDGE + count] - (faces[t, 1 : 1 + count] - faces[t, :count])
        if copies:
            copies[t].start()


def poles_kernel(
    lat_count, field, offset, part, north, block_matrix, from_east, from_far, from_west, pole_one, pole_two,
    given, wide, inner, faces,
):
    del given
    depth, row_count, cells = field.shape
    lat = lax.axis_index("lat")
    south = lat == 0

    @pl.when(south | (lat == lat_count - 1))
    def _():
        pole_rows_step(
            south, field, offset, part, from_east, from_far, from_west, pole_one, pole_two, block_matrix, wide
        )
        inner_rows(wide, north, faces, inner)


def pole_rows_step(
    south, field, offset, part, from_east, from_far, from_west, pole_one, pole_two, block_matrix, wide
):
    depth, row_count, cells = field.shape
    base = pl.multiple_of(jnp.where(south, 0, row_count - POLE), 8)
    polar_at = pl.ds(pl.multiple_of(jnp.where(south, 0, row_count - POLAR), 8), POLAR)
    band_at = pl.ds(pl.multiple_of(jnp.where(south, POLAR, row_count - POLE), 8), BAND)

    def stacked(ref, rows):
        return ref[:, rows, :].reshape(-1, cells)

    def unpacked(ref, rows, lane):
        value = ref[rows]
        return jnp.concatenate([rolled(value, lane - t * SEG) for t in range(depth)], axis=0)

    own_polar, own_band = stacked(field, polar_at), stacked(field, band_at)
    west_polar = pole_one[BAND:]
    west_two = pole_two[...]
    far = unpacked(from_far, polar_at, cells - WEST)
    east = unpacked(from_east, band_at, -WEST)
    rest = pole_one[:BAND]
    lane = lanes(rest.shape)
    half = cells // 2
    west_band = []
    for t in range(depth):
        value = rest
        if t // 2 < (depth - 1) // 2:
            value = from_west[pl.ds(pl.multiple_of(base + t // 2 * BAND, 8), BAND)]
        value = rolled(value, half) if t % 2 else value
        inner = jnp.where(lane >= half - 3, rolled(rest, half - 3 - 3 * t), 0.0)
        west_band.append(jnp.where(lane >= half, value, inner))
    west_band = jnp.concatenate(west_band, axis=0)

    def with_sides(west, own, east):
        beside = jnp.where(lanes(own.shape) < half, east, west)
        return jnp.concatenate([own, beside], axis=1)

    rows = jnp.concatenate(
        [
            with_sides(own_polar, own_polar, own_polar),
            with_sides(west_two, west_polar, own_polar),
            with_sides(far, west_two, west_polar),
            with_sides(west_band, own_band, east),
            with_sides(west_band, west_band, own_band),
        ],
        axis=0,
    )
    tables = times(rows, block_matrix[...])

    def table(which, t):
        first = (which * depth + t) * POLAR
        return split(tables[first : first + POLAR], cells)

    for rows_at, is_polar in ((polar_at, True), (band_at, False)):
        shape = (POLAR, cells)
        beyond = from_east[rows_at]
        common = (
            offset[rows_at],
            part[rows_at],
            pick(beyond, jnp.full(shape, OFF_LANE, i32)).astype(i32),
            pick(beyond, jnp.full(shape, FRAC_LANE, i32)),
        )
        for t in range(depth):
            at = slice(t * POLAR, (t + 1) * POLAR)
            if is_polar:
                wide[t, rows_at] = polar_rows(
                    (table(0, t), table(1, t), table(2, t)), own_polar[at], west_polar[at], west_two[at], *common
                )
            else:
                wide[t, rows_at] = band_rows(
                    (table(3, t), table(4, t)), own_band[at], west_band[at], *common
                )


def last_kernel(
    lat_count, wide, inner, north, message_b, message_a, partial, out, low, high, result, sems
):
    del partial
    depth, row_count, cells = wide.shape
    count = row_count - 2 * EDGE
    lat = lax.axis_index("lat")
    even = lat % 2 == 0
    south, top = lat == 0, lat == lat_count - 1
    inner_copy = pltpu.make_async_copy(inner, out.at[:, pl.ds(EDGE, count)], sems.at[2])

    @pl.when(south | top)
    def _():
        inner_copy.start()

    end = 3 * depth
    north_courant = jnp.where(even, message_a[end : end + 1], message_b[end : end + 1])
    north_courant = jnp.where(top, 0.0, north_courant)
    first_row = lax.broadcasted_iota(i32, (EDGE, cells), 0)
    low_courant = jnp.where(south & (first_row == 0), 0.0, north[:EDGE])
    high_next = jnp.concatenate([north[row_count - EDGE + 1 :], north_courant], axis=0)
    for t in range(depth):
        rows = slice(3 * t, 3 * t + 3)
        from_a, from_b = message_a[rows], message_b[rows]
        low[t, EDGE - 3 : EDGE] = jnp.where(south, 0.0, jnp.where(even, from_b, from_a))
        low[t, EDGE : 3 * EDGE] = wide[t, : 2 * EDGE]
        high[t, : 2 * EDGE] = wide[t, row_count - 2 * EDGE :]
        high[t, 2 * EDGE : 2 * EDGE + 3] = jnp.where(top, 0.0, jnp.where(even, from_a, from_b))
    for t in range(depth):
        south_face = merid_flux(low, t, low_courant, EDGE, EDGE)
        north_face = merid_flux(low, t, north[1 : EDGE + 1], EDGE + 1, EDGE)
        result[0, t] = low[t, EDGE : 2 * EDGE] - (north_face - south_face)
        south_face = merid_flux(high, t, north[row_count - EDGE :], EDGE, EDGE)
        north_face = merid_flux(high, t, high_next, EDGE + 1, EDGE)
        result[1, t] = high[t, EDGE : 2 * EDGE] - (north_face - south_face)
    copies = [
        pltpu.make_async_copy(result.at[i], out.at[:, pl.ds(first, EDGE)], sems.at[i])
        for i, first in enumerate((0, row_count - EDGE))
    ]
    for copy in copies:
        copy.start()
    for copy in copies:
        copy.wait()

    @pl.when(south | top)
    def _():
        inner_copy.wait()


def cost(microseconds):
    return pl.CostEstimate(
        flops=int(microseconds * 1e8), bytes_accessed=int(microseconds * 3e6), transcendentals=0
    )


def in_vmem(*values):
    return [pltpu.with_memory_space_constraint(value, VMEM) for value in values]


def whole(count):
    return [pl.BlockSpec(memory_space=VMEM)] * count


def anywhere(count):
    return [pl.BlockSpec(memory_space=pl.ANY)] * count


def on_device(lat_count, lon_count, tracers, offsets, fraction, courant_north):
    tracer_count, level_count, row_count, cells = tracers.shape
    depth = tracer_count * level_count
    shape = (row_count, cells)
    stack = (depth, row_count, cells)
    dma = pltpu.SemaphoreType.DMA

    def along_lon(value, steps, everywhere=True):
        pairs = []
        for l in range(lat_count):
            from_pole = min(l, lat_count - 1 - l)
            for o in range(lon_count):
                if everywhere or from_pole == 0 or lat_count % 2 or lon_count % 2:
                    target = (l, (o + steps) % lon_count)
                else:
                    target = (l, o ^ 1) if from_pole == 1 else (l ^ 1, o)
                pairs.append((l * lon_count + o, target[0] * lon_count + target[1]))
        return lax.ppermute(value, ("lat", "lon"), pairs)

    def along_lat(value, first):
        pairs = []
        for l in range(first, lat_count if lat_count % 2 == 0 else lat_count - 1, 2):
            for o in range(lon_count):
                low, high = l * lon_count + o, (l + 1) % lat_count * lon_count + o
                pairs += [(low, high), (high, low)]
        return lax.ppermute(value, ("lat", "lon"), pairs)

    field, offset, part, north, packed, to_east, pole_one, pole_two = in_vmem(
        *pl.pallas_call(
            functools.partial(pack_kernel, lat_count),
            out_shape=[
                VMEM(stack, f32),
                VMEM(shape, i32),
                VMEM(shape, f32),
                VMEM(shape, f32),
                VMEM(shape, f32),
                VMEM(shape, f32),
                VMEM((BAND + depth * POLAR, cells), f32),
                VMEM((depth * POLAR, cells), f32),
            ],
            in_specs=anywhere(4),
            out_specs=whole(8),
            scratch_shapes=[dma((4,))],
            cost_estimate=cost(1.0),
            name="pack",
        )(tracers.reshape(stack), offsets, fraction, courant_north)
    )
    from_west = along_lon(to_east, 1)
    from_east = along_lon(packed, -1)
    from_far = from_east if lon_count == 4 else along_lon(packed, 3)
    pole_one = along_lon(pole_one, 1, False)
    pole_two = along_lon(pole_two, 2, False)

    flux, seam_index, seam_part, block_matrix, seam_matrix = in_vmem(
        *pl.pallas_call(
            functools.partial(own_kernel, lat_count),
            out_shape=[
                VMEM(stack, f32),
                VMEM((2, *shape), i32),
                VMEM((2, *shape), f32),
                VMEM((2 * cells, 4 * cells), bf16),
                VMEM((cells, 3 * cells), bf16),
            ],
            in_specs=whole(3),
            out_specs=whole(5),
            cost_estimate=cost(2.0),
            name="own",
        )(field, offset, part)
    )
    from_west, from_east, from_far, pole_one, pole_two = in_vmem(
        from_west, from_east, from_far, pole_one, pole_two
    )

    message = (3 * depth + 1, cells)
    message_a, message_b = pl.pallas_call(
        edge_kernel,
        out_shape=[VMEM(message, f32), VMEM(message, f32)],
        in_specs=whole(9),
        out_specs=whole(2),
        cost_estimate=cost(2.0),
        name="edge",
    )(field, flux, packed, seam_index, seam_part, seam_matrix, north, from_east, from_west)
    message_a = along_lat(message_a, 0)
    message_b = along_lat(message_b, 1)

    wide, partial = pl.pallas_call(
        functools.partial(middle_kernel, lat_count),
        out_shape=[VMEM(stack, f32), jax.ShapeDtypeStruct(stack, f32)],
        in_specs=whole(9),
        out_specs=whole(1) + anywhere(1),
        scratch_shapes=[
            VMEM((depth, row_count - 2 * EDGE, cells), f32),
            VMEM((depth, row_count - EDGE, cells), f32),
            dma((depth,)),
        ],
        cost_estimate=cost(3.0),
        name="middle",
    )(field, north, flux, packed, seam_index, seam_part, seam_matrix, from_east, from_west)

    inner = (depth, row_count - 2 * EDGE, cells)
    faces = VMEM((depth, row_count - EDGE, cells), f32)
    wide, inner = pl.pallas_call(
        functools.partial(poles_kernel, lat_count),
        out_shape=[VMEM(stack, f32), VMEM(inner, f32)],
        in_specs=whole(11),
        out_specs=whole(2),
        scratch_shapes=[faces],
        input_output_aliases={10: 0},
        cost_estimate=cost(3.0),
        name="poles",
    )(
        field, offset, part, north, block_matrix, from_east, from_far, from_west, pole_one, pole_two,
        *in_vmem(wide),
    )

    out = pl.pallas_call(
        functools.partial(last_kernel, lat_count),
        out_shape=jax.ShapeDtypeStruct(stack, f32),
        in_specs=whole(5) + anywhere(1),
        out_specs=pl.BlockSpec(memory_space=pl.ANY),
        scratch_shapes=[
            VMEM((depth, 3 * EDGE, cells), f32),
            VMEM((depth, 3 * EDGE, cells), f32),
            VMEM((2, depth, EDGE, cells), f32),
            dma((3,)),
        ],
        input_output_aliases={5: 0},
        cost_estimate=cost(0.7),
        name="last",
    )(*in_vmem(wide, inner), north, *in_vmem(message_b, message_a), partial)
    return out.reshape(tracers.shape)


def solution(mesh):
    placed = (P(None, None, "lat", "lon"), P("lat", "lon"), P("lat", "lon"), P("lat", "lon"))
    return jax.shard_map(
        functools.partial(on_device, mesh.shape["lat"], mesh.shape["lon"]),
        mesh=mesh,
        in_specs=placed,
        out_specs=P(None, None, "lat", "lon"),
        check_vma=False,
    )
```

```python
import functools

import jax
import jax.numpy as jnp
from jax import lax
from jax.experimental import pallas as pl
from jax.experimental.pallas import tpu as pltpu
from jax.sharding import PartitionSpec as P

POLAR = 24
BAND = 24
POLE = POLAR + BAND
WEST = 12
SEG = 24
FACES = 11
OFF_LANE = 120
FRAC_LANE = 121
PAIR = 4
EDGE = 8

f32 = jnp.float32
bf16 = jnp.bfloat16
i32 = jnp.int32
VMEM = pltpu.VMEM


def lanes(shape):
    return lax.broadcasted_iota(i32, shape, 1)


def rolled(value, steps):
    steps = steps % value.shape[1]
    return pltpu.roll(value, steps, 1) if steps else value


def pick(table, index):
    return jnp.take_along_axis(table, index, axis=1, mode="promise_in_bounds")


def parabola(c, right, left, centre):
    jump = right - left
    curve = 6.0 * centre - 3.0 * (left + right)
    return c * (right - 0.5 * c * (jump - (1.0 - (2.0 / 3.0) * c) * curve))


def times(value, matrix):
    high = value.astype(bf16)
    low = (value - high.astype(f32)).astype(bf16)
    return jnp.dot(high, matrix, preferred_element_type=f32) + jnp.dot(
        low, matrix, preferred_element_type=f32
    )


def for_west(packed):
    half, cells = packed.shape[0] // 2, packed.shape[1]
    lane = lanes((half, cells))
    place = lane % SEG
    first = (lane >= OFF_LANE) & (lane < OFF_LANE + 2)
    first = first | ((lane < OFF_LANE) & (place >= WEST - 2) & (place < WEST + 2))
    return jnp.where(first, packed[:half], rolled(packed[half:], PAIR))


def edge_weights(gap):
    def weight(gap):
        inner = (gap == 0) | (gap == 1)
        outer = (gap == -1) | (gap == 2)
        return jnp.where(inner, 7.0, jnp.where(outer, -1.0, 0.0))

    return weight(gap), weight(gap + 1)


def split(table, cells):
    return [table[:, i : i + cells] for i in range(0, table.shape[1], cells)]


def pack_kernel(
    lat_count, tracers, offsets, fraction, courant,
    field, offset, part, north, packed, to_east, to_west, pole, sems,
):
    depth, row_count, cells = field.shape
    copies = [
        pltpu.make_async_copy(source, target, sems.at[i])
        for i, (source, target) in enumerate(
            ((tracers, field), (offsets, offset), (fraction, part), (courant, north))
        )
    ]
    for copy in copies:
        copy.start()
    for copy in copies[:3]:
        copy.wait()
    shape = (row_count, cells)
    lane = lanes(shape)
    message = jnp.where(
        lane == OFF_LANE,
        rolled(offset[...].astype(f32), OFF_LANE),
        jnp.where(lane == FRAC_LANE, rolled(part[...], FRAC_LANE), 0.0),
    )
    for t in range(depth):
        mine = (lane >= t * SEG) & (lane < (t + 1) * SEG)
        message = jnp.where(mine, rolled(field[t], t * SEG + WEST), message)
    packed[...] = message
    to_east[:row_count] = message
    to_west[...] = for_west(message)
    lat = lax.axis_index("lat")
    south = lat == 0

    @pl.when(south | (lat == lat_count - 1))
    def _():
        base, band, polar, mid = pole_places(south, row_count)
        rows = [field[t, pl.ds(band, BAND)] for t in range(depth)]
        lane = lanes(rows[0].shape)
        half = cells // 2
        for t in range(0, depth - 1, 2):
            value = jnp.where(lane >= half, rows[t], rolled(rows[t + 1], half))
            to_east[pl.ds(pl.multiple_of(base + t // 2 * BAND, 8), BAND)] = value
        rest = rolled(rows[depth - 1], OFF_LANE - cells)
        for t in range(depth):
            mine = (lane >= 3 * t) & (lane < 3 * t + 3)
            rest = jnp.where(mine, rolled(rows[t], 3 * t + 3 - half), rest)
        kept = (lane % SEG < WEST) | (lane >= OFF_LANE)
        for i, value in enumerate((rest, rolled(rest, WEST))):
            at = pl.ds(pl.multiple_of(mid + i * BAND, 8), BAND)
            to_east[at] = jnp.where(kept, to_east[at], value)
        for t in range(depth):
            value = field[t, pl.ds(polar, POLAR)]
            first = row_count + t * POLAR
            to_east[first : first + POLAR] = value
            pole[t * POLAR : (t + 1) * POLAR] = value
    copies[3].wait()


def pole_places(south, row_count):
    places = (
        jnp.where(south, 0, row_count - POLE),
        jnp.where(south, POLAR, row_count - POLE),
        jnp.where(south, 0, row_count - POLAR),
        jnp.where(south, POLE, 0),
    )
    return [pl.multiple_of(place, 8) for place in places]


def by_place(lat_count, away, south, north):
    lat = lax.axis_index("lat")
    if away is not None:
        pl.when((lat > 0) & (lat < lat_count - 1))(away)
    pl.when(lat == 0)(south)
    pl.when(lat == lat_count - 1)(north)


def pieces(row_count):
    middle = [(POLE, row_count - 2 * POLE)] if row_count > 2 * POLE else []
    return [(0, POLE), *middle, (row_count - POLE, POLE)]


def mid_pieces(row_count):
    return pieces(row_count), pieces(row_count)[1:], pieces(row_count)[:-1]


def own_faces(first_row, count, field, offset, part, block_matrix, flux, seam_index, seam_part):
    depth, _, cells = field.shape
    at = pl.ds(first_row, count)
    shape = (count, cells)
    lane = lanes(shape)
    place = lane % SEG
    offsets = offset[at]
    courant = part[at]
    index = (lane - offsets - 1) & (cells - 1)
    own = field[:, at].reshape(depth * count, cells)
    tables = times(own, block_matrix[:cells, : 3 * cells])
    for t in range(depth):
        sums, right, left = split(tables[t * count : (t + 1) * count], cells)
        value = field[t, at]
        flux[t, at] = (
            sums
            - value
            - pick(sums, index)
            + parabola(
                courant, pick(right, index) * (1 / 12), pick(left, index) * (1 / 12), pick(value, index)
            )
        )
    first = (place - WEST) & (cells - 1)
    final = jnp.full(shape, cells - 1, i32)
    seam_index[0, at] = (lane - pick(offsets, first) - 1) & (cells - 1)
    seam_index[1, at] = (lane - pick(offsets, final) - 1) & (cells - 1)
    seam_part[0, at] = pick(courant, first)
    seam_part[1, at] = pick(courant, final)


def own_kernel(lat_count, field, offset, part, flux, seam_index, seam_part, block_matrix, seam_matrix):
    _, row_count, cells = field.shape
    shape = (cells, cells)
    source = lax.broadcasted_iota(i32, shape, 0)
    target = lax.broadcasted_iota(i32, shape, 1)
    gap = source - target
    upto = jnp.where(gap <= 0, 1.0, 0.0)
    right, left = edge_weights(gap)
    block_matrix[:cells] = jnp.concatenate([upto, right, left, jnp.ones(shape, f32)], axis=1).astype(bf16)
    zeros = jnp.zeros(shape, f32)
    beyond = gap + jnp.where(source < cells // 2, cells, -cells)
    block_matrix[cells:] = jnp.concatenate([zeros, *edge_weights(beyond), zeros], axis=1).astype(bf16)
    together = source // SEG == target // SEG
    seam_matrix[...] = jnp.concatenate([jnp.where(together, upto, 0.0), right, left], axis=1).astype(bf16)

    def step(parts):
        for first, count in parts:
            own_faces(first, count, field, offset, part, block_matrix, flux, seam_index, seam_part)

    by_place(lat_count, *(functools.partial(step, parts) for parts in mid_pieces(row_count)))


def rows_after(field, flux, packed, seam_index, seam_part, from_west, from_east, seam_matrix, parts):
    def take(ref, *lead):
        return jnp.concatenate([ref[(*lead, part)] for part in parts], axis=0)

    mine, west = take(packed), take(from_west)
    east = from_east if isinstance(from_east, jax.Array) else take(from_east)
    count, cells = mine.shape
    shape = mine.shape
    lane = lanes(shape)
    place = lane % SEG
    near = place < WEST
    rows = jnp.concatenate([jnp.where(near, west, mine), jnp.where(near, mine, east)], axis=0)
    next_face = place == WEST
    next_offset = pick(east, jnp.full(shape, OFF_LANE, i32)).astype(i32)
    next_part = pick(east, jnp.full(shape, FRAC_LANE, i32))
    next_index = (lane - next_offset - 1) & (cells - 1)
    index = jnp.concatenate(
        [take(seam_index, 0), jnp.where(next_face, next_index, take(seam_index, 1))], axis=0
    )
    courant = jnp.concatenate(
        [take(seam_part, 0), jnp.where(next_face, next_part, take(seam_part, 1))], axis=0
    )
    sums, right, left = split(times(rows, seam_matrix[...]), cells)
    faces = (
        sums
        - rows
        - pick(sums, index)
        + parabola(
            courant, pick(right, index) * (1 / 12), pick(left, index) * (1 / 12), pick(rows, index)
        )
    )
    east_faces = faces[count:]
    both = jnp.where(place == WEST - 1, east_faces, faces[:count])
    outside = (lane < FACES) | (lane == cells - 1)
    results = []
    for t in range(field.shape[0]):
        steps = -(t * SEG + WEST)
        face = jnp.where(outside, rolled(both, steps), take(flux, t))
        following = jnp.where(lane == cells - 1, rolled(east_faces, steps - 1), rolled(face, -1))
        results.append(take(field, t) - (following - face))
    return results


def edge_kernel(
    lat_count, field, flux, packed, seam_index, seam_part, seam_matrix, north, from_east, from_west,
    message_a, message_b, wide, east,
):
    depth, row_count, _ = field.shape
    half = row_count // 2
    even = lax.axis_index("lat") % 2 == 0

    def step(parts, beyond):
        return rows_after(
            field, flux, packed, seam_index, seam_part, from_west, beyond, seam_matrix, parts
        )

    def send(t, top, bottom):
        rows = slice(3 * t, 3 * t + 3)
        message_a[rows] = jnp.where(even, top, bottom)
        message_b[rows] = jnp.where(even, bottom, top)

    def away():
        beyond = jnp.concatenate(
            [from_east[:EDGE], rolled(from_east[half - EDGE :], -PAIR)], axis=0
        )
        after = step((pl.ds(0, EDGE), pl.ds(row_count - EDGE, EDGE)), beyond)
        for t in range(depth):
            send(t, after[t][2 * EDGE - 3 :], after[t][:3])

    def polar_device(parts):
        east[:half] = from_east[...]
        east[half:] = rolled(from_east[...], -PAIR)
        for first, count in parts:
            after = step((pl.ds(first, count),), east)
            for t in range(depth):
                wide[t, first : first + count] = after[t]
        for t in range(depth):
            send(t, wide[t, row_count - 3 :], wide[t, :3])

    by_place(
        lat_count, away, *(functools.partial(polar_device, parts) for parts in mid_pieces(row_count)[1:])
    )
    message_a[3 * depth : 3 * depth + 1] = north[:1]
    message_b[3 * depth : 3 * depth + 1] = north[:1]


def polar_rows(tables, own, west, west_two, offset, courant, next_offset, next_courant):
    cells = own.shape[1]
    lane = lanes(own.shape)
    (sums, _, _, total), one, two = tables
    source = lane - offset - 1
    index = source & (cells - 1)
    close = source >= -cells

    def both(here, there):
        return jnp.where(close, pick(here, index), pick(there, index))

    face = (
        sums
        - own
        + one[3]
        - both(one[0], two[0] - two[3])
        + parabola(
            courant, both(one[1], two[1]) * (1 / 12), both(one[2], two[2]) * (1 / 12), both(west, west_two)
        )
    )
    index = (cells - 1 - next_offset) & (cells - 1)
    last = parabola(next_courant, one[1] * (1 / 12), one[2] * (1 / 12), west) - one[0]
    last = total + one[3] + pick(last, index)
    following = rolled(jnp.where(lane == 0, last, face), -1)
    return own - (following - face)


def band_rows(tables, own, west, offset, courant, next_offset, next_courant):
    cells = own.shape[1]
    lane = lanes(own.shape)
    here, one = tables
    source = lane - offset - 1
    index = source & (cells - 1)
    inside = source >= 0

    def both(inner, outer):
        return jnp.where(inside, pick(inner, index), pick(outer, index))

    face = (
        here[0]
        - own
        - both(here[0], one[0] - one[3])
        + parabola(
            courant, both(here[1], one[1]) * (1 / 12), both(here[2], one[2]) * (1 / 12), both(own, west)
        )
    )
    index = (cells - 1 - next_offset) & (cells - 1)
    last = parabola(next_courant, here[1] * (1 / 12), here[2] * (1 / 12), own) - here[0]
    last = here[3] + pick(last, index)
    following = rolled(jnp.where(lane == 0, last, face), -1)
    return own - (following - face)


def merid_flux(wide, t, courant, first, count):
    cell = [wide[t, first + k : first + k + count] for k in (-3, -2, -1, 0, 1)]
    left = (7.0 * (cell[1] + cell[2]) - (cell[0] + cell[3])) * (1 / 12)
    right = (7.0 * (cell[2] + cell[3]) - (cell[1] + cell[4])) * (1 / 12)
    return parabola(courant, right, left, cell[2])


def middle_kernel(
    lat_count, field, offset, part, north, flux, packed, seam_index, seam_part, seam_matrix, block_matrix,
    from_east, from_far, from_west, given_wide, given_east, wide, east, inner, far, faces,
):
    del given_wide, given_east
    depth, row_count, cells = field.shape
    half = row_count // 2
    far[:half] = from_far[...]
    far[half:] = rolled(from_far[...], -PAIR)

    def away():
        east[:half] = from_east[...]
        east[half:] = rolled(from_east[...], -PAIR)
        for first, count in pieces(row_count):
            after = rows_after(
                field, flux, packed, seam_index, seam_part, from_west, east, seam_matrix, (pl.ds(first, count),)
            )
            for t in range(depth):
                wide[t, first : first + count] = after[t]
        inner_rows(wide, north, faces, inner, EDGE, row_count - 2 * EDGE)

    def polar_device(south):
        band_step(south, field, offset, part, east, from_west, block_matrix, wide)
        first, _ = near_pole(south, row_count)
        inner_rows(
            wide, north, faces, inner, first + POLAR if south else EDGE, row_count - 2 * EDGE - POLAR
        )

    by_place(
        lat_count, away, functools.partial(polar_device, True), functools.partial(polar_device, False)
    )


def near_pole(south, row_count):
    return (EDGE, POLAR) if south else (row_count - EDGE - POLAR, POLAR)


def inner_rows(wide, north, faces, result, first, count):
    for t in range(wide.shape[0]):
        faces[t, :count] = merid_flux(wide, t, north[first : first + count], first, count)
        end = first + count
        faces[t, count : count + 1] = merid_flux(wide, t, north[end : end + 1], end, 1)
        result[t, first - EDGE : end - EDGE] = wide[t, first:end] - (
            faces[t, 1 : 1 + count] - faces[t, :count]
        )


def with_sides(west, own, east):
    beside = jnp.where(lanes(own.shape) < own.shape[1] // 2, east, west)
    return jnp.concatenate([own, beside], axis=1)


def unpacked(ref, rows, lane, depth):
    value = ref[rows]
    return jnp.concatenate([rolled(value, lane - t * SEG) for t in range(depth)], axis=0)


def stacked(ref, rows):
    return ref[:, rows, :].reshape(-1, ref.shape[2])


def row_values(offset, part, east, rows):
    beyond = east[rows]
    return (
        offset[rows],
        part[rows],
        pick(beyond, jnp.full(beyond.shape, OFF_LANE, i32)).astype(i32),
        pick(beyond, jnp.full(beyond.shape, FRAC_LANE, i32)),
    )


def band_step(south, field, offset, part, east, from_west, block_matrix, wide):
    depth, row_count, cells = field.shape
    base, band, _, mid = (int(place) for place in static_places(south, row_count))
    rows = pl.ds(band, BAND)
    own = stacked(field, rows)
    half = cells // 2
    pair = from_west[mid : mid + BAND], from_west[mid + BAND : mid + 2 * BAND]
    lane = lanes(pair[0].shape)
    rest = jnp.where(lane % SEG >= WEST, pair[0], rolled(pair[1], -WEST))
    west = []
    for t in range(depth):
        if t < depth - 1:
            value = from_west[base + t // 2 * BAND : base + (t // 2 + 1) * BAND]
            value = rolled(value, half) if t % 2 else value
        else:
            value = rolled(rest, cells - OFF_LANE)
        inner = jnp.where(lane >= half - 3, rolled(rest, half - 3 - 3 * t), 0.0)
        west.append(jnp.where(lane >= half, value, inner))
    west = jnp.concatenate(west, axis=0)
    beyond = unpacked(east, rows, -WEST, depth)
    tables = jnp.concatenate([with_sides(west, own, beyond), with_sides(west, west, own)], axis=0)
    tables = times(tables, block_matrix[...])
    common = row_values(offset, part, east, rows)
    for t in range(depth):
        at = slice(t * BAND, (t + 1) * BAND)
        both = [split(tables[first : first + BAND], cells) for first in (t * BAND, (depth + t) * BAND)]
        wide[t, rows] = band_rows(both, own[at], west[at], *common)


def static_places(south, row_count):
    return (0, POLAR, 0, POLE) if south else (row_count - POLE, row_count - POLE, row_count - POLAR, 0)


def edge_rows(lat_count, wide, north, message_b, message_a, low, high, result):
    depth, row_count, cells = wide.shape
    lat = lax.axis_index("lat")
    even = lat % 2 == 0
    south, top = lat == 0, lat == lat_count - 1
    end = 3 * depth
    north_courant = jnp.where(even, message_a[end : end + 1], message_b[end : end + 1])
    north_courant = jnp.where(top, 0.0, north_courant)
    first_row = lax.broadcasted_iota(i32, (EDGE, cells), 0)
    low_courant = jnp.where(south & (first_row == 0), 0.0, north[:EDGE])
    high_next = jnp.concatenate([north[row_count - EDGE + 1 :], north_courant], axis=0)
    for t in range(depth):
        rows = slice(3 * t, 3 * t + 3)
        from_a, from_b = message_a[rows], message_b[rows]
        low[t, EDGE - 3 : EDGE] = jnp.where(south, 0.0, jnp.where(even, from_b, from_a))
        low[t, EDGE : 3 * EDGE] = wide[t, : 2 * EDGE]
        high[t, : 2 * EDGE] = wide[t, row_count - 2 * EDGE :]
        high[t, 2 * EDGE : 2 * EDGE + 3] = jnp.where(top, 0.0, jnp.where(even, from_a, from_b))
    for t in range(depth):
        south_face = merid_flux(low, t, low_courant, EDGE, EDGE)
        north_face = merid_flux(low, t, north[1 : EDGE + 1], EDGE + 1, EDGE)
        result[0, t] = low[t, EDGE : 2 * EDGE] - (north_face - south_face)
        south_face = merid_flux(high, t, north[row_count - EDGE :], EDGE, EDGE)
        north_face = merid_flux(high, t, high_next, EDGE + 1, EDGE)
        result[1, t] = high[t, EDGE : 2 * EDGE] - (north_face - south_face)


def copy_edges(result, out, sems):
    row_count = out.shape[1]
    return [
        pltpu.make_async_copy(result.at[i], out.at[:, pl.ds(first, EDGE)], sems.at[i])
        for i, first in enumerate((0, row_count - EDGE))
    ]


def poles_kernel(
    lat_count, field, offset, part, north, block_matrix, east, far, from_west, pole_two, message_b, message_a,
    given_wide, given_inner, wide, inner, out, faces, low, high, result, sems,
):
    del given_wide, given_inner

    def polar_device(south):
        depth, row_count, cells = field.shape
        near, beside = near_pole(south, row_count)
        done = near + POLAR if south else EDGE
        count = row_count - 2 * EDGE - POLAR
        copies = [
            pltpu.make_async_copy(
                inner.at[:, pl.ds(first - EDGE, size)], out.at[:, pl.ds(first, size)], sems.at[2 + i]
            )
            for i, (first, size) in enumerate(((done, count), (near, beside)))
        ]
        copies[0].start()
        first = static_places(south, row_count)[2]
        rows = pl.ds(first, POLAR)
        own, west, west_two = stacked(field, rows), from_west[row_count:], pole_two[...]
        beyond = unpacked(far, rows, cells - WEST, depth)
        tables = jnp.concatenate(
            [with_sides(west_two, west, own), with_sides(beyond, west_two, west)], axis=0
        )
        tables = times(tables, block_matrix[...])
        own_tables = times(own, block_matrix[:cells])
        common = row_values(offset, part, east, rows)
        for t in range(depth):
            at = slice(t * POLAR, (t + 1) * POLAR)
            one, two = (
                split(tables[start : start + POLAR], cells) for start in (t * POLAR, (depth + t) * POLAR)
            )
            wide[t, rows] = polar_rows(
                (split(own_tables[at], cells), one, two), own[at], west[at], west_two[at], *common
            )
        inner_rows(wide, north, faces, inner, near, beside)
        copies[1].start()
        edge_rows(lat_count, wide, north, message_b, message_a, low, high, result)
        copies += copy_edges(result, out, sems)
        for copy in copies[2:]:
            copy.start()
        for copy in copies:
            copy.wait()

    by_place(
        lat_count, None, functools.partial(polar_device, True), functools.partial(polar_device, False)
    )


def last_kernel(
    lat_count, wide, inner, north, message_b, message_a, given_out, out, low, high, result, sems
):
    del given_out

    def away():
        count = inner.shape[1]
        inner_copy = pltpu.make_async_copy(inner, out.at[:, pl.ds(EDGE, count)], sems.at[2])
        inner_copy.start()
        edge_rows(lat_count, wide, north, message_b, message_a, low, high, result)
        copies = copy_edges(result, out, sems)
        for copy in copies:
            copy.start()
        for copy in (inner_copy, *copies):
            copy.wait()

    lat = lax.axis_index("lat")
    pl.when((lat > 0) & (lat < lat_count - 1))(away)


def cost(microseconds):
    return pl.CostEstimate(
        flops=int(microseconds * 1e8), bytes_accessed=int(microseconds * 3e6), transcendentals=0
    )


def in_vmem(*values):
    return [pltpu.with_memory_space_constraint(value, VMEM) for value in values]


def whole(count):
    return [pl.BlockSpec(memory_space=VMEM)] * count


def anywhere(count):
    return [pl.BlockSpec(memory_space=pl.ANY)] * count


def on_device(lat_count, lon_count, tracers, offsets, fraction, courant_north):
    tracer_count, level_count, row_count, cells = tracers.shape
    depth = tracer_count * level_count
    shape = (row_count, cells)
    stack = (depth, row_count, cells)
    dma = pltpu.SemaphoreType.DMA

    partner = {l: l ^ 1 for l in range(2, lat_count - 2)}
    if lat_count % 2 == 0 and lat_count >= 8:
        for l, other in ((1, 3), (2, lat_count - 2)):
            partner[l], partner[other] = other, l

    def along_lon(value, steps, everywhere=True):
        pairs = []
        for l in range(lat_count):
            for o in range(lon_count):
                if everywhere or len(partner) < lat_count - 2 or l in (0, lat_count - 1):
                    target = (l, (o + steps) % lon_count)
                else:
                    target = (partner[l], o)
                pairs.append((l * lon_count + o, target[0] * lon_count + target[1]))
        return lax.ppermute(value, ("lat", "lon"), pairs)

    def along_lat(value, first):
        pairs = []
        for l in range(lat_count):
            other = l + 1 if (l - first) % 2 == 0 else l - 1
            for o in range(lon_count):
                if 0 <= other < lat_count:
                    target = (other, o)
                else:
                    target = (l, (o + 1) % lon_count if lon_count % 2 else o ^ 1)
                pairs.append((l * lon_count + o, target[0] * lon_count + target[1]))
        return lax.ppermute(value, ("lat", "lon"), pairs)

    field, offset, part, north, packed, to_east, to_west, pole = in_vmem(
        *pl.pallas_call(
            functools.partial(pack_kernel, lat_count),
            out_shape=[
                VMEM(stack, f32),
                VMEM(shape, i32),
                VMEM(shape, f32),
                VMEM(shape, f32),
                VMEM(shape, f32),
                VMEM((row_count + depth * POLAR, cells), f32),
                VMEM((row_count // 2, cells), f32),
                VMEM((depth * POLAR, cells), f32),
            ],
            in_specs=anywhere(4),
            out_specs=whole(8),
            scratch_shapes=[dma((4,))],
            cost_estimate=cost(1.0),
            name="pack",
        )(tracers.reshape(stack), offsets, fraction, courant_north)
    )
    from_west = along_lon(to_east, 1)
    from_east = along_lon(to_west, -1)
    from_far = from_east if lon_count == 4 else along_lon(to_west, 3)
    pole_two = along_lon(pole, 2, False)

    flux, seam_index, seam_part, block_matrix, seam_matrix = in_vmem(
        *pl.pallas_call(
            functools.partial(own_kernel, lat_count),
            out_shape=[
                VMEM(stack, f32),
                VMEM((2, *shape), i32),
                VMEM((2, *shape), f32),
                VMEM((2 * cells, 4 * cells), bf16),
                VMEM((cells, 3 * cells), bf16),
            ],
            in_specs=whole(3),
            out_specs=whole(5),
            cost_estimate=cost(2.0),
            name="own",
        )(field, offset, part)
    )
    from_west, from_east, from_far, pole_two = in_vmem(from_west, from_east, from_far, pole_two)

    message = (3 * depth + 1, cells)
    longer = 56
    message_a, message_b, wide, east = in_vmem(
        *pl.pallas_call(
            functools.partial(edge_kernel, lat_count),
            out_shape=[VMEM(message, f32), VMEM((longer, cells), f32), VMEM(stack, f32), VMEM(shape, f32)],
            in_specs=whole(9),
            out_specs=whole(4),
            cost_estimate=cost(4.0),
            name="edge",
        )(field, flux, packed, seam_index, seam_part, seam_matrix, north, from_east, from_west)
    )
    message_a = along_lat(message_a, 0)
    message_b = along_lat(message_b, 1)

    inner = VMEM((depth, row_count - 2 * EDGE, cells), f32)
    faces = VMEM((depth, row_count - EDGE, cells), f32)
    wide, east, inner_part, far = in_vmem(
        *pl.pallas_call(
            functools.partial(middle_kernel, lat_count),
            out_shape=[VMEM(stack, f32), VMEM(shape, f32), inner, VMEM(shape, f32)],
            in_specs=whole(15),
            out_specs=whole(4),
            scratch_shapes=[faces],
            input_output_aliases={13: 0, 14: 1},
            cost_estimate=cost(3.0),
            name="middle",
        )(
            field, offset, part, north, flux, packed, seam_index, seam_part, seam_matrix, block_matrix,
            from_east, from_far, from_west, wide, east,
        )
    )

    message_a, message_b = in_vmem(message_a, message_b)
    scratch = [
        VMEM((depth, 3 * EDGE, cells), f32),
        VMEM((depth, 3 * EDGE, cells), f32),
        VMEM((2, depth, EDGE, cells), f32),
        dma((4,)),
    ]
    polar_b = message_b if lat_count % 2 else message_a
    wide, inner, out = pl.pallas_call(
        functools.partial(poles_kernel, lat_count),
        out_shape=[VMEM(stack, f32), inner, jax.ShapeDtypeStruct(stack, f32)],
        in_specs=whole(13),
        out_specs=whole(2) + anywhere(1),
        scratch_shapes=[faces, *scratch],
        input_output_aliases={11: 0, 12: 1},
        cost_estimate=cost(0.0),
        name="poles",
    )(
        field, offset, part, north, block_matrix, east, far, from_west, pole_two, polar_b, message_a,
        wide, inner_part,
    )

    out = pl.pallas_call(
        functools.partial(last_kernel, lat_count),
        out_shape=jax.ShapeDtypeStruct(stack, f32),
        in_specs=whole(5) + anywhere(1),
        out_specs=pl.BlockSpec(memory_space=pl.ANY),
        scratch_shapes=scratch,
        input_output_aliases={5: 0},
        cost_estimate=cost(0.7),
        name="last",
    )(*in_vmem(wide, inner), north, message_b, message_a, out)
    return out.reshape(tracers.shape)


def solution(mesh):
    placed = (P(None, None, "lat", "lon"), P("lat", "lon"), P("lat", "lon"), P("lat", "lon"))
    return jax.shard_map(
        functools.partial(on_device, mesh.shape["lat"], mesh.shape["lon"]),
        mesh=mesh,
        in_specs=placed,
        out_specs=P(None, None, "lat", "lon"),
        check_vma=False,
    )
```

```python
import functools

import jax
import jax.numpy as jnp
from jax import lax
from jax.experimental import pallas as pl
from jax.experimental.pallas import tpu as pltpu
from jax.sharding import PartitionSpec as P

POLAR = 24
BAND = 24
POLE = POLAR + BAND
WEST = 12
SEG = 24
FACES = 11
OFF_LANE = 120
FRAC_LANE = 121
PAIR = 4
EDGE = 8

f32 = jnp.float32
bf16 = jnp.bfloat16
i32 = jnp.int32
VMEM = pltpu.VMEM


def lanes(shape):
    return lax.broadcasted_iota(i32, shape, 1)


def rolled(value, steps):
    steps = steps % value.shape[1]
    return pltpu.roll(value, steps, 1) if steps else value


def pick(table, index):
    return jnp.take_along_axis(table, index, axis=1, mode="promise_in_bounds")


def parabola(c, right, left, centre):
    jump = right - left
    curve = 72.0 * centre - 3.0 * (left + right)
    return c * (1 / 12) * (right - 0.5 * c * (jump - (1.0 - (2.0 / 3.0) * c) * curve))


def times(value, matrix):
    high = value.astype(bf16)
    low = (value - high.astype(f32)).astype(bf16)
    return jnp.dot(jnp.concatenate([high, low], axis=1), matrix, preferred_element_type=f32)


def for_west(packed):
    half, cells = packed.shape[0] // 2, packed.shape[1]
    lane = lanes((half, cells))
    place = lane % SEG
    first = (lane >= OFF_LANE) & (lane < OFF_LANE + 2)
    first = first | ((lane < OFF_LANE) & (place >= WEST - 2) & (place < WEST + 2))
    return jnp.where(first, packed[:half], rolled(packed[half:], PAIR))


def edge_weights(gap):
    def weight(gap):
        inner = (gap == 0) | (gap == 1)
        outer = (gap == -1) | (gap == 2)
        return jnp.where(inner, 7.0, jnp.where(outer, -1.0, 0.0))

    return weight(gap), weight(gap + 1)


def split(table, cells):
    return [table[:, i : i + cells] for i in range(0, table.shape[1], cells)]


def pack_kernel(
    lat_count, tracers, offsets, fraction, courant,
    field, offset, part, north, packed, to_east, to_west, pole, sems,
):
    depth, row_count, cells = field.shape
    copies = [
        pltpu.make_async_copy(source, target, sems.at[i])
        for i, (source, target) in enumerate(
            ((tracers, field), (offsets, offset), (fraction, part), (courant, north))
        )
    ]
    for copy in copies:
        copy.start()
    for copy in copies[:3]:
        copy.wait()
    shape = (row_count, cells)
    lane = lanes(shape)
    message = jnp.where(
        lane == OFF_LANE,
        rolled(offset[...].astype(f32), OFF_LANE),
        jnp.where(lane == FRAC_LANE, rolled(part[...], FRAC_LANE), 0.0),
    )
    for t in range(depth):
        mine = (lane >= t * SEG) & (lane < (t + 1) * SEG)
        message = jnp.where(mine, rolled(field[t], t * SEG + WEST), message)
    packed[...] = message
    to_east[...] = message
    to_west[...] = for_west(message)
    lat = lax.axis_index("lat")
    south = lat == 0

    @pl.when(south | (lat == lat_count - 1))
    def _():
        base, band, polar, mid = pole_places(south, row_count)
        rows = [field[t, pl.ds(band, BAND)] for t in range(depth)]
        lane = lanes(rows[0].shape)
        half = cells // 2
        for t in range(0, depth - 1, 2):
            value = jnp.where(lane >= half, rows[t], rolled(rows[t + 1], half))
            to_east[pl.ds(pl.multiple_of(base + t // 2 * BAND, 8), BAND)] = value
        rest = rolled(rows[depth - 1], OFF_LANE - cells)
        for t in range(depth):
            mine = (lane >= 3 * t) & (lane < 3 * t + 3)
            rest = jnp.where(mine, rolled(rows[t], 3 * t + 3 - half), rest)
        kept = (lane % SEG < WEST) | (lane >= OFF_LANE)
        for i, value in enumerate((rest, rolled(rest, WEST))):
            at = pl.ds(pl.multiple_of(mid + i * BAND, 8), BAND)
            to_east[at] = jnp.where(kept, to_east[at], value)
        for t in range(depth):
            pole[t * POLAR : (t + 1) * POLAR] = field[t, pl.ds(polar, POLAR)]
    copies[3].wait()


def pole_places(south, row_count):
    places = (
        jnp.where(south, 0, row_count - POLE),
        jnp.where(south, POLAR, row_count - POLE),
        jnp.where(south, 0, row_count - POLAR),
        jnp.where(south, POLE, 0),
    )
    return [pl.multiple_of(place, 8) for place in places]


def by_place(lat_count, away, south, north):
    lat = lax.axis_index("lat")
    if away is not None:
        pl.when((lat > 0) & (lat < lat_count - 1))(away)
    pl.when(lat == 0)(south)
    pl.when(lat == lat_count - 1)(north)


def pieces(row_count):
    middle = [(POLE, row_count - 2 * POLE)] if row_count > 2 * POLE else []
    return [(0, POLE), *middle, (row_count - POLE, POLE)]


def mid_pieces(row_count):
    return pieces(row_count), pieces(row_count)[1:], pieces(row_count)[:-1]


def own_faces(first_row, count, field, offset, part, own_matrix, flux, seam_index, seam_part):
    depth, _, cells = field.shape
    at = pl.ds(first_row, count)
    shape = (count, cells)
    lane = lanes(shape)
    place = lane % SEG
    offsets = offset[at]
    courant = part[at]
    index = (lane - offsets - 1) & (cells - 1)
    own = field[:, at].reshape(depth * count, cells)
    tables = times(own, own_matrix[...])
    for t in range(depth):
        sums, right, left = split(tables[t * count : (t + 1) * count], cells)
        value = field[t, at]
        flux[t, at] = (
            sums
            - value
            - pick(sums, index)
            + parabola(
                courant, pick(right, index), pick(left, index), pick(value, index)
            )
        )
    first = (place - WEST) & (cells - 1)
    final = jnp.full(shape, cells - 1, i32)
    seam_index[0, at] = (lane - pick(offsets, first) - 1) & (cells - 1)
    seam_index[1, at] = (lane - pick(offsets, final) - 1) & (cells - 1)
    seam_part[0, at] = pick(courant, first)
    seam_part[1, at] = pick(courant, final)


def own_kernel(
    lat_count, field, offset, part, flux, seam_index, seam_part, block_matrix, seam_matrix, own_matrix
):
    _, row_count, cells = field.shape
    shape = (cells, cells)
    source = lax.broadcasted_iota(i32, shape, 0)
    target = lax.broadcasted_iota(i32, shape, 1)
    gap = source - target
    upto = jnp.where(gap <= 0, 1.0, 0.0)
    right, left = edge_weights(gap)
    own = jnp.concatenate([upto, right, left, upto - 1.0], axis=1).astype(bf16)
    zeros = jnp.zeros(shape, f32)
    beyond = gap + jnp.where(source < cells // 2, cells, -cells)
    beside = jnp.concatenate([zeros, *edge_weights(beyond), zeros], axis=1).astype(bf16)
    together = source // SEG == target // SEG
    seam = jnp.concatenate([jnp.where(together, upto, 0.0), right, left], axis=1).astype(bf16)
    for i in range(2):
        block_matrix[2 * i * cells : (2 * i + 1) * cells] = own
        block_matrix[(2 * i + 1) * cells : (2 * i + 2) * cells] = beside
        own_matrix[i * cells : (i + 1) * cells] = own[:, : 3 * cells]
        seam_matrix[i * cells : (i + 1) * cells] = seam

    def step(parts):
        for first, count in parts:
            own_faces(first, count, field, offset, part, own_matrix, flux, seam_index, seam_part)

    by_place(lat_count, *(functools.partial(step, parts) for parts in mid_pieces(row_count)))


def rows_after(field, flux, packed, seam_index, seam_part, from_west, from_east, seam_matrix, parts):
    def take(ref, *lead):
        return jnp.concatenate([ref[(*lead, part)] for part in parts], axis=0)

    mine, west = take(packed), take(from_west)
    east = from_east if isinstance(from_east, jax.Array) else take(from_east)
    count, cells = mine.shape
    shape = mine.shape
    lane = lanes(shape)
    place = lane % SEG
    near = place < WEST
    rows = jnp.concatenate([jnp.where(near, west, mine), jnp.where(near, mine, east)], axis=0)
    next_face = place == WEST
    next_offset = pick(east, jnp.full(shape, OFF_LANE, i32)).astype(i32)
    next_part = pick(east, jnp.full(shape, FRAC_LANE, i32))
    next_index = (lane - next_offset - 1) & (cells - 1)
    index = jnp.concatenate(
        [take(seam_index, 0), jnp.where(next_face, next_index, take(seam_index, 1))], axis=0
    )
    courant = jnp.concatenate(
        [take(seam_part, 0), jnp.where(next_face, next_part, take(seam_part, 1))], axis=0
    )
    sums, right, left = split(times(rows, seam_matrix[...]), cells)
    faces = (
        sums
        - rows
        - pick(sums, index)
        + parabola(
            courant, pick(right, index), pick(left, index), pick(rows, index)
        )
    )
    east_faces = faces[count:]
    both = jnp.where(place == WEST - 1, east_faces, faces[:count])
    outside = (lane < FACES) | (lane == cells - 1)
    results = []
    for t in range(field.shape[0]):
        steps = -(t * SEG + WEST)
        face = jnp.where(outside, rolled(both, steps), take(flux, t))
        following = jnp.where(lane == cells - 1, rolled(east_faces, steps - 1), rolled(face, -1))
        results.append(take(field, t) - (following - face))
    return results


def edge_kernel(
    lat_count, field, flux, packed, seam_index, seam_part, seam_matrix, north, from_east, from_west,
    message_a, message_b, wide, east,
):
    depth, row_count, _ = field.shape
    half = row_count // 2
    even = lax.axis_index("lat") % 2 == 0

    def step(parts, beyond):
        return rows_after(
            field, flux, packed, seam_index, seam_part, from_west, beyond, seam_matrix, parts
        )

    def send(t, top, bottom):
        rows = slice(3 * t, 3 * t + 3)
        message_a[rows] = jnp.where(even, top, bottom)
        message_b[rows] = jnp.where(even, bottom, top)

    def away():
        beyond = jnp.concatenate(
            [from_east[:EDGE], rolled(from_east[half - EDGE :], -PAIR)], axis=0
        )
        after = step((pl.ds(0, EDGE), pl.ds(row_count - EDGE, EDGE)), beyond)
        for t in range(depth):
            send(t, after[t][2 * EDGE - 3 :], after[t][:3])

    def polar_device(parts):
        east[:half] = from_east[...]
        east[half:] = rolled(from_east[...], -PAIR)
        for first, count in parts:
            after = step((pl.ds(first, count),), east)
            for t in range(depth):
                wide[t, first : first + count] = after[t]
        for t in range(depth):
            send(t, wide[t, row_count - 3 :], wide[t, :3])

    by_place(
        lat_count, away, *(functools.partial(polar_device, parts) for parts in mid_pieces(row_count)[1:])
    )
    message_a[3 * depth : 3 * depth + 1] = north[:1]
    message_b[3 * depth : 3 * depth + 1] = north[:1]


def rows_between(near, far, near_field, far_field, first, offset, courant, next_offset, next_courant):
    cells = near_field.shape[1]
    lane = lanes(near_field.shape)
    source = lane - offset - 1
    index = source & (cells - 1)
    close = source >= first

    def both(here, there):
        return jnp.where(close, pick(here, index), pick(there, index))

    face = both(near[0], far[3]) - parabola(
        courant, both(near[1], far[1]), both(near[2], far[2]), both(near_field, far_field)
    )
    last = near[0] - parabola(next_courant, near[1], near[2], near_field)
    last = pick(last, (cells - 1 - next_offset) & (cells - 1))
    return rolled(jnp.where(lane == 0, last, face), -1) - face


def merid_flux(wide, t, courant, first, count):
    cell = [wide[t, first + k : first + k + count] for k in (-3, -2, -1, 0, 1)]
    left = 7.0 * (cell[1] + cell[2]) - (cell[0] + cell[3])
    right = 7.0 * (cell[2] + cell[3]) - (cell[1] + cell[4])
    return parabola(courant, right, left, cell[2])


def middle_kernel(
    lat_count, field, offset, part, north, flux, packed, seam_index, seam_part, seam_matrix, block_matrix,
    from_east, from_far, from_west, given_wide, given_east, wide, east, inner, far, faces,
):
    del given_wide, given_east
    depth, row_count, cells = field.shape
    half = row_count // 2
    far[:half] = from_far[...]
    far[half:] = rolled(from_far[...], -PAIR)

    def away():
        east[:half] = from_east[...]
        east[half:] = rolled(from_east[...], -PAIR)
        for first, count in pieces(row_count):
            after = rows_after(
                field, flux, packed, seam_index, seam_part, from_west, east, seam_matrix, (pl.ds(first, count),)
            )
            for t in range(depth):
                wide[t, first : first + count] = after[t]
        inner_rows(wide, north, faces, inner, EDGE, row_count - 2 * EDGE)

    def polar_device(south):
        band_step(south, field, offset, part, east, from_west, block_matrix, wide)
        first, _ = near_pole(south, row_count)
        inner_rows(
            wide, north, faces, inner, first + POLAR if south else EDGE, row_count - 2 * EDGE - POLAR
        )

    by_place(
        lat_count, away, functools.partial(polar_device, True), functools.partial(polar_device, False)
    )


def near_pole(south, row_count):
    return (EDGE, POLAR) if south else (row_count - EDGE - POLAR, POLAR)


def inner_rows(wide, north, faces, result, first, count):
    for t in range(wide.shape[0]):
        faces[t, :count] = merid_flux(wide, t, north[first : first + count], first, count)
        end = first + count
        faces[t, count : count + 1] = merid_flux(wide, t, north[end : end + 1], end, 1)
        result[t, first - EDGE : end - EDGE] = wide[t, first:end] - (
            faces[t, 1 : 1 + count] - faces[t, :count]
        )


def with_sides(west, own, east):
    beside = jnp.where(lanes(own.shape) < own.shape[1] // 2, east, west)
    return jnp.concatenate([own, beside], axis=1)


def unpacked(ref, rows, lane, depth):
    value = ref[rows]
    return jnp.concatenate([rolled(value, lane - t * SEG) for t in range(depth)], axis=0)


def stacked(ref, rows):
    return ref[:, rows, :].reshape(-1, ref.shape[2])


def row_values(offset, part, east, rows):
    beyond = east[rows]
    return (
        offset[rows],
        part[rows],
        pick(beyond, jnp.full(beyond.shape, OFF_LANE, i32)).astype(i32),
        pick(beyond, jnp.full(beyond.shape, FRAC_LANE, i32)),
    )


def band_step(south, field, offset, part, east, from_west, block_matrix, wide):
    depth, row_count, cells = field.shape
    base, band, _, mid = (int(place) for place in static_places(south, row_count))
    rows = pl.ds(band, BAND)
    own = stacked(field, rows)
    half = cells // 2
    pair = from_west[mid : mid + BAND], from_west[mid + BAND : mid + 2 * BAND]
    lane = lanes(pair[0].shape)
    rest = jnp.where(lane % SEG >= WEST, pair[0], rolled(pair[1], -WEST))
    west = []
    for t in range(depth):
        if t < depth - 1:
            value = from_west[base + t // 2 * BAND : base + (t // 2 + 1) * BAND]
            value = rolled(value, half) if t % 2 else value
        else:
            value = rolled(rest, cells - OFF_LANE)
        inner = jnp.where(lane >= half - 3, rolled(rest, half - 3 - 3 * t), 0.0)
        west.append(jnp.where(lane >= half, value, inner))
    west = jnp.concatenate(west, axis=0)
    beyond = unpacked(east, rows, -WEST, depth)
    tables = jnp.concatenate([with_sides(west, own, beyond), with_sides(west, west, own)], axis=0)
    tables = times(tables, block_matrix[...])
    common = row_values(offset, part, east, rows)
    for t in range(depth):
        at = slice(t * BAND, (t + 1) * BAND)
        both = [split(tables[first : first + BAND], cells) for first in (t * BAND, (depth + t) * BAND)]
        wide[t, rows] = rows_between(*both, own[at], west[at], 0, *common)


def static_places(south, row_count):
    return (0, POLAR, 0, POLE) if south else (row_count - POLE, row_count - POLE, row_count - POLAR, 0)


def edge_rows(lat_count, wide, north, message_b, message_a, low, high, result):
    depth, row_count, cells = wide.shape
    lat = lax.axis_index("lat")
    even = lat % 2 == 0
    south, top = lat == 0, lat == lat_count - 1
    end = 3 * depth
    north_courant = jnp.where(even, message_a[end : end + 1], message_b[end : end + 1])
    north_courant = jnp.where(top, 0.0, north_courant)
    first_row = lax.broadcasted_iota(i32, (EDGE, cells), 0)
    low_courant = jnp.where(south & (first_row == 0), 0.0, north[:EDGE])
    high_next = jnp.concatenate([north[row_count - EDGE + 1 :], north_courant], axis=0)
    for t in range(depth):
        rows = slice(3 * t, 3 * t + 3)
        from_a, from_b = message_a[rows], message_b[rows]
        low[t, EDGE - 3 : EDGE] = jnp.where(south, 0.0, jnp.where(even, from_b, from_a))
        low[t, EDGE : 3 * EDGE] = wide[t, : 2 * EDGE]
        high[t, : 2 * EDGE] = wide[t, row_count - 2 * EDGE :]
        high[t, 2 * EDGE : 2 * EDGE + 3] = jnp.where(top, 0.0, jnp.where(even, from_a, from_b))
    for t in range(depth):
        south_face = merid_flux(low, t, low_courant, EDGE, EDGE)
        north_face = merid_flux(low, t, north[1 : EDGE + 1], EDGE + 1, EDGE)
        result[0, t] = low[t, EDGE : 2 * EDGE] - (north_face - south_face)
        south_face = merid_flux(high, t, north[row_count - EDGE :], EDGE, EDGE)
        north_face = merid_flux(high, t, high_next, EDGE + 1, EDGE)
        result[1, t] = high[t, EDGE : 2 * EDGE] - (north_face - south_face)


def copy_edges(result, out, sems):
    row_count = out.shape[1]
    return [
        pltpu.make_async_copy(result.at[i], out.at[:, pl.ds(first, EDGE)], sems.at[i])
        for i, first in enumerate((0, row_count - EDGE))
    ]


def poles_kernel(
    lat_count, field, offset, part, north, block_matrix, east, far, pole_one, pole_two, message_b, message_a,
    given_wide, given_inner, wide, inner, out, faces, low, high, result, sems,
):
    del given_wide, given_inner

    def polar_device(south):
        depth, row_count, cells = field.shape
        near, beside = near_pole(south, row_count)
        done = near + POLAR if south else EDGE
        count = row_count - 2 * EDGE - POLAR
        copies = [
            pltpu.make_async_copy(
                inner.at[:, pl.ds(first - EDGE, size)], out.at[:, pl.ds(first, size)], sems.at[2 + i]
            )
            for i, (first, size) in enumerate(((done, count), (near, beside)))
        ]
        copies[0].start()
        first = static_places(south, row_count)[2]
        rows = pl.ds(first, POLAR)
        own, west, west_two = stacked(field, rows), pole_one[...], pole_two[...]
        beyond = unpacked(far, rows, cells - WEST, depth)
        tables = jnp.concatenate(
            [with_sides(west_two, west, own), with_sides(beyond, west_two, west)], axis=0
        )
        tables = times(tables, block_matrix[...])
        common = row_values(offset, part, east, rows)
        for t in range(depth):
            at = slice(t * POLAR, (t + 1) * POLAR)
            both = [split(tables[start : start + POLAR], cells) for start in (t * POLAR, (depth + t) * POLAR)]
            wide[t, rows] = rows_between(*both, west[at], west_two[at], -cells, *common)
        inner_rows(wide, north, faces, inner, near, beside)
        copies[1].start()
        edge_rows(lat_count, wide, north, message_b, message_a, low, high, result)
        copies += copy_edges(result, out, sems)
        for copy in copies[2:]:
            copy.start()
        for copy in copies:
            copy.wait()

    by_place(
        lat_count, None, functools.partial(polar_device, True), functools.partial(polar_device, False)
    )


def last_kernel(
    lat_count, wide, inner, north, message_b, message_a, given_out, out, low, high, result, sems
):
    del given_out

    def away():
        count = inner.shape[1]
        inner_copy = pltpu.make_async_copy(inner, out.at[:, pl.ds(EDGE, count)], sems.at[2])
        inner_copy.start()
        edge_rows(lat_count, wide, north, message_b, message_a, low, high, result)
        copies = copy_edges(result, out, sems)
        for copy in copies:
            copy.start()
        for copy in (inner_copy, *copies):
            copy.wait()

    lat = lax.axis_index("lat")
    pl.when((lat > 0) & (lat < lat_count - 1))(away)


def cost(microseconds):
    return pl.CostEstimate(
        flops=int(microseconds * 1e8), bytes_accessed=int(microseconds * 3e6), transcendentals=0
    )


def in_vmem(*values):
    return [pltpu.with_memory_space_constraint(value, VMEM) for value in values]


def whole(count):
    return [pl.BlockSpec(memory_space=VMEM)] * count


def anywhere(count):
    return [pl.BlockSpec(memory_space=pl.ANY)] * count


def on_device(lat_count, lon_count, tracers, offsets, fraction, courant_north):
    tracer_count, level_count, row_count, cells = tracers.shape
    depth = tracer_count * level_count
    shape = (row_count, cells)
    stack = (depth, row_count, cells)
    dma = pltpu.SemaphoreType.DMA

    partner = {l: l ^ 1 for l in range(2, lat_count - 2)}
    if lat_count % 2 == 0 and lat_count >= 8:
        for l, other in ((1, 3), (2, lat_count - 2)):
            partner[l], partner[other] = other, l

    def along_lon(value, steps, everywhere=True):
        pairs = []
        for l in range(lat_count):
            for o in range(lon_count):
                if everywhere or len(partner) < lat_count - 2 or l in (0, lat_count - 1):
                    target = (l, (o + steps) % lon_count)
                else:
                    target = (partner[l], o)
                pairs.append((l * lon_count + o, target[0] * lon_count + target[1]))
        return lax.ppermute(value, ("lat", "lon"), pairs)

    def along_lat(value, first):
        pairs = []
        last_lat, last_lon = lat_count - 1, lon_count - 1
        for l in range(lat_count):
            other = l + 1 if (l - first) % 2 == 0 else l - 1
            for o in range(lon_count):
                if 0 <= other < lat_count:
                    target = (other, o)
                elif lat_count % 2:
                    target = (l, (o + 1) % lon_count)
                elif l == 0:
                    target = (0, o - 1) if o else (last_lat, 0)
                else:
                    target = (last_lat, o + 1) if o < last_lon else (0, last_lon)
                pairs.append((l * lon_count + o, target[0] * lon_count + target[1]))
        return lax.ppermute(value, ("lat", "lon"), pairs)

    field, offset, part, north, packed, to_east, to_west, pole = in_vmem(
        *pl.pallas_call(
            functools.partial(pack_kernel, lat_count),
            out_shape=[
                VMEM(stack, f32),
                VMEM(shape, i32),
                VMEM(shape, f32),
                VMEM(shape, f32),
                VMEM(shape, f32),
                VMEM(shape, f32),
                VMEM((row_count // 2, cells), f32),
                VMEM((depth * POLAR, cells), f32),
            ],
            in_specs=anywhere(4),
            out_specs=whole(8),
            scratch_shapes=[dma((4,))],
            cost_estimate=cost(1.0),
            name="pack",
        )(tracers.reshape(stack), offsets, fraction, courant_north)
    )
    from_west = along_lon(to_east, 1)
    from_east = along_lon(to_west, -1)
    from_far = from_east if lon_count == 4 else along_lon(to_west, 3)
    pole_one = along_lon(pole, 1, False)
    pole_two = along_lon(pole, 2, False)

    flux, seam_index, seam_part, block_matrix, seam_matrix = in_vmem(
        *pl.pallas_call(
            functools.partial(own_kernel, lat_count),
            out_shape=[
                VMEM(stack, f32),
                VMEM((2, *shape), i32),
                VMEM((2, *shape), f32),
                VMEM((4 * cells, 4 * cells), bf16),
                VMEM((2 * cells, 3 * cells), bf16),
            ],
            in_specs=whole(3),
            out_specs=whole(5),
            scratch_shapes=[VMEM((2 * cells, 3 * cells), bf16)],
            cost_estimate=cost(2.0),
            name="own",
        )(field, offset, part)
    )
    from_west, from_east, from_far, pole_one, pole_two = in_vmem(
        from_west, from_east, from_far, pole_one, pole_two
    )

    message = (3 * depth + 1, cells)
    longer = 64
    message_a, message_b, wide, east = in_vmem(
        *pl.pallas_call(
            functools.partial(edge_kernel, lat_count),
            out_shape=[VMEM(message, f32), VMEM((longer, cells), f32), VMEM(stack, f32), VMEM(shape, f32)],
            in_specs=whole(9),
            out_specs=whole(4),
            cost_estimate=cost(4.0),
            name="edge",
        )(field, flux, packed, seam_index, seam_part, seam_matrix, north, from_east, from_west)
    )
    message_a = along_lat(message_a, 0)
    message_b = along_lat(message_b, 1)

    inner = VMEM((depth, row_count - 2 * EDGE, cells), f32)
    faces = VMEM((depth, row_count - EDGE, cells), f32)
    wide, east, inner_part, far = in_vmem(
        *pl.pallas_call(
            functools.partial(middle_kernel, lat_count),
            out_shape=[VMEM(stack, f32), VMEM(shape, f32), inner, VMEM(shape, f32)],
            in_specs=whole(15),
            out_specs=whole(4),
            scratch_shapes=[faces],
            input_output_aliases={13: 0, 14: 1},
            cost_estimate=cost(3.0),
            name="middle",
        )(
            field, offset, part, north, flux, packed, seam_index, seam_part, seam_matrix, block_matrix,
            from_east, from_far, from_west, wide, east,
        )
    )

    message_a, message_b = in_vmem(message_a, message_b)
    scratch = [
        VMEM((depth, 3 * EDGE, cells), f32),
        VMEM((depth, 3 * EDGE, cells), f32),
        VMEM((2, depth, EDGE, cells), f32),
        dma((4,)),
    ]
    polar_b = message_b if lat_count % 2 else message_a
    wide, inner, out = pl.pallas_call(
        functools.partial(poles_kernel, lat_count),
        out_shape=[VMEM(stack, f32), inner, jax.ShapeDtypeStruct(stack, f32)],
        in_specs=whole(13),
        out_specs=whole(2) + anywhere(1),
        scratch_shapes=[faces, *scratch],
        input_output_aliases={11: 0, 12: 1},
        cost_estimate=cost(0.0),
        name="poles",
    )(
        field, offset, part, north, block_matrix, east, far, pole_one, pole_two, polar_b, message_a,
        wide, inner_part,
    )

    out = pl.pallas_call(
        functools.partial(last_kernel, lat_count),
        out_shape=jax.ShapeDtypeStruct(stack, f32),
        in_specs=whole(5) + anywhere(1),
        out_specs=pl.BlockSpec(memory_space=pl.ANY),
        scratch_shapes=scratch,
        input_output_aliases={5: 0},
        cost_estimate=cost(0.7),
        name="last",
    )(*in_vmem(wide, inner), north, message_b, message_a, out)
    return out.reshape(tracers.shape)


def solution(mesh):
    placed = (P(None, None, "lat", "lon"), P("lat", "lon"), P("lat", "lon"), P("lat", "lon"))
    return jax.shard_map(
        functools.partial(on_device, mesh.shape["lat"], mesh.shape["lon"]),
        mesh=mesh,
        in_specs=placed,
        out_specs=P(None, None, "lat", "lon"),
        check_vma=False,
    )
```

```python
import functools

import jax
import jax.numpy as jnp
from jax import lax
from jax.experimental import pallas as pl
from jax.experimental.pallas import tpu as pltpu
from jax.sharding import PartitionSpec as P

POLAR = 24
BAND = 24
POLE = POLAR + BAND
WEST = 12
SEG = 24
FACES = 11
OFF_LANE = 120
FRAC_LANE = 121
PAIR = 4
EDGE = 8

f32 = jnp.float32
bf16 = jnp.bfloat16
i32 = jnp.int32
VMEM = pltpu.VMEM


def lanes(shape):
    return lax.broadcasted_iota(i32, shape, 1)


def rolled(value, steps):
    steps = steps % value.shape[1]
    return pltpu.roll(value, steps, 1) if steps else value


def pick(table, index):
    return jnp.take_along_axis(table, index, axis=1, mode="promise_in_bounds")


def parabola(c, right, left, centre):
    jump = right - left
    curve = 72.0 * centre - 3.0 * (left + right)
    return c * (1 / 12) * (right - 0.5 * c * (jump - (1.0 - (2.0 / 3.0) * c) * curve))


def times(value, matrix):
    high = value.astype(bf16)
    low = (value - high.astype(f32)).astype(bf16)
    return jnp.dot(jnp.concatenate([high, low], axis=1), matrix, preferred_element_type=f32)


def for_west(packed):
    half, cells = packed.shape[0] // 2, packed.shape[1]
    lane = lanes((half, cells))
    place = lane % SEG
    first = (lane >= OFF_LANE) & (lane < OFF_LANE + 2)
    first = first | ((lane < OFF_LANE) & (place >= WEST - 2) & (place < WEST + 2))
    return jnp.where(first, packed[:half], rolled(packed[half:], PAIR))


def edge_weights(gap):
    def weight(gap):
        inner = (gap == 0) | (gap == 1)
        outer = (gap == -1) | (gap == 2)
        return jnp.where(inner, 7.0, jnp.where(outer, -1.0, 0.0))

    return weight(gap), weight(gap + 1)


def split(table, cells):
    return [table[:, i : i + cells] for i in range(0, table.shape[1], cells)]


def pack_kernel(
    lat_count, tracers, offsets, fraction, courant,
    field, offset, part, north, packed, to_east, to_west, pole, sems,
):
    depth, row_count, cells = field.shape
    copies = [
        pltpu.make_async_copy(source, target, sems.at[i])
        for i, (source, target) in enumerate(
            ((tracers, field), (offsets, offset), (fraction, part), (courant, north))
        )
    ]
    for copy in copies:
        copy.start()
    for copy in copies[:3]:
        copy.wait()
    shape = (row_count, cells)
    lane = lanes(shape)
    message = jnp.where(
        lane == OFF_LANE,
        rolled(offset[...].astype(f32), OFF_LANE),
        jnp.where(lane == FRAC_LANE, rolled(part[...], FRAC_LANE), 0.0),
    )
    for t in range(depth):
        mine = (lane >= t * SEG) & (lane < (t + 1) * SEG)
        message = jnp.where(mine, rolled(field[t], t * SEG + WEST), message)
    packed[...] = message
    to_east[...] = message
    to_west[...] = for_west(message)
    lat = lax.axis_index("lat")
    south = lat == 0

    @pl.when(south | (lat == lat_count - 1))
    def _():
        base, band, polar, mid = pole_places(south, row_count)
        rows = [field[t, pl.ds(band, BAND)] for t in range(depth)]
        lane = lanes(rows[0].shape)
        half = cells // 2
        for t in range(0, depth - 1, 2):
            value = jnp.where(lane >= half, rows[t], rolled(rows[t + 1], half))
            to_east[pl.ds(pl.multiple_of(base + t // 2 * BAND, 8), BAND)] = value
        rest = rolled(rows[depth - 1], OFF_LANE - cells)
        for t in range(depth):
            mine = (lane >= 3 * t) & (lane < 3 * t + 3)
            rest = jnp.where(mine, rolled(rows[t], 3 * t + 3 - half), rest)
        kept = (lane % SEG < WEST) | (lane >= OFF_LANE)
        for i, value in enumerate((rest, rolled(rest, WEST))):
            at = pl.ds(pl.multiple_of(mid + i * BAND, 8), BAND)
            to_east[at] = jnp.where(kept, to_east[at], value)
        for t in range(depth):
            pole[t * POLAR : (t + 1) * POLAR] = field[t, pl.ds(polar, POLAR)]
    copies[3].wait()


def pole_places(south, row_count):
    places = (
        jnp.where(south, 0, row_count - POLE),
        jnp.where(south, POLAR, row_count - POLE),
        jnp.where(south, 0, row_count - POLAR),
        jnp.where(south, POLE, 0),
    )
    return [pl.multiple_of(place, 8) for place in places]


def by_place(lat_count, away, south, north):
    lat = lax.axis_index("lat")
    if away is not None:
        pl.when((lat > 0) & (lat < lat_count - 1))(away)
    pl.when(lat == 0)(south)
    pl.when(lat == lat_count - 1)(north)


def pieces(row_count):
    middle = [(POLE, row_count - 2 * POLE)] if row_count > 2 * POLE else []
    return [(0, POLE), *middle, (row_count - POLE, POLE)]


def mid_pieces(row_count):
    return pieces(row_count), pieces(row_count)[1:], pieces(row_count)[:-1]


def own_faces(first_row, count, field, offset, part, own_matrix, flux, seam_index, seam_part):
    depth, _, cells = field.shape
    at = pl.ds(first_row, count)
    shape = (count, cells)
    lane = lanes(shape)
    place = lane % SEG
    offsets = offset[at]
    courant = part[at]
    index = (lane - offsets - 1) & (cells - 1)
    own = field[:, at].reshape(depth * count, cells)
    tables = times(own, own_matrix[...])
    for t in range(depth):
        sums, right, left = split(tables[t * count : (t + 1) * count], cells)
        value = field[t, at]
        flux[t, at] = (
            sums
            - value
            - pick(sums, index)
            + parabola(
                courant, pick(right, index), pick(left, index), pick(value, index)
            )
        )
    first = (place - WEST) & (cells - 1)
    final = jnp.full(shape, cells - 1, i32)
    seam_index[0, at] = (lane - pick(offsets, first) - 1) & (cells - 1)
    seam_index[1, at] = (lane - pick(offsets, final) - 1) & (cells - 1)
    seam_part[0, at] = pick(courant, first)
    seam_part[1, at] = pick(courant, final)


def own_kernel(
    lat_count, field, offset, part, flux, seam_index, seam_part, block_matrix, seam_matrix, own_matrix
):
    _, row_count, cells = field.shape
    shape = (cells, cells)
    source = lax.broadcasted_iota(i32, shape, 0)
    target = lax.broadcasted_iota(i32, shape, 1)
    gap = source - target
    upto = jnp.where(gap <= 0, 1.0, 0.0)
    right, left = edge_weights(gap)
    own = jnp.concatenate([upto, right, left, upto - 1.0], axis=1).astype(bf16)
    zeros = jnp.zeros(shape, f32)
    beyond = gap + jnp.where(source < cells // 2, cells, -cells)
    beside = jnp.concatenate([zeros, *edge_weights(beyond), zeros], axis=1).astype(bf16)
    together = source // SEG == target // SEG
    seam = jnp.concatenate([jnp.where(together, upto, 0.0), right, left], axis=1).astype(bf16)
    for i in range(2):
        block_matrix[2 * i * cells : (2 * i + 1) * cells] = own
        block_matrix[(2 * i + 1) * cells : (2 * i + 2) * cells] = beside
        own_matrix[i * cells : (i + 1) * cells] = own[:, : 3 * cells]
        seam_matrix[i * cells : (i + 1) * cells] = seam

    def step(parts):
        for first, count in parts:
            own_faces(first, count, field, offset, part, own_matrix, flux, seam_index, seam_part)

    by_place(lat_count, *(functools.partial(step, parts) for parts in mid_pieces(row_count)))


def rows_after(field, flux, packed, seam_index, seam_part, from_west, from_east, seam_matrix, parts):
    def take(ref, *lead):
        return jnp.concatenate([ref[(*lead, part)] for part in parts], axis=0)

    mine, west = take(packed), take(from_west)
    east = from_east if isinstance(from_east, jax.Array) else take(from_east)
    count, cells = mine.shape
    shape = mine.shape
    lane = lanes(shape)
    place = lane % SEG
    near = place < WEST
    rows = jnp.concatenate([jnp.where(near, west, mine), jnp.where(near, mine, east)], axis=0)
    next_face = place == WEST
    next_offset = pick(east, jnp.full(shape, OFF_LANE, i32)).astype(i32)
    next_part = pick(east, jnp.full(shape, FRAC_LANE, i32))
    next_index = (lane - next_offset - 1) & (cells - 1)
    index = jnp.concatenate(
        [take(seam_index, 0), jnp.where(next_face, next_index, take(seam_index, 1))], axis=0
    )
    courant = jnp.concatenate(
        [take(seam_part, 0), jnp.where(next_face, next_part, take(seam_part, 1))], axis=0
    )
    sums, right, left = split(times(rows, seam_matrix[...]), cells)
    faces = (
        sums
        - rows
        - pick(sums, index)
        + parabola(
            courant, pick(right, index), pick(left, index), pick(rows, index)
        )
    )
    east_faces = faces[count:]
    both = jnp.where(place == WEST - 1, east_faces, faces[:count])
    outside = (lane < FACES) | (lane == cells - 1)
    results = []
    for t in range(field.shape[0]):
        steps = -(t * SEG + WEST)
        face = jnp.where(outside, rolled(both, steps), take(flux, t))
        following = jnp.where(lane == cells - 1, rolled(east_faces, steps - 1), rolled(face, -1))
        results.append(take(field, t) - (following - face))
    return results


def edge_kernel(
    lat_count, field, flux, packed, seam_index, seam_part, seam_matrix, north, from_east, from_west,
    message_a, message_b, wide, east,
):
    depth, row_count, _ = field.shape
    half = row_count // 2
    even = lax.axis_index("lat") % 2 == 0

    def step(parts, beyond):
        return rows_after(
            field, flux, packed, seam_index, seam_part, from_west, beyond, seam_matrix, parts
        )

    def send(t, top, bottom):
        rows = slice(3 * t, 3 * t + 3)
        message_a[rows] = jnp.where(even, top, bottom)
        message_b[rows] = jnp.where(even, bottom, top)

    def away():
        beyond = jnp.concatenate(
            [from_east[:EDGE], rolled(from_east[half - EDGE :], -PAIR)], axis=0
        )
        after = step((pl.ds(0, EDGE), pl.ds(row_count - EDGE, EDGE)), beyond)
        for t in range(depth):
            send(t, after[t][2 * EDGE - 3 :], after[t][:3])

    def polar_device(parts):
        east[:half] = from_east[...]
        east[half:] = rolled(from_east[...], -PAIR)
        for first, count in parts:
            after = step((pl.ds(first, count),), east)
            for t in range(depth):
                wide[t, first : first + count] = after[t]
        for t in range(depth):
            send(t, wide[t, row_count - 3 :], wide[t, :3])

    by_place(
        lat_count, away, *(functools.partial(polar_device, parts) for parts in mid_pieces(row_count)[1:])
    )
    message_a[3 * depth : 3 * depth + 1] = north[:1]
    message_b[3 * depth : 3 * depth + 1] = north[:1]


def rows_between(near, far, near_field, far_field, first, offset, courant, next_offset, next_courant):
    cells = near_field.shape[1]
    lane = lanes(near_field.shape)
    source = lane - offset - 1
    index = source & (cells - 1)
    close = source >= first

    def both(here, there):
        return jnp.where(close, pick(here, index), pick(there, index))

    face = both(near[0], far[3]) - parabola(
        courant, both(near[1], far[1]), both(near[2], far[2]), both(near_field, far_field)
    )
    last = near[0] - parabola(next_courant, near[1], near[2], near_field)
    last = pick(last, (cells - 1 - next_offset) & (cells - 1))
    return rolled(jnp.where(lane == 0, last, face), -1) - face


def merid_flux(wide, t, courant, first, count):
    cell = [wide[t, first + k : first + k + count] for k in (-3, -2, -1, 0, 1)]
    left = 7.0 * (cell[1] + cell[2]) - (cell[0] + cell[3])
    right = 7.0 * (cell[2] + cell[3]) - (cell[1] + cell[4])
    return parabola(courant, right, left, cell[2])


def middle_kernel(
    lat_count, field, offset, part, north, flux, packed, seam_index, seam_part, seam_matrix, block_matrix,
    from_east, from_far, from_west, given_wide, given_east, wide, east, inner, far, faces,
):
    del given_wide, given_east
    depth, row_count, cells = field.shape
    half = row_count // 2
    far[:half] = from_far[...]
    far[half:] = rolled(from_far[...], -PAIR)

    def away():
        east[:half] = from_east[...]
        east[half:] = rolled(from_east[...], -PAIR)
        for first, count in pieces(row_count):
            after = rows_after(
                field, flux, packed, seam_index, seam_part, from_west, east, seam_matrix, (pl.ds(first, count),)
            )
            for t in range(depth):
                wide[t, first : first + count] = after[t]
        inner_rows(wide, north, faces, inner, EDGE, row_count - 2 * EDGE)

    def polar_device(south):
        band_step(south, field, offset, part, east, from_west, block_matrix, wide)
        first, _ = near_pole(south, row_count)
        inner_rows(
            wide, north, faces, inner, first + POLAR if south else EDGE, row_count - 2 * EDGE - POLAR
        )

    by_place(
        lat_count, away, functools.partial(polar_device, True), functools.partial(polar_device, False)
    )


def near_pole(south, row_count):
    return (EDGE, POLAR) if south else (row_count - EDGE - POLAR, POLAR)


def inner_rows(wide, north, faces, result, first, count):
    for t in range(wide.shape[0]):
        faces[t, :count] = merid_flux(wide, t, north[first : first + count], first, count)
        end = first + count
        faces[t, count : count + 1] = merid_flux(wide, t, north[end : end + 1], end, 1)
        result[t, first - EDGE : end - EDGE] = wide[t, first:end] - (
            faces[t, 1 : 1 + count] - faces[t, :count]
        )


def with_sides(west, own, east):
    beside = jnp.where(lanes(own.shape) < own.shape[1] // 2, east, west)
    return jnp.concatenate([own, beside], axis=1)


def unpacked(ref, rows, lane, depth):
    value = ref[rows]
    return jnp.concatenate([rolled(value, lane - t * SEG) for t in range(depth)], axis=0)


def stacked(ref, rows):
    return ref[:, rows, :].reshape(-1, ref.shape[2])


def row_values(offset, part, east, rows):
    beyond = east[rows]
    return (
        offset[rows],
        part[rows],
        pick(beyond, jnp.full(beyond.shape, OFF_LANE, i32)).astype(i32),
        pick(beyond, jnp.full(beyond.shape, FRAC_LANE, i32)),
    )


def band_step(south, field, offset, part, east, from_west, block_matrix, wide):
    depth, row_count, cells = field.shape
    base, band, _, mid = (int(place) for place in static_places(south, row_count))
    rows = pl.ds(band, BAND)
    own = stacked(field, rows)
    half = cells // 2
    pair = from_west[mid : mid + BAND], from_west[mid + BAND : mid + 2 * BAND]
    lane = lanes(pair[0].shape)
    rest = jnp.where(lane % SEG >= WEST, pair[0], rolled(pair[1], -WEST))
    west = []
    for t in range(depth):
        if t < depth - 1:
            value = from_west[base + t // 2 * BAND : base + (t // 2 + 1) * BAND]
            value = rolled(value, half) if t % 2 else value
        else:
            value = rolled(rest, cells - OFF_LANE)
        inner = jnp.where(lane >= half - 3, rolled(rest, half - 3 - 3 * t), 0.0)
        west.append(jnp.where(lane >= half, value, inner))
    west = jnp.concatenate(west, axis=0)
    beyond = unpacked(east, rows, -WEST, depth)
    tables = jnp.concatenate([with_sides(west, own, beyond), with_sides(west, west, own)], axis=0)
    tables = times(tables, block_matrix[...])
    common = row_values(offset, part, east, rows)
    for t in range(depth):
        at = slice(t * BAND, (t + 1) * BAND)
        both = [split(tables[first : first + BAND], cells) for first in (t * BAND, (depth + t) * BAND)]
        wide[t, rows] = rows_between(*both, own[at], west[at], 0, *common)


def static_places(south, row_count):
    return (0, POLAR, 0, POLE) if south else (row_count - POLE, row_count - POLE, row_count - POLAR, 0)


def edge_rows(lat_count, wide, north, message_b, message_a, low, high, result):
    depth, row_count, cells = wide.shape
    lat = lax.axis_index("lat")
    even = lat % 2 == 0
    south, top = lat == 0, lat == lat_count - 1
    end = 3 * depth
    north_courant = jnp.where(even, message_a[end : end + 1], message_b[end : end + 1])
    north_courant = jnp.where(top, 0.0, north_courant)
    first_row = lax.broadcasted_iota(i32, (EDGE, cells), 0)
    low_courant = jnp.where(south & (first_row == 0), 0.0, north[:EDGE])
    high_next = jnp.concatenate([north[row_count - EDGE + 1 :], north_courant], axis=0)
    for t in range(depth):
        rows = slice(3 * t, 3 * t + 3)
        from_a, from_b = message_a[rows], message_b[rows]
        low[t, EDGE - 3 : EDGE] = jnp.where(south, 0.0, jnp.where(even, from_b, from_a))
        low[t, EDGE : 3 * EDGE] = wide[t, : 2 * EDGE]
        high[t, : 2 * EDGE] = wide[t, row_count - 2 * EDGE :]
        high[t, 2 * EDGE : 2 * EDGE + 3] = jnp.where(top, 0.0, jnp.where(even, from_a, from_b))
    for t in range(depth):
        south_face = merid_flux(low, t, low_courant, EDGE, EDGE)
        north_face = merid_flux(low, t, north[1 : EDGE + 1], EDGE + 1, EDGE)
        result[0, t] = low[t, EDGE : 2 * EDGE] - (north_face - south_face)
        south_face = merid_flux(high, t, north[row_count - EDGE :], EDGE, EDGE)
        north_face = merid_flux(high, t, high_next, EDGE + 1, EDGE)
        result[1, t] = high[t, EDGE : 2 * EDGE] - (north_face - south_face)


def copy_edges(result, out, sems):
    row_count = out.shape[1]
    return [
        pltpu.make_async_copy(result.at[i], out.at[:, pl.ds(first, EDGE)], sems.at[i])
        for i, first in enumerate((0, row_count - EDGE))
    ]


def poles_kernel(
    lat_count, field, offset, part, north, block_matrix, east, far, pole_one, pole_two, message_b, message_a,
    given_wide, given_inner, wide, inner, out, faces, low, high, result, sems,
):
    del given_wide, given_inner

    def polar_device(south):
        depth, row_count, cells = field.shape
        near, beside = near_pole(south, row_count)
        done = near + POLAR if south else EDGE
        count = row_count - 2 * EDGE - POLAR
        copies = [
            pltpu.make_async_copy(
                inner.at[:, pl.ds(first - EDGE, size)], out.at[:, pl.ds(first, size)], sems.at[2 + i]
            )
            for i, (first, size) in enumerate(((done, count), (near, beside)))
        ]
        copies[0].start()
        first = static_places(south, row_count)[2]
        rows = pl.ds(first, POLAR)
        own, west, west_two = stacked(field, rows), pole_one[...], pole_two[...]
        beyond = unpacked(far, rows, cells - WEST, depth)
        tables = jnp.concatenate(
            [with_sides(west_two, west, own), with_sides(beyond, west_two, west)], axis=0
        )
        tables = times(tables, block_matrix[...])
        common = row_values(offset, part, east, rows)
        for t in range(depth):
            at = slice(t * POLAR, (t + 1) * POLAR)
            both = [split(tables[start : start + POLAR], cells) for start in (t * POLAR, (depth + t) * POLAR)]
            wide[t, rows] = rows_between(*both, west[at], west_two[at], -cells, *common)
        inner_rows(wide, north, faces, inner, near, beside)
        copies[1].start()
        edge_rows(lat_count, wide, north, message_b, message_a, low, high, result)
        copies += copy_edges(result, out, sems)
        for copy in copies[2:]:
            copy.start()
        for copy in copies:
            copy.wait()

    by_place(
        lat_count, None, functools.partial(polar_device, True), functools.partial(polar_device, False)
    )


def last_kernel(
    lat_count, wide, inner, north, message_b, message_a, given_out, out, low, high, result, sems
):
    del given_out

    def away():
        count = inner.shape[1]
        inner_copy = pltpu.make_async_copy(inner, out.at[:, pl.ds(EDGE, count)], sems.at[2])
        inner_copy.start()
        edge_rows(lat_count, wide, north, message_b, message_a, low, high, result)
        copies = copy_edges(result, out, sems)
        for copy in copies:
            copy.start()
        for copy in (inner_copy, *copies):
            copy.wait()

    lat = lax.axis_index("lat")
    pl.when((lat > 0) & (lat < lat_count - 1))(away)


def cost(microseconds):
    return pl.CostEstimate(
        flops=int(microseconds * 1e8), bytes_accessed=int(microseconds * 3e6), transcendentals=0
    )


def in_vmem(*values):
    return [pltpu.with_memory_space_constraint(value, VMEM) for value in values]


def whole(count):
    return [pl.BlockSpec(memory_space=VMEM)] * count


def anywhere(count):
    return [pl.BlockSpec(memory_space=pl.ANY)] * count


def on_device(lat_count, lon_count, tracers, offsets, fraction, courant_north):
    tracer_count, level_count, row_count, cells = tracers.shape
    depth = tracer_count * level_count
    shape = (row_count, cells)
    stack = (depth, row_count, cells)
    dma = pltpu.SemaphoreType.DMA

    partner = {l: l ^ 1 for l in range(2, lat_count - 2)}
    if lat_count % 2 == 0 and lat_count >= 8:
        for l, other in ((1, 3), (2, lat_count - 2)):
            partner[l], partner[other] = other, l

    def along_lon(value, steps, everywhere=True):
        pairs = []
        for l in range(lat_count):
            for o in range(lon_count):
                if everywhere or len(partner) < lat_count - 2 or l in (0, lat_count - 1):
                    target = (l, (o + steps) % lon_count)
                else:
                    target = (partner[l], o)
                pairs.append((l * lon_count + o, target[0] * lon_count + target[1]))
        return lax.ppermute(value, ("lat", "lon"), pairs)

    def along_lat(value, first):
        pairs = []
        last_lat, last_lon = lat_count - 1, lon_count - 1
        for l in range(lat_count):
            other = l + 1 if (l - first) % 2 == 0 else l - 1
            for o in range(lon_count):
                if 0 <= other < lat_count:
                    target = (other, o)
                elif lat_count % 2:
                    target = (l, (o + 1) % lon_count)
                elif l == 0:
                    target = (0, o - 1) if o else (last_lat, 0)
                else:
                    target = (last_lat, o + 1) if o < last_lon else (0, last_lon)
                pairs.append((l * lon_count + o, target[0] * lon_count + target[1]))
        return lax.ppermute(value, ("lat", "lon"), pairs)

    field, offset, part, north, packed, to_east, to_west, pole = in_vmem(
        *pl.pallas_call(
            functools.partial(pack_kernel, lat_count),
            out_shape=[
                VMEM(stack, f32),
                VMEM(shape, i32),
                VMEM(shape, f32),
                VMEM(shape, f32),
                VMEM(shape, f32),
                VMEM(shape, f32),
                VMEM((row_count // 2, cells), f32),
                VMEM((depth * POLAR, cells), f32),
            ],
            in_specs=anywhere(4),
            out_specs=whole(8),
            scratch_shapes=[dma((4,))],
            cost_estimate=cost(1.0),
            name="pack",
        )(tracers.reshape(stack), offsets, fraction, courant_north)
    )
    from_west = along_lon(to_east, 1)
    from_east = along_lon(to_west, -1)
    from_far = from_east if lon_count == 4 else along_lon(to_west, 3)
    pole_one = along_lon(pole, 1, False)
    pole_two = along_lon(pole, 2, False)

    flux, seam_index, seam_part, block_matrix, seam_matrix = in_vmem(
        *pl.pallas_call(
            functools.partial(own_kernel, lat_count),
            out_shape=[
                VMEM(stack, f32),
                VMEM((2, *shape), i32),
                VMEM((2, *shape), f32),
                VMEM((4 * cells, 4 * cells), bf16),
                VMEM((2 * cells, 3 * cells), bf16),
            ],
            in_specs=whole(3),
            out_specs=whole(5),
            scratch_shapes=[VMEM((2 * cells, 3 * cells), bf16)],
            cost_estimate=cost(2.0),
            name="own",
        )(field, offset, part)
    )
    from_west, from_east, from_far, pole_one, pole_two = in_vmem(
        from_west, from_east, from_far, pole_one, pole_two
    )

    message = (3 * depth + 1, cells)
    longer = 24
    message_a, message_b, wide, east = in_vmem(
        *pl.pallas_call(
            functools.partial(edge_kernel, lat_count),
            out_shape=[VMEM(message, f32), VMEM((longer, cells), f32), VMEM(stack, f32), VMEM(shape, f32)],
            in_specs=whole(9),
            out_specs=whole(4),
            cost_estimate=cost(4.0),
            name="edge",
        )(field, flux, packed, seam_index, seam_part, seam_matrix, north, from_east, from_west)
    )
    message_a = along_lat(message_a, 0)
    message_b = along_lat(message_b, 1)

    inner = VMEM((depth, row_count - 2 * EDGE, cells), f32)
    faces = VMEM((depth, row_count - EDGE, cells), f32)
    wide, east, inner_part, far = in_vmem(
        *pl.pallas_call(
            functools.partial(middle_kernel, lat_count),
            out_shape=[VMEM(stack, f32), VMEM(shape, f32), inner, VMEM(shape, f32)],
            in_specs=whole(15),
            out_specs=whole(4),
            scratch_shapes=[faces],
            input_output_aliases={13: 0, 14: 1},
            cost_estimate=cost(0.0),
            name="middle",
        )(
            field, offset, part, north, flux, packed, seam_index, seam_part, seam_matrix, block_matrix,
            from_east, from_far, from_west, wide, east,
        )
    )

    message_a, message_b = in_vmem(message_a, message_b)
    scratch = [
        VMEM((depth, 3 * EDGE, cells), f32),
        VMEM((depth, 3 * EDGE, cells), f32),
        VMEM((2, depth, EDGE, cells), f32),
        dma((4,)),
    ]
    polar_b = message_b if lat_count % 2 else message_a
    wide, inner, out = pl.pallas_call(
        functools.partial(poles_kernel, lat_count),
        out_shape=[VMEM(stack, f32), inner, jax.ShapeDtypeStruct(stack, f32)],
        in_specs=whole(13),
        out_specs=whole(2) + anywhere(1),
        scratch_shapes=[faces, *scratch],
        input_output_aliases={11: 0, 12: 1},
        cost_estimate=cost(0.0),
        name="poles",
    )(
        field, offset, part, north, block_matrix, east, far, pole_one, pole_two, polar_b, message_a,
        wide, inner_part,
    )

    out = pl.pallas_call(
        functools.partial(last_kernel, lat_count),
        out_shape=jax.ShapeDtypeStruct(stack, f32),
        in_specs=whole(5) + anywhere(1),
        out_specs=pl.BlockSpec(memory_space=pl.ANY),
        scratch_shapes=scratch,
        input_output_aliases={5: 0},
        cost_estimate=cost(0.7),
        name="last",
    )(*in_vmem(wide, inner), north, message_b, message_a, out)
    return out.reshape(tracers.shape)


def solution(mesh):
    placed = (P(None, None, "lat", "lon"), P("lat", "lon"), P("lat", "lon"), P("lat", "lon"))
    return jax.shard_map(
        functools.partial(on_device, mesh.shape["lat"], mesh.shape["lon"]),
        mesh=mesh,
        in_specs=placed,
        out_specs=P(None, None, "lat", "lon"),
        check_vma=False,
    )
```

```python
import functools

import jax
import jax.numpy as jnp
from jax import lax
from jax.experimental import pallas as pl
from jax.experimental.pallas import tpu as pltpu
from jax.sharding import PartitionSpec as P

POLAR = 24
BAND = 24
POLE = POLAR + BAND
WEST = 12
SEG = 24
FACES = 11
OFF_LANE = 120
FRAC_LANE = 121
PAIR = 4
WITH_WEST = 2
EDGE = 8

f32 = jnp.float32
bf16 = jnp.bfloat16
i32 = jnp.int32
VMEM = pltpu.VMEM


def lanes(shape):
    return lax.broadcasted_iota(i32, shape, 1)


def rolled(value, steps):
    steps = steps % value.shape[1]
    return pltpu.roll(value, steps, 1) if steps else value


def pick(table, index):
    return jnp.take_along_axis(table, index, axis=1, mode="promise_in_bounds")


def parabola(c, right, left, centre):
    jump = right - left
    curve = 72.0 * centre - 3.0 * (left + right)
    return c * (1 / 12) * (right - 0.5 * c * (jump - (1.0 - (2.0 / 3.0) * c) * curve))


def times(value, matrix):
    high = value.astype(bf16)
    low = (value - high.astype(f32)).astype(bf16)
    return jnp.dot(jnp.concatenate([high, low], axis=1), matrix, preferred_element_type=f32)


def for_west(packed):
    half, cells = packed.shape[0] // 2, packed.shape[1]
    lane = lanes((half, cells))
    place = lane % SEG
    first = (lane >= OFF_LANE) & (lane < OFF_LANE + 2)
    first = first | ((lane < OFF_LANE) & (place >= WEST - 2) & (place < WEST + 2))
    return jnp.where(first, packed[:half], rolled(packed[half:], PAIR))


def edge_weights(gap):
    def weight(gap):
        inner = (gap == 0) | (gap == 1)
        outer = (gap == -1) | (gap == 2)
        return jnp.where(inner, 7.0, jnp.where(outer, -1.0, 0.0))

    return weight(gap), weight(gap + 1)


def split(table, cells):
    return [table[:, i : i + cells] for i in range(0, table.shape[1], cells)]


def pack_kernel(
    lat_count, tracers, offsets, fraction, courant,
    field, offset, part, north, packed, to_east, to_west, pole, pole_rest, flux, seam_index, seam_part, block_matrix,
    seam_matrix, own_matrix, sems,
):
    depth, row_count, cells = field.shape
    copies = [
        pltpu.make_async_copy(source, target, sems.at[i])
        for i, (source, target) in enumerate(
            ((tracers, field), (offsets, offset), (fraction, part), (courant, north))
        )
    ]
    for copy in copies:
        copy.start()
    for copy in copies[:3]:
        copy.wait()
    shape = (row_count, cells)
    lane = lanes(shape)
    message = jnp.where(
        lane == OFF_LANE,
        rolled(offset[...].astype(f32), OFF_LANE),
        jnp.where(lane == FRAC_LANE, rolled(part[...], FRAC_LANE), 0.0),
    )
    for t in range(depth):
        mine = (lane >= t * SEG) & (lane < (t + 1) * SEG)
        message = jnp.where(mine, rolled(field[t], t * SEG + WEST), message)
    packed[...] = message
    to_east[:row_count] = message
    to_west[...] = for_west(message)
    lat = lax.axis_index("lat")
    south = lat == 0

    @pl.when(south | (lat == lat_count - 1))
    def _():
        base, band, polar, mid = pole_places(south, row_count)
        rows = [field[t, pl.ds(band, BAND)] for t in range(depth)]
        lane = lanes(rows[0].shape)
        half = cells // 2
        for t in range(0, depth - 1, 2):
            value = jnp.where(lane >= half, rows[t], rolled(rows[t + 1], half))
            to_east[pl.ds(pl.multiple_of(base + t // 2 * BAND, 8), BAND)] = value
        rest = rolled(rows[depth - 1], OFF_LANE - cells)
        for t in range(depth):
            mine = (lane >= 3 * t) & (lane < 3 * t + 3)
            rest = jnp.where(mine, rolled(rows[t], 3 * t + 3 - half), rest)
        kept = (lane % SEG < WEST) | (lane >= OFF_LANE)
        for i, value in enumerate((rest, rolled(rest, WEST))):
            at = pl.ds(pl.multiple_of(mid + i * BAND, 8), BAND)
            to_east[at] = jnp.where(kept, to_east[at], value)
        for t in range(depth):
            value = field[t, pl.ds(polar, POLAR)]
            pole[t * POLAR : (t + 1) * POLAR] = value
            if t < WITH_WEST:
                to_east[row_count + t * POLAR : row_count + (t + 1) * POLAR] = value
            else:
                pole_rest[(t - WITH_WEST) * POLAR : (t - WITH_WEST + 1) * POLAR] = value
    pl.when(goes_early())(
        lambda: own_work(
            lat_count, field, offset, part, flux, seam_index, seam_part, block_matrix, seam_matrix, own_matrix
        )
    )
    copies[3].wait()


def pole_places(south, row_count):
    places = (
        jnp.where(south, 0, row_count - POLE),
        jnp.where(south, POLAR, row_count - POLE),
        jnp.where(south, 0, row_count - POLAR),
        jnp.where(south, POLE, 0),
    )
    return [pl.multiple_of(place, 8) for place in places]


def by_place(lat_count, away, south, north):
    lat = lax.axis_index("lat")
    if away is not None:
        pl.when((lat > 0) & (lat < lat_count - 1))(away)
    pl.when(lat == 0)(south)
    pl.when(lat == lat_count - 1)(north)


def pieces(row_count):
    middle = [(POLE, row_count - 2 * POLE)] if row_count > 2 * POLE else []
    return [(0, POLE), *middle, (row_count - POLE, POLE)]


def mid_pieces(row_count):
    return pieces(row_count), pieces(row_count)[1:], pieces(row_count)[:-1]


def own_faces(first_row, count, field, offset, part, own_matrix, flux, seam_index, seam_part):
    depth, _, cells = field.shape
    at = pl.ds(first_row, count)
    shape = (count, cells)
    lane = lanes(shape)
    place = lane % SEG
    offsets = offset[at]
    courant = part[at]
    index = (lane - offsets - 1) & (cells - 1)
    own = field[:, at].reshape(depth * count, cells)
    tables = times(own, own_matrix[...])
    for t in range(depth):
        sums, right, left = split(tables[t * count : (t + 1) * count], cells)
        value = field[t, at]
        flux[t, at] = (
            sums
            - value
            - pick(sums, index)
            + parabola(
                courant, pick(right, index), pick(left, index), pick(value, index)
            )
        )
    first = (place - WEST) & (cells - 1)
    final = jnp.full(shape, cells - 1, i32)
    seam_index[0, at] = (lane - pick(offsets, first) - 1) & (cells - 1)
    seam_index[1, at] = (lane - pick(offsets, final) - 1) & (cells - 1)
    seam_part[0, at] = pick(courant, first)
    seam_part[1, at] = pick(courant, final)


def goes_early():
    lat, lon = lax.axis_index("lat"), lax.axis_index("lon")
    return (lon == 0) & (lat < 2)


def own_kernel(
    lat_count, field, offset, part, flux_given, index_given, part_given, block_given, seam_given,
    flux, seam_index, seam_part, block_matrix, seam_matrix, own_matrix,
):
    del flux_given, index_given, part_given, block_given, seam_given
    pl.when(~goes_early())(
        lambda: own_work(
            lat_count, field, offset, part, flux, seam_index, seam_part, block_matrix, seam_matrix, own_matrix
        )
    )


def own_work(
    lat_count, field, offset, part, flux, seam_index, seam_part, block_matrix, seam_matrix, own_matrix
):
    _, row_count, cells = field.shape
    shape = (cells, cells)
    source = lax.broadcasted_iota(i32, shape, 0)
    target = lax.broadcasted_iota(i32, shape, 1)
    gap = source - target
    upto = jnp.where(gap <= 0, 1.0, 0.0)
    right, left = edge_weights(gap)
    own = jnp.concatenate([upto, right, left, upto - 1.0], axis=1).astype(bf16)
    zeros = jnp.zeros(shape, f32)
    beyond = gap + jnp.where(source < cells // 2, cells, -cells)
    beside = jnp.concatenate([zeros, *edge_weights(beyond), zeros], axis=1).astype(bf16)
    together = source // SEG == target // SEG
    seam = jnp.concatenate([jnp.where(together, upto, 0.0), right, left], axis=1).astype(bf16)
    for i in range(2):
        block_matrix[2 * i * cells : (2 * i + 1) * cells] = own
        block_matrix[(2 * i + 1) * cells : (2 * i + 2) * cells] = beside
        own_matrix[i * cells : (i + 1) * cells] = own[:, : 3 * cells]
        seam_matrix[i * cells : (i + 1) * cells] = seam

    def step(parts):
        for first, count in parts:
            own_faces(first, count, field, offset, part, own_matrix, flux, seam_index, seam_part)

    by_place(lat_count, *(functools.partial(step, parts) for parts in mid_pieces(row_count)))


def rows_after(field, flux, packed, seam_index, seam_part, from_west, from_east, seam_matrix, parts):
    def take(ref, *lead):
        return jnp.concatenate([ref[(*lead, part)] for part in parts], axis=0)

    mine, west = take(packed), take(from_west)
    east = from_east if isinstance(from_east, jax.Array) else take(from_east)
    count, cells = mine.shape
    shape = mine.shape
    lane = lanes(shape)
    place = lane % SEG
    near = place < WEST
    rows = jnp.concatenate([jnp.where(near, west, mine), jnp.where(near, mine, east)], axis=0)
    next_face = place == WEST
    next_offset = pick(east, jnp.full(shape, OFF_LANE, i32)).astype(i32)
    next_part = pick(east, jnp.full(shape, FRAC_LANE, i32))
    next_index = (lane - next_offset - 1) & (cells - 1)
    index = jnp.concatenate(
        [take(seam_index, 0), jnp.where(next_face, next_index, take(seam_index, 1))], axis=0
    )
    courant = jnp.concatenate(
        [take(seam_part, 0), jnp.where(next_face, next_part, take(seam_part, 1))], axis=0
    )
    sums, right, left = split(times(rows, seam_matrix[...]), cells)
    faces = (
        sums
        - rows
        - pick(sums, index)
        + parabola(
            courant, pick(right, index), pick(left, index), pick(rows, index)
        )
    )
    east_faces = faces[count:]
    both = jnp.where(place == WEST - 1, east_faces, faces[:count])
    outside = (lane < FACES) | (lane == cells - 1)
    results = []
    for t in range(field.shape[0]):
        steps = -(t * SEG + WEST)
        face = jnp.where(outside, rolled(both, steps), take(flux, t))
        following = jnp.where(lane == cells - 1, rolled(east_faces, steps - 1), rolled(face, -1))
        results.append(take(field, t) - (following - face))
    return results


def edge_kernel(
    lat_count, field, flux, packed, seam_index, seam_part, seam_matrix, north, from_east, from_west,
    message_a, message_b, wide, east,
):
    depth, row_count, _ = field.shape
    half = row_count // 2
    even = lax.axis_index("lat") % 2 == 0

    def step(parts, beyond):
        return rows_after(
            field, flux, packed, seam_index, seam_part, from_west, beyond, seam_matrix, parts
        )

    def send(t, top, bottom):
        rows = slice(3 * t, 3 * t + 3)
        message_a[rows] = jnp.where(even, top, bottom)
        message_b[rows] = jnp.where(even, bottom, top)

    def away():
        beyond = jnp.concatenate(
            [from_east[:EDGE], rolled(from_east[half - EDGE :], -PAIR)], axis=0
        )
        after = step((pl.ds(0, EDGE), pl.ds(row_count - EDGE, EDGE)), beyond)
        for t in range(depth):
            send(t, after[t][2 * EDGE - 3 :], after[t][:3])

    def polar_device(parts):
        east[:half] = from_east[...]
        east[half:] = rolled(from_east[...], -PAIR)
        for first, count in parts:
            after = step((pl.ds(first, count),), east)
            for t in range(depth):
                wide[t, first : first + count] = after[t]
        for t in range(depth):
            send(t, wide[t, row_count - 3 :], wide[t, :3])

    by_place(
        lat_count, away, *(functools.partial(polar_device, parts) for parts in mid_pieces(row_count)[1:])
    )
    message_a[3 * depth : 3 * depth + 1] = north[:1]
    message_b[3 * depth : 3 * depth + 1] = north[:1]


def rows_between(near, far, near_field, far_field, first, offset, courant, next_offset, next_courant):
    cells = near_field.shape[1]
    lane = lanes(near_field.shape)
    source = lane - offset - 1
    index = source & (cells - 1)
    close = source >= first

    def both(here, there):
        return jnp.where(close, pick(here, index), pick(there, index))

    face = both(near[0], far[3]) - parabola(
        courant, both(near[1], far[1]), both(near[2], far[2]), both(near_field, far_field)
    )
    last = near[0] - parabola(next_courant, near[1], near[2], near_field)
    last = pick(last, (cells - 1 - next_offset) & (cells - 1))
    return rolled(jnp.where(lane == 0, last, face), -1) - face


def merid_flux(wide, t, courant, first, count):
    cell = [wide[t, first + k : first + k + count] for k in (-3, -2, -1, 0, 1)]
    left = 7.0 * (cell[1] + cell[2]) - (cell[0] + cell[3])
    right = 7.0 * (cell[2] + cell[3]) - (cell[1] + cell[4])
    return parabola(courant, right, left, cell[2])


def middle_kernel(
    lat_count, field, offset, part, north, flux, packed, seam_index, seam_part, seam_matrix, block_matrix,
    from_east, from_far, from_west, given_wide, given_east, wide, east, inner, far, faces,
):
    del given_wide, given_east
    depth, row_count, cells = field.shape
    half = row_count // 2
    far[:half] = from_far[...]
    far[half:] = rolled(from_far[...], -PAIR)

    def away():
        east[:half] = from_east[...]
        east[half:] = rolled(from_east[...], -PAIR)
        for first, count in pieces(row_count):
            after = rows_after(
                field, flux, packed, seam_index, seam_part, from_west, east, seam_matrix, (pl.ds(first, count),)
            )
            for t in range(depth):
                wide[t, first : first + count] = after[t]
        inner_rows(wide, north, faces, inner, EDGE, row_count - 2 * EDGE)

    def polar_device(south):
        band_step(south, field, offset, part, east, from_west, block_matrix, wide)
        first, _ = near_pole(south, row_count)
        inner_rows(
            wide, north, faces, inner, first + POLAR if south else EDGE, row_count - 2 * EDGE - POLAR
        )

    by_place(
        lat_count, away, functools.partial(polar_device, True), functools.partial(polar_device, False)
    )


def near_pole(south, row_count):
    return (EDGE, POLAR) if south else (row_count - EDGE - POLAR, POLAR)


def inner_rows(wide, north, faces, result, first, count):
    for t in range(wide.shape[0]):
        faces[t, :count] = merid_flux(wide, t, north[first : first + count], first, count)
        end = first + count
        faces[t, count : count + 1] = merid_flux(wide, t, north[end : end + 1], end, 1)
        result[t, first - EDGE : end - EDGE] = wide[t, first:end] - (
            faces[t, 1 : 1 + count] - faces[t, :count]
        )


def with_sides(west, own, east):
    beside = jnp.where(lanes(own.shape) < own.shape[1] // 2, east, west)
    return jnp.concatenate([own, beside], axis=1)


def unpacked(ref, rows, lane, depth):
    value = ref[rows]
    return jnp.concatenate([rolled(value, lane - t * SEG) for t in range(depth)], axis=0)


def stacked(ref, rows):
    return ref[:, rows, :].reshape(-1, ref.shape[2])


def row_values(offset, part, east, rows):
    beyond = east[rows]
    return (
        offset[rows],
        part[rows],
        pick(beyond, jnp.full(beyond.shape, OFF_LANE, i32)).astype(i32),
        pick(beyond, jnp.full(beyond.shape, FRAC_LANE, i32)),
    )


def band_step(south, field, offset, part, east, from_west, block_matrix, wide):
    depth, row_count, cells = field.shape
    base, band, _, mid = (int(place) for place in static_places(south, row_count))
    rows = pl.ds(band, BAND)
    own = stacked(field, rows)
    half = cells // 2
    pair = from_west[mid : mid + BAND], from_west[mid + BAND : mid + 2 * BAND]
    lane = lanes(pair[0].shape)
    rest = jnp.where(lane % SEG >= WEST, pair[0], rolled(pair[1], -WEST))
    west = []
    for t in range(depth):
        if t < depth - 1:
            value = from_west[base + t // 2 * BAND : base + (t // 2 + 1) * BAND]
            value = rolled(value, half) if t % 2 else value
        else:
            value = rolled(rest, cells - OFF_LANE)
        inner = jnp.where(lane >= half - 3, rolled(rest, half - 3 - 3 * t), 0.0)
        west.append(jnp.where(lane >= half, value, inner))
    west = jnp.concatenate(west, axis=0)
    beyond = unpacked(east, rows, -WEST, depth)
    tables = jnp.concatenate([with_sides(west, own, beyond), with_sides(west, west, own)], axis=0)
    tables = times(tables, block_matrix[...])
    common = row_values(offset, part, east, rows)
    for t in range(depth):
        at = slice(t * BAND, (t + 1) * BAND)
        both = [split(tables[first : first + BAND], cells) for first in (t * BAND, (depth + t) * BAND)]
        wide[t, rows] = rows_between(*both, own[at], west[at], 0, *common)


def static_places(south, row_count):
    return (0, POLAR, 0, POLE) if south else (row_count - POLE, row_count - POLE, row_count - POLAR, 0)


def edge_rows(lat_count, wide, north, message_b, message_a, low, high, result):
    depth, row_count, cells = wide.shape
    lat = lax.axis_index("lat")
    even = lat % 2 == 0
    south, top = lat == 0, lat == lat_count - 1
    end = 3 * depth
    north_courant = jnp.where(even, message_a[end : end + 1], message_b[end : end + 1])
    north_courant = jnp.where(top, 0.0, north_courant)
    first_row = lax.broadcasted_iota(i32, (EDGE, cells), 0)
    low_courant = jnp.where(south & (first_row == 0), 0.0, north[:EDGE])
    high_next = jnp.concatenate([north[row_count - EDGE + 1 :], north_courant], axis=0)
    for t in range(depth):
        rows = slice(3 * t, 3 * t + 3)
        from_a, from_b = message_a[rows], message_b[rows]
        low[t, EDGE - 3 : EDGE] = jnp.where(south, 0.0, jnp.where(even, from_b, from_a))
        low[t, EDGE : 3 * EDGE] = wide[t, : 2 * EDGE]
        high[t, : 2 * EDGE] = wide[t, row_count - 2 * EDGE :]
        high[t, 2 * EDGE : 2 * EDGE + 3] = jnp.where(top, 0.0, jnp.where(even, from_a, from_b))
    for t in range(depth):
        south_face = merid_flux(low, t, low_courant, EDGE, EDGE)
        north_face = merid_flux(low, t, north[1 : EDGE + 1], EDGE + 1, EDGE)
        result[0, t] = low[t, EDGE : 2 * EDGE] - (north_face - south_face)
        south_face = merid_flux(high, t, north[row_count - EDGE :], EDGE, EDGE)
        north_face = merid_flux(high, t, high_next, EDGE + 1, EDGE)
        result[1, t] = high[t, EDGE : 2 * EDGE] - (north_face - south_face)


def copy_edges(result, out, sems):
    row_count = out.shape[1]
    return [
        pltpu.make_async_copy(result.at[i], out.at[:, pl.ds(first, EDGE)], sems.at[i])
        for i, first in enumerate((0, row_count - EDGE))
    ]


def join_kernel(from_west, rest, after, joined):
    del after
    count = joined.shape[0] - rest.shape[0]
    joined[:count] = from_west[from_west.shape[0] - count :]
    joined[count:] = rest[...]


def poles_kernel(
    lat_count, field, offset, part, north, block_matrix, east, far, pole_one, pole_two, message_b, message_a,
    given_wide, given_inner, wide, inner, out, faces, low, high, result, sems,
):
    del given_wide, given_inner

    def polar_device(south):
        depth, row_count, cells = field.shape
        near, beside = near_pole(south, row_count)
        done = near + POLAR if south else EDGE
        count = row_count - 2 * EDGE - POLAR
        copies = [
            pltpu.make_async_copy(
                inner.at[:, pl.ds(first - EDGE, size)], out.at[:, pl.ds(first, size)], sems.at[2 + i]
            )
            for i, (first, size) in enumerate(((done, count), (near, beside)))
        ]
        copies[0].start()
        first = static_places(south, row_count)[2]
        rows = pl.ds(first, POLAR)
        own, west, west_two = stacked(field, rows), pole_one[...], pole_two[...]
        beyond = unpacked(far, rows, cells - WEST, depth)
        tables = jnp.concatenate(
            [with_sides(west_two, west, own), with_sides(beyond, west_two, west)], axis=0
        )
        tables = times(tables, block_matrix[...])
        common = row_values(offset, part, east, rows)
        for t in range(depth):
            at = slice(t * POLAR, (t + 1) * POLAR)
            both = [split(tables[start : start + POLAR], cells) for start in (t * POLAR, (depth + t) * POLAR)]
            wide[t, rows] = rows_between(*both, west[at], west_two[at], -cells, *common)
        inner_rows(wide, north, faces, inner, near, beside)
        copies[1].start()
        edge_rows(lat_count, wide, north, message_b, message_a, low, high, result)
        copies += copy_edges(result, out, sems)
        for copy in copies[2:]:
            copy.start()
        for copy in copies:
            copy.wait()

    by_place(
        lat_count, None, functools.partial(polar_device, True), functools.partial(polar_device, False)
    )


def last_kernel(
    lat_count, wide, inner, north, message_b, message_a, given_out, out, low, high, result, sems
):
    del given_out

    def away():
        count = inner.shape[1]
        inner_copy = pltpu.make_async_copy(inner, out.at[:, pl.ds(EDGE, count)], sems.at[2])
        inner_copy.start()
        edge_rows(lat_count, wide, north, message_b, message_a, low, high, result)
        copies = copy_edges(result, out, sems)
        for copy in copies:
            copy.start()
        for copy in (inner_copy, *copies):
            copy.wait()

    lat = lax.axis_index("lat")
    pl.when((lat > 0) & (lat < lat_count - 1))(away)


def cost(microseconds):
    return pl.CostEstimate(
        flops=int(microseconds * 1e8), bytes_accessed=int(microseconds * 3e6), transcendentals=0
    )


def in_vmem(*values):
    return [pltpu.with_memory_space_constraint(value, VMEM) for value in values]


def whole(count):
    return [pl.BlockSpec(memory_space=VMEM)] * count


def anywhere(count):
    return [pl.BlockSpec(memory_space=pl.ANY)] * count


def on_device(lat_count, lon_count, tracers, offsets, fraction, courant_north):
    tracer_count, level_count, row_count, cells = tracers.shape
    depth = tracer_count * level_count
    shape = (row_count, cells)
    stack = (depth, row_count, cells)
    dma = pltpu.SemaphoreType.DMA

    def along_lon(value, steps, everywhere=True):
        pairs = []
        for l in range(lat_count):
            from_pole = min(l, lat_count - 1 - l)
            for o in range(lon_count):
                if everywhere or from_pole == 0 or lat_count % 2 or lon_count % 2:
                    target = (l, (o + steps) % lon_count)
                else:
                    target = (l, o ^ 1) if from_pole == 1 else (l ^ 1, o)
                pairs.append((l * lon_count + o, target[0] * lon_count + target[1]))
        return lax.ppermute(value, ("lat", "lon"), pairs)

    def along_lat(value, first):
        pairs = []
        last_lat, last_lon = lat_count - 1, lon_count - 1
        for l in range(lat_count):
            other = l + 1 if (l - first) % 2 == 0 else l - 1
            for o in range(lon_count):
                if 0 <= other < lat_count:
                    target = (other, o)
                elif lat_count % 2:
                    target = (l, (o + 1) % lon_count)
                elif l == 0:
                    target = (0, o - 1) if o else (last_lat, 0)
                else:
                    target = (last_lat, o + 1) if o < last_lon else (0, last_lon)
                pairs.append((l * lon_count + o, target[0] * lon_count + target[1]))
        return lax.ppermute(value, ("lat", "lon"), pairs)

    own_shapes = [
        VMEM(stack, f32),
        VMEM((2, *shape), i32),
        VMEM((2, *shape), f32),
        VMEM((4 * cells, 4 * cells), bf16),
        VMEM((2 * cells, 3 * cells), bf16),
    ]
    own_matrix = VMEM((2 * cells, 3 * cells), bf16)
    field, offset, part, north, packed, to_east, to_west, pole, pole_rest, *own = in_vmem(
        *pl.pallas_call(
            functools.partial(pack_kernel, lat_count),
            out_shape=[
                VMEM(stack, f32),
                VMEM(shape, i32),
                VMEM(shape, f32),
                VMEM(shape, f32),
                VMEM(shape, f32),
                VMEM((row_count + WITH_WEST * POLAR, cells), f32),
                VMEM((row_count // 2, cells), f32),
                VMEM((depth * POLAR, cells), f32),
                VMEM(((depth - WITH_WEST) * POLAR, cells), f32),
                *own_shapes,
            ],
            in_specs=anywhere(4),
            out_specs=whole(14),
            scratch_shapes=[own_matrix, dma((4,))],
            cost_estimate=cost(1.0),
            name="pack",
        )(tracers.reshape(stack), offsets, fraction, courant_north)
    )
    from_west = along_lon(to_east, 1)
    from_east = along_lon(to_west, -1)
    from_far = from_east if lon_count == 4 else along_lon(to_west, 3)
    pole_one = along_lon(pole_rest, 1, False)
    pole_two = along_lon(pole, 2, False)

    flux, seam_index, seam_part, block_matrix, seam_matrix = in_vmem(
        *pl.pallas_call(
            functools.partial(own_kernel, lat_count),
            out_shape=own_shapes,
            in_specs=whole(8),
            out_specs=whole(5),
            scratch_shapes=[own_matrix],
            input_output_aliases={3 + i: i for i in range(5)},
            cost_estimate=cost(2.0),
            name="own",
        )(field, offset, part, *own)
    )
    from_west, from_east, from_far, pole_one, pole_two = in_vmem(
        from_west, from_east, from_far, pole_one, pole_two
    )

    message = (3 * depth + 1, cells)
    longer = 24
    message_a, message_b, wide, east = in_vmem(
        *pl.pallas_call(
            functools.partial(edge_kernel, lat_count),
            out_shape=[VMEM(message, f32), VMEM((longer, cells), f32), VMEM(stack, f32), VMEM(shape, f32)],
            in_specs=whole(9),
            out_specs=whole(4),
            cost_estimate=cost(4.0),
            name="edge",
        )(field, flux, packed, seam_index, seam_part, seam_matrix, north, from_east, from_west)
    )
    message_a = along_lat(message_a, 0)
    message_b = along_lat(message_b, 1)

    inner = VMEM((depth, row_count - 2 * EDGE, cells), f32)
    faces = VMEM((depth, row_count - EDGE, cells), f32)
    wide, east, inner_part, far = in_vmem(
        *pl.pallas_call(
            functools.partial(middle_kernel, lat_count),
            out_shape=[VMEM(stack, f32), VMEM(shape, f32), inner, VMEM(shape, f32)],
            in_specs=whole(15),
            out_specs=whole(4),
            scratch_shapes=[faces],
            input_output_aliases={13: 0, 14: 1},
            cost_estimate=cost(0.0),
            name="middle",
        )(
            field, offset, part, north, flux, packed, seam_index, seam_part, seam_matrix, block_matrix,
            from_east, from_far, from_west, wide, east,
        )
    )

    pole_one = pl.pallas_call(
        join_kernel,
        out_shape=VMEM((depth * POLAR, cells), f32),
        in_specs=whole(3),
        out_specs=pl.BlockSpec(memory_space=VMEM),
        cost_estimate=cost(0.3),
        name="join",
    )(from_west, pole_one, far)
    pole_one, message_a, message_b = in_vmem(pole_one, message_a, message_b)
    scratch = [
        VMEM((depth, 3 * EDGE, cells), f32),
        VMEM((depth, 3 * EDGE, cells), f32),
        VMEM((2, depth, EDGE, cells), f32),
        dma((4,)),
    ]
    polar_b = message_b if lat_count % 2 else message_a
    wide, inner, out = pl.pallas_call(
        functools.partial(poles_kernel, lat_count),
        out_shape=[VMEM(stack, f32), inner, jax.ShapeDtypeStruct(stack, f32)],
        in_specs=whole(13),
        out_specs=whole(2) + anywhere(1),
        scratch_shapes=[faces, *scratch],
        input_output_aliases={11: 0, 12: 1},
        cost_estimate=cost(0.0),
        name="poles",
    )(
        field, offset, part, north, block_matrix, east, far, pole_one, pole_two, polar_b, message_a,
        wide, inner_part,
    )

    out = pl.pallas_call(
        functools.partial(last_kernel, lat_count),
        out_shape=jax.ShapeDtypeStruct(stack, f32),
        in_specs=whole(5) + anywhere(1),
        out_specs=pl.BlockSpec(memory_space=pl.ANY),
        scratch_shapes=scratch,
        input_output_aliases={5: 0},
        cost_estimate=cost(0.7),
        name="last",
    )(*in_vmem(wide, inner), north, message_b, message_a, out)
    return out.reshape(tracers.shape)


def solution(mesh):
    placed = (P(None, None, "lat", "lon"), P("lat", "lon"), P("lat", "lon"), P("lat", "lon"))
    return jax.shard_map(
        functools.partial(on_device, mesh.shape["lat"], mesh.shape["lon"]),
        mesh=mesh,
        in_specs=placed,
        out_specs=P(None, None, "lat", "lon"),
        check_vma=False,
    )
```

```python
import functools

import jax
import jax.numpy as jnp
from jax import lax
from jax.experimental import pallas as pl
from jax.experimental.pallas import tpu as pltpu
from jax.sharding import PartitionSpec as P

POLAR = 24
BAND = 24
POLE = POLAR + BAND
WEST = 12
SEG = 24
FACES = 11
OFF_LANE = 120
FRAC_LANE = 121
PAIR = 4
WITH_WEST = 2
EDGE = 8

f32 = jnp.float32
bf16 = jnp.bfloat16
i32 = jnp.int32
VMEM = pltpu.VMEM


def lanes(shape):
    return lax.broadcasted_iota(i32, shape, 1)


def rolled(value, steps):
    steps = steps % value.shape[1]
    return pltpu.roll(value, steps, 1) if steps else value


def pick(table, index):
    return jnp.take_along_axis(table, index, axis=1, mode="promise_in_bounds")


def parabola(c, right, left, centre):
    jump = right - left
    curve = 72.0 * centre - 3.0 * (left + right)
    return c * (1 / 12) * (right - 0.5 * c * (jump - (1.0 - (2.0 / 3.0) * c) * curve))


def times(value, matrix):
    high = value.astype(bf16)
    low = (value - high.astype(f32)).astype(bf16)
    return jnp.dot(jnp.concatenate([high, low], axis=1), matrix, preferred_element_type=f32)


def for_west(packed):
    half, cells = packed.shape[0] // 2, packed.shape[1]
    lane = lanes((half, cells))
    place = lane % SEG
    first = (lane >= OFF_LANE) & (lane < OFF_LANE + 2)
    first = first | ((lane < OFF_LANE) & (place >= WEST - 2) & (place < WEST + 2))
    return jnp.where(first, packed[:half], rolled(packed[half:], PAIR))


def edge_weights(gap):
    def weight(gap):
        inner = (gap == 0) | (gap == 1)
        outer = (gap == -1) | (gap == 2)
        return jnp.where(inner, 7.0, jnp.where(outer, -1.0, 0.0))

    return weight(gap), weight(gap + 1)


def split(table, cells):
    return [table[:, i : i + cells] for i in range(0, table.shape[1], cells)]


def pack_kernel(
    lat_count, tracers, offsets, fraction, courant,
    field, offset, part, north, packed, to_east, to_west, pole, pole_rest, flux, seam_index, seam_part, block_matrix,
    seam_matrix, own_matrix, sems,
):
    depth, row_count, cells = field.shape
    copies = [
        pltpu.make_async_copy(source, target, sems.at[i])
        for i, (source, target) in enumerate(
            ((tracers, field), (offsets, offset), (fraction, part), (courant, north))
        )
    ]
    for copy in copies:
        copy.start()
    for copy in copies:
        copy.wait()
    shape = (row_count, cells)
    lane = lanes(shape)
    message = jnp.where(
        lane == OFF_LANE,
        rolled(offset[...].astype(f32), OFF_LANE),
        jnp.where(lane == FRAC_LANE, rolled(part[...], FRAC_LANE), 0.0),
    )
    for t in range(depth):
        mine = (lane >= t * SEG) & (lane < (t + 1) * SEG)
        message = jnp.where(mine, rolled(field[t], t * SEG + WEST), message)
    packed[...] = message
    to_east[:row_count] = message
    to_west[...] = for_west(message)
    lat = lax.axis_index("lat")
    south = lat == 0

    @pl.when(south | (lat == lat_count - 1))
    def _():
        base, band, polar, mid = pole_places(south, row_count)
        rows = [field[t, pl.ds(band, BAND)] for t in range(depth)]
        lane = lanes(rows[0].shape)
        half = cells // 2
        for t in range(0, depth - 1, 2):
            value = jnp.where(lane >= half, rows[t], rolled(rows[t + 1], half))
            to_east[pl.ds(pl.multiple_of(base + t // 2 * BAND, 8), BAND)] = value
        rest = rolled(rows[depth - 1], OFF_LANE - cells)
        for t in range(depth):
            mine = (lane >= 3 * t) & (lane < 3 * t + 3)
            rest = jnp.where(mine, rolled(rows[t], 3 * t + 3 - half), rest)
        kept = (lane % SEG < WEST) | (lane >= OFF_LANE)
        for i, value in enumerate((rest, rolled(rest, WEST))):
            at = pl.ds(pl.multiple_of(mid + i * BAND, 8), BAND)
            to_east[at] = jnp.where(kept, to_east[at], value)
        for t in range(depth):
            value = field[t, pl.ds(polar, POLAR)]
            pole[t * POLAR : (t + 1) * POLAR] = value
            if t < WITH_WEST:
                to_east[row_count + t * POLAR : row_count + (t + 1) * POLAR] = value
            else:
                pole_rest[(t - WITH_WEST) * POLAR : (t - WITH_WEST + 1) * POLAR] = value
    pl.when(goes_early())(
        lambda: own_work(
            lat_count, field, offset, part, flux, seam_index, seam_part, block_matrix, seam_matrix, own_matrix
        )
    )


def pole_places(south, row_count):
    places = (
        jnp.where(south, 0, row_count - POLE),
        jnp.where(south, POLAR, row_count - POLE),
        jnp.where(south, 0, row_count - POLAR),
        jnp.where(south, POLE, 0),
    )
    return [pl.multiple_of(place, 8) for place in places]


def by_place(lat_count, away, south, north):
    lat = lax.axis_index("lat")
    if away is not None:
        pl.when((lat > 0) & (lat < lat_count - 1))(away)
    pl.when(lat == 0)(south)
    pl.when(lat == lat_count - 1)(north)


def pieces(row_count):
    middle = [(POLE, row_count - 2 * POLE)] if row_count > 2 * POLE else []
    return [(0, POLE), *middle, (row_count - POLE, POLE)]


def mid_pieces(row_count):
    return pieces(row_count), pieces(row_count)[1:], pieces(row_count)[:-1]


def own_faces(first_row, count, field, offset, part, own_matrix, flux, seam_index, seam_part):
    depth, _, cells = field.shape
    at = pl.ds(first_row, count)
    shape = (count, cells)
    lane = lanes(shape)
    place = lane % SEG
    offsets = offset[at]
    courant = part[at]
    index = (lane - offsets - 1) & (cells - 1)
    own = field[:, at].reshape(depth * count, cells)
    tables = times(own, own_matrix[...])
    for t in range(depth):
        sums, right, left = split(tables[t * count : (t + 1) * count], cells)
        value = field[t, at]
        flux[t, at] = (
            sums
            - value
            - pick(sums, index)
            + parabola(
                courant, pick(right, index), pick(left, index), pick(value, index)
            )
        )
    first = (place - WEST) & (cells - 1)
    final = jnp.full(shape, cells - 1, i32)
    seam_index[0, at] = (lane - pick(offsets, first) - 1) & (cells - 1)
    seam_index[1, at] = (lane - pick(offsets, final) - 1) & (cells - 1)
    seam_part[0, at] = pick(courant, first)
    seam_part[1, at] = pick(courant, final)


def goes_early():
    lat, lon = lax.axis_index("lat"), lax.axis_index("lon")
    return (lon == 0) & (lat < 2)


def own_kernel(
    lat_count, field, offset, part, flux_given, index_given, part_given, block_given, seam_given,
    flux, seam_index, seam_part, block_matrix, seam_matrix, own_matrix,
):
    del flux_given, index_given, part_given, block_given, seam_given
    pl.when(~goes_early())(
        lambda: own_work(
            lat_count, field, offset, part, flux, seam_index, seam_part, block_matrix, seam_matrix, own_matrix
        )
    )


def own_work(
    lat_count, field, offset, part, flux, seam_index, seam_part, block_matrix, seam_matrix, own_matrix
):
    _, row_count, cells = field.shape
    shape = (cells, cells)
    source = lax.broadcasted_iota(i32, shape, 0)
    target = lax.broadcasted_iota(i32, shape, 1)
    gap = source - target
    upto = jnp.where(gap <= 0, 1.0, 0.0)
    right, left = edge_weights(gap)
    own = jnp.concatenate([upto, right, left, upto - 1.0], axis=1).astype(bf16)
    zeros = jnp.zeros(shape, f32)
    beyond = gap + jnp.where(source < cells // 2, cells, -cells)
    beside = jnp.concatenate([zeros, *edge_weights(beyond), zeros], axis=1).astype(bf16)
    together = source // SEG == target // SEG
    seam = jnp.concatenate([jnp.where(together, upto, 0.0), right, left], axis=1).astype(bf16)
    for i in range(2):
        block_matrix[2 * i * cells : (2 * i + 1) * cells] = own
        block_matrix[(2 * i + 1) * cells : (2 * i + 2) * cells] = beside
        own_matrix[i * cells : (i + 1) * cells] = own[:, : 3 * cells]
        seam_matrix[i * cells : (i + 1) * cells] = seam

    def step(parts):
        for first, count in parts:
            own_faces(first, count, field, offset, part, own_matrix, flux, seam_index, seam_part)

    by_place(lat_count, *(functools.partial(step, parts) for parts in mid_pieces(row_count)))


def rows_after(field, flux, packed, seam_index, seam_part, from_west, from_east, seam_matrix, parts):
    def take(ref, *lead):
        return jnp.concatenate([ref[(*lead, part)] for part in parts], axis=0)

    mine, west = take(packed), take(from_west)
    east = from_east if isinstance(from_east, jax.Array) else take(from_east)
    count, cells = mine.shape
    shape = mine.shape
    lane = lanes(shape)
    place = lane % SEG
    near = place < WEST
    rows = jnp.concatenate([jnp.where(near, west, mine), jnp.where(near, mine, east)], axis=0)
    next_face = place == WEST
    next_offset = pick(east, jnp.full(shape, OFF_LANE, i32)).astype(i32)
    next_part = pick(east, jnp.full(shape, FRAC_LANE, i32))
    next_index = (lane - next_offset - 1) & (cells - 1)
    index = jnp.concatenate(
        [take(seam_index, 0), jnp.where(next_face, next_index, take(seam_index, 1))], axis=0
    )
    courant = jnp.concatenate(
        [take(seam_part, 0), jnp.where(next_face, next_part, take(seam_part, 1))], axis=0
    )
    sums, right, left = split(times(rows, seam_matrix[...]), cells)
    faces = (
        sums
        - rows
        - pick(sums, index)
        + parabola(
            courant, pick(right, index), pick(left, index), pick(rows, index)
        )
    )
    east_faces = faces[count:]
    both = jnp.where(place == WEST - 1, east_faces, faces[:count])
    outside = (lane < FACES) | (lane == cells - 1)
    results = []
    for t in range(field.shape[0]):
        steps = -(t * SEG + WEST)
        face = jnp.where(outside, rolled(both, steps), take(flux, t))
        following = jnp.where(lane == cells - 1, rolled(east_faces, steps - 1), rolled(face, -1))
        results.append(take(field, t) - (following - face))
    return results


def edge_kernel(
    lat_count, field, flux, packed, seam_index, seam_part, seam_matrix, north, from_east, from_west,
    message_a, message_b, wide, east,
):
    depth, row_count, _ = field.shape
    half = row_count // 2
    even = lax.axis_index("lat") % 2 == 0

    def step(parts, beyond):
        return rows_after(
            field, flux, packed, seam_index, seam_part, from_west, beyond, seam_matrix, parts
        )

    def send(t, top, bottom):
        rows = slice(3 * t, 3 * t + 3)
        message_a[rows] = jnp.where(even, top, bottom)
        message_b[rows] = jnp.where(even, bottom, top)

    def away():
        beyond = jnp.concatenate(
            [from_east[:EDGE], rolled(from_east[half - EDGE :], -PAIR)], axis=0
        )
        after = step((pl.ds(0, EDGE), pl.ds(row_count - EDGE, EDGE)), beyond)
        for t in range(depth):
            send(t, after[t][2 * EDGE - 3 :], after[t][:3])

    def polar_device(parts):
        east[:half] = from_east[...]
        east[half:] = rolled(from_east[...], -PAIR)
        for first, count in parts:
            after = step((pl.ds(first, count),), east)
            for t in range(depth):
                wide[t, first : first + count] = after[t]
        for t in range(depth):
            send(t, wide[t, row_count - 3 :], wide[t, :3])

    by_place(
        lat_count, away, *(functools.partial(polar_device, parts) for parts in mid_pieces(row_count)[1:])
    )
    message_a[3 * depth : 3 * depth + 1] = north[:1]
    message_b[3 * depth : 3 * depth + 1] = north[:1]


def rows_between(near, far, near_field, far_field, first, offset, courant, next_offset, next_courant):
    cells = near_field.shape[1]
    lane = lanes(near_field.shape)
    source = lane - offset - 1
    index = source & (cells - 1)
    close = source >= first

    def both(here, there):
        return jnp.where(close, pick(here, index), pick(there, index))

    face = both(near[0], far[3]) - parabola(
        courant, both(near[1], far[1]), both(near[2], far[2]), both(near_field, far_field)
    )
    last = near[0] - parabola(next_courant, near[1], near[2], near_field)
    last = pick(last, (cells - 1 - next_offset) & (cells - 1))
    return rolled(jnp.where(lane == 0, last, face), -1) - face


def merid_flux(wide, t, courant, first, count):
    cell = [wide[t, first + k : first + k + count] for k in (-3, -2, -1, 0, 1)]
    left = 7.0 * (cell[1] + cell[2]) - (cell[0] + cell[3])
    right = 7.0 * (cell[2] + cell[3]) - (cell[1] + cell[4])
    return parabola(courant, right, left, cell[2])


def middle_kernel(
    lat_count, field, offset, part, north, flux, packed, seam_index, seam_part, seam_matrix, block_matrix,
    from_east, from_far, from_west, given_wide, given_east, wide, east, inner, far, faces,
):
    del given_wide, given_east
    depth, row_count, cells = field.shape
    half = row_count // 2
    far[:half] = from_far[...]
    far[half:] = rolled(from_far[...], -PAIR)

    def away():
        east[:half] = from_east[...]
        east[half:] = rolled(from_east[...], -PAIR)
        for first, count in pieces(row_count):
            after = rows_after(
                field, flux, packed, seam_index, seam_part, from_west, east, seam_matrix, (pl.ds(first, count),)
            )
            for t in range(depth):
                wide[t, first : first + count] = after[t]
        inner_rows(wide, north, faces, inner, EDGE, row_count - 2 * EDGE)

    def polar_device(south):
        band_step(south, field, offset, part, east, from_west, block_matrix, wide)
        first, _ = near_pole(south, row_count)
        inner_rows(
            wide, north, faces, inner, first + POLAR if south else EDGE, row_count - 2 * EDGE - POLAR
        )

    by_place(
        lat_count, away, functools.partial(polar_device, True), functools.partial(polar_device, False)
    )


def near_pole(south, row_count):
    return (EDGE, POLAR) if south else (row_count - EDGE - POLAR, POLAR)


def inner_rows(wide, north, faces, result, first, count):
    for t in range(wide.shape[0]):
        faces[t, :count] = merid_flux(wide, t, north[first : first + count], first, count)
        end = first + count
        faces[t, count : count + 1] = merid_flux(wide, t, north[end : end + 1], end, 1)
        result[t, first - EDGE : end - EDGE] = wide[t, first:end] - (
            faces[t, 1 : 1 + count] - faces[t, :count]
        )


def with_sides(west, own, east):
    beside = jnp.where(lanes(own.shape) < own.shape[1] // 2, east, west)
    return jnp.concatenate([own, beside], axis=1)


def unpacked(ref, rows, lane, depth):
    value = ref[rows]
    return jnp.concatenate([rolled(value, lane - t * SEG) for t in range(depth)], axis=0)


def stacked(ref, rows):
    return ref[:, rows, :].reshape(-1, ref.shape[2])


def row_values(offset, part, east, rows):
    beyond = east[rows]
    return (
        offset[rows],
        part[rows],
        pick(beyond, jnp.full(beyond.shape, OFF_LANE, i32)).astype(i32),
        pick(beyond, jnp.full(beyond.shape, FRAC_LANE, i32)),
    )


def band_step(south, field, offset, part, east, from_west, block_matrix, wide):
    depth, row_count, cells = field.shape
    base, band, _, mid = (int(place) for place in static_places(south, row_count))
    rows = pl.ds(band, BAND)
    own = stacked(field, rows)
    half = cells // 2
    pair = from_west[mid : mid + BAND], from_west[mid + BAND : mid + 2 * BAND]
    lane = lanes(pair[0].shape)
    rest = jnp.where(lane % SEG >= WEST, pair[0], rolled(pair[1], -WEST))
    west = []
    for t in range(depth):
        if t < depth - 1:
            value = from_west[base + t // 2 * BAND : base + (t // 2 + 1) * BAND]
            value = rolled(value, half) if t % 2 else value
        else:
            value = rolled(rest, cells - OFF_LANE)
        inner = jnp.where(lane >= half - 3, rolled(rest, half - 3 - 3 * t), 0.0)
        west.append(jnp.where(lane >= half, value, inner))
    west = jnp.concatenate(west, axis=0)
    beyond = unpacked(east, rows, -WEST, depth)
    tables = jnp.concatenate([with_sides(west, own, beyond), with_sides(west, west, own)], axis=0)
    tables = times(tables, block_matrix[...])
    common = row_values(offset, part, east, rows)
    for t in range(depth):
        at = slice(t * BAND, (t + 1) * BAND)
        both = [split(tables[first : first + BAND], cells) for first in (t * BAND, (depth + t) * BAND)]
        wide[t, rows] = rows_between(*both, own[at], west[at], 0, *common)


def static_places(south, row_count):
    return (0, POLAR, 0, POLE) if south else (row_count - POLE, row_count - POLE, row_count - POLAR, 0)


def edge_rows(lat_count, wide, north, message_b, message_a, low, high, result):
    depth, row_count, cells = wide.shape
    lat = lax.axis_index("lat")
    even = lat % 2 == 0
    south, top = lat == 0, lat == lat_count - 1
    end = 3 * depth
    north_courant = jnp.where(even, message_a[end : end + 1], message_b[end : end + 1])
    north_courant = jnp.where(top, 0.0, north_courant)
    first_row = lax.broadcasted_iota(i32, (EDGE, cells), 0)
    low_courant = jnp.where(south & (first_row == 0), 0.0, north[:EDGE])
    high_next = jnp.concatenate([north[row_count - EDGE + 1 :], north_courant], axis=0)
    for t in range(depth):
        rows = slice(3 * t, 3 * t + 3)
        from_a, from_b = message_a[rows], message_b[rows]
        low[t, EDGE - 3 : EDGE] = jnp.where(south, 0.0, jnp.where(even, from_b, from_a))
        low[t, EDGE : 3 * EDGE] = wide[t, : 2 * EDGE]
        high[t, : 2 * EDGE] = wide[t, row_count - 2 * EDGE :]
        high[t, 2 * EDGE : 2 * EDGE + 3] = jnp.where(top, 0.0, jnp.where(even, from_a, from_b))
    for t in range(depth):
        south_face = merid_flux(low, t, low_courant, EDGE, EDGE)
        north_face = merid_flux(low, t, north[1 : EDGE + 1], EDGE + 1, EDGE)
        result[0, t] = low[t, EDGE : 2 * EDGE] - (north_face - south_face)
        south_face = merid_flux(high, t, north[row_count - EDGE :], EDGE, EDGE)
        north_face = merid_flux(high, t, high_next, EDGE + 1, EDGE)
        result[1, t] = high[t, EDGE : 2 * EDGE] - (north_face - south_face)


def copy_edges(result, out, sems):
    row_count = out.shape[1]
    return [
        pltpu.make_async_copy(result.at[i], out.at[:, pl.ds(first, EDGE)], sems.at[i])
        for i, first in enumerate((0, row_count - EDGE))
    ]


def join_kernel(from_west, rest, after, joined):
    del after
    count = joined.shape[0] - rest.shape[0]
    joined[:count] = from_west[from_west.shape[0] - count :]
    joined[count:] = rest[...]


def poles_kernel(
    lat_count, field, offset, part, north, block_matrix, east, far, pole_one, pole_two, message_b, message_a,
    given_wide, given_inner, wide, inner, out, faces, low, high, result, sems,
):
    del given_wide, given_inner

    def polar_device(south):
        depth, row_count, cells = field.shape
        near, beside = near_pole(south, row_count)
        done = near + POLAR if south else EDGE
        count = row_count - 2 * EDGE - POLAR
        copies = [
            pltpu.make_async_copy(
                inner.at[:, pl.ds(first - EDGE, size)], out.at[:, pl.ds(first, size)], sems.at[2 + i]
            )
            for i, (first, size) in enumerate(((done, count), (near, beside)))
        ]
        copies[0].start()
        first = static_places(south, row_count)[2]
        rows = pl.ds(first, POLAR)
        own, west, west_two = stacked(field, rows), pole_one[...], pole_two[...]
        beyond = unpacked(far, rows, cells - WEST, depth)
        tables = jnp.concatenate(
            [with_sides(west_two, west, own), with_sides(beyond, west_two, west)], axis=0
        )
        tables = times(tables, block_matrix[...])
        common = row_values(offset, part, east, rows)
        for t in range(depth):
            at = slice(t * POLAR, (t + 1) * POLAR)
            both = [split(tables[start : start + POLAR], cells) for start in (t * POLAR, (depth + t) * POLAR)]
            wide[t, rows] = rows_between(*both, west[at], west_two[at], -cells, *common)
        inner_rows(wide, north, faces, inner, near, beside)
        copies[1].start()
        edge_rows(lat_count, wide, north, message_b, message_a, low, high, result)
        copies += copy_edges(result, out, sems)
        for copy in copies[2:]:
            copy.start()
        for copy in copies:
            copy.wait()

    by_place(
        lat_count, None, functools.partial(polar_device, True), functools.partial(polar_device, False)
    )


def last_kernel(
    lat_count, wide, inner, north, message_b, message_a, given_out, out, low, high, result, sems
):
    del given_out

    def away():
        count = inner.shape[1]
        inner_copy = pltpu.make_async_copy(inner, out.at[:, pl.ds(EDGE, count)], sems.at[2])
        inner_copy.start()
        edge_rows(lat_count, wide, north, message_b, message_a, low, high, result)
        copies = copy_edges(result, out, sems)
        for copy in copies:
            copy.start()
        for copy in (inner_copy, *copies):
            copy.wait()

    lat = lax.axis_index("lat")
    pl.when((lat > 0) & (lat < lat_count - 1))(away)


def cost(microseconds):
    return pl.CostEstimate(
        flops=int(microseconds * 1e8), bytes_accessed=int(microseconds * 3e6), transcendentals=0
    )


def in_vmem(*values):
    return [pltpu.with_memory_space_constraint(value, VMEM) for value in values]


def whole(count):
    return [pl.BlockSpec(memory_space=VMEM)] * count


def anywhere(count):
    return [pl.BlockSpec(memory_space=pl.ANY)] * count


def on_device(lat_count, lon_count, tracers, offsets, fraction, courant_north):
    tracer_count, level_count, row_count, cells = tracers.shape
    depth = tracer_count * level_count
    shape = (row_count, cells)
    stack = (depth, row_count, cells)
    dma = pltpu.SemaphoreType.DMA

    def along_lon(value, steps, everywhere=True):
        pairs = []
        for l in range(lat_count):
            from_pole = min(l, lat_count - 1 - l)
            for o in range(lon_count):
                if everywhere or from_pole == 0 or lat_count % 2 or lon_count % 2:
                    target = (l, (o + steps) % lon_count)
                else:
                    target = (l, o ^ 1) if from_pole == 1 else (l ^ 1, o)
                pairs.append((l * lon_count + o, target[0] * lon_count + target[1]))
        return lax.ppermute(value, ("lat", "lon"), pairs)

    def along_lat(value, first):
        pairs = []
        last_lat, last_lon = lat_count - 1, lon_count - 1
        for l in range(lat_count):
            other = l + 1 if (l - first) % 2 == 0 else l - 1
            for o in range(lon_count):
                if 0 <= other < lat_count:
                    target = (other, o)
                elif lat_count % 2:
                    target = (l, (o + 1) % lon_count)
                elif l == 0:
                    target = (0, o - 1) if o else (last_lat, 0)
                else:
                    target = (last_lat, o + 1) if o < last_lon else (0, last_lon)
                pairs.append((l * lon_count + o, target[0] * lon_count + target[1]))
        return lax.ppermute(value, ("lat", "lon"), pairs)

    own_shapes = [
        VMEM(stack, f32),
        VMEM((2, *shape), i32),
        VMEM((2, *shape), f32),
        VMEM((4 * cells, 4 * cells), bf16),
        VMEM((2 * cells, 3 * cells), bf16),
    ]
    own_matrix = VMEM((2 * cells, 3 * cells), bf16)
    field, offset, part, north, packed, to_east, to_west, pole, pole_rest, *own = in_vmem(
        *pl.pallas_call(
            functools.partial(pack_kernel, lat_count),
            out_shape=[
                VMEM(stack, f32),
                VMEM(shape, i32),
                VMEM(shape, f32),
                VMEM(shape, f32),
                VMEM(shape, f32),
                VMEM((row_count + WITH_WEST * POLAR, cells), f32),
                VMEM((row_count // 2, cells), f32),
                VMEM((depth * POLAR, cells), f32),
                VMEM(((depth - WITH_WEST) * POLAR, cells), f32),
                *own_shapes,
            ],
            in_specs=anywhere(4),
            out_specs=whole(14),
            scratch_shapes=[own_matrix, dma((4,))],
            cost_estimate=cost(1.0),
            name="pack",
        )(tracers.reshape(stack), offsets, fraction, courant_north)
    )
    from_west = along_lon(to_east, 1)
    from_east = along_lon(to_west, -1)
    from_far = from_east if lon_count == 4 else along_lon(to_west, 3)
    pole_one = along_lon(pole_rest, 1, False)
    pole_two = along_lon(pole, 2, False)

    flux, seam_index, seam_part, block_matrix, seam_matrix = in_vmem(
        *pl.pallas_call(
            functools.partial(own_kernel, lat_count),
            out_shape=own_shapes,
            in_specs=whole(8),
            out_specs=whole(5),
            scratch_shapes=[own_matrix],
            input_output_aliases={3 + i: i for i in range(5)},
            cost_estimate=cost(2.0),
            name="own",
        )(field, offset, part, *own)
    )
    from_west, from_east, from_far, pole_one, pole_two = in_vmem(
        from_west, from_east, from_far, pole_one, pole_two
    )

    message = (3 * depth + 1, cells)
    longer = 24
    message_a, message_b, wide, east = in_vmem(
        *pl.pallas_call(
            functools.partial(edge_kernel, lat_count),
            out_shape=[VMEM(message, f32), VMEM((longer, cells), f32), VMEM(stack, f32), VMEM(shape, f32)],
            in_specs=whole(9),
            out_specs=whole(4),
            cost_estimate=cost(4.0),
            name="edge",
        )(field, flux, packed, seam_index, seam_part, seam_matrix, north, from_east, from_west)
    )
    message_a = along_lat(message_a, 0)
    message_b = along_lat(message_b, 1)

    inner = VMEM((depth, row_count - 2 * EDGE, cells), f32)
    faces = VMEM((depth, row_count - EDGE, cells), f32)
    wide, east, inner_part, far = in_vmem(
        *pl.pallas_call(
            functools.partial(middle_kernel, lat_count),
            out_shape=[VMEM(stack, f32), VMEM(shape, f32), inner, VMEM(shape, f32)],
            in_specs=whole(15),
            out_specs=whole(4),
            scratch_shapes=[faces],
            input_output_aliases={13: 0, 14: 1},
            cost_estimate=cost(0.0),
            name="middle",
        )(
            field, offset, part, north, flux, packed, seam_index, seam_part, seam_matrix, block_matrix,
            from_east, from_far, from_west, wide, east,
        )
    )

    pole_one = pl.pallas_call(
        join_kernel,
        out_shape=VMEM((depth * POLAR, cells), f32),
        in_specs=whole(3),
        out_specs=pl.BlockSpec(memory_space=VMEM),
        cost_estimate=cost(0.3),
        name="join",
    )(from_west, pole_one, far)
    pole_one, message_a, message_b = in_vmem(pole_one, message_a, message_b)
    scratch = [
        VMEM((depth, 3 * EDGE, cells), f32),
        VMEM((depth, 3 * EDGE, cells), f32),
        VMEM((2, depth, EDGE, cells), f32),
        dma((4,)),
    ]
    polar_b = message_b if lat_count % 2 else message_a
    wide, inner, out = pl.pallas_call(
        functools.partial(poles_kernel, lat_count),
        out_shape=[VMEM(stack, f32), inner, jax.ShapeDtypeStruct(stack, f32)],
        in_specs=whole(13),
        out_specs=whole(2) + anywhere(1),
        scratch_shapes=[faces, *scratch],
        input_output_aliases={11: 0, 12: 1},
        cost_estimate=cost(0.0),
        name="poles",
    )(
        field, offset, part, north, block_matrix, east, far, pole_one, pole_two, polar_b, message_a,
        wide, inner_part,
    )

    out = pl.pallas_call(
        functools.partial(last_kernel, lat_count),
        out_shape=jax.ShapeDtypeStruct(stack, f32),
        in_specs=whole(5) + anywhere(1),
        out_specs=pl.BlockSpec(memory_space=pl.ANY),
        scratch_shapes=scratch,
        input_output_aliases={5: 0},
        cost_estimate=cost(0.7),
        name="last",
    )(*in_vmem(wide, inner), north, message_b, message_a, out)
    return out.reshape(tracers.shape)


def solution(mesh):
    placed = (P(None, None, "lat", "lon"), P("lat", "lon"), P("lat", "lon"), P("lat", "lon"))
    return jax.shard_map(
        functools.partial(on_device, mesh.shape["lat"], mesh.shape["lon"]),
        mesh=mesh,
        in_specs=placed,
        out_specs=P(None, None, "lat", "lon"),
        check_vma=False,
    )
```

```python
import functools

import jax
import jax.numpy as jnp
from jax import lax
from jax.experimental import pallas as pl
from jax.experimental.pallas import tpu as pltpu
from jax.sharding import PartitionSpec as P

POLAR = 24
BAND = 24
POLE = POLAR + BAND
WEST = 12
SEG = 24
FACES = 11
OFF_LANE = 120
FRAC_LANE = 121
PAIR = 4
WITH_WEST = 3
EDGE = 8

f32 = jnp.float32
bf16 = jnp.bfloat16
i32 = jnp.int32
VMEM = pltpu.VMEM


def lanes(shape):
    return lax.broadcasted_iota(i32, shape, 1)


def rolled(value, steps):
    steps = steps % value.shape[1]
    return pltpu.roll(value, steps, 1) if steps else value


def pick(table, index):
    return jnp.take_along_axis(table, index, axis=1, mode="promise_in_bounds")


def parabola(c, right, left, centre):
    jump = right - left
    curve = 72.0 * centre - 3.0 * (left + right)
    return c * (1 / 12) * (right - 0.5 * c * (jump - (1.0 - (2.0 / 3.0) * c) * curve))


def times(value, matrix):
    high = value.astype(bf16)
    low = (value - high.astype(f32)).astype(bf16)
    return jnp.dot(jnp.concatenate([high, low], axis=1), matrix, preferred_element_type=f32)


def for_west(packed):
    half, cells = packed.shape[0] // 2, packed.shape[1]
    lane = lanes((half, cells))
    place = lane % SEG
    first = (lane >= OFF_LANE) & (lane < OFF_LANE + 2)
    first = first | ((lane < OFF_LANE) & (place >= WEST - 2) & (place < WEST + 2))
    return jnp.where(first, packed[:half], rolled(packed[half:], PAIR))


def edge_weights(gap):
    def weight(gap):
        inner = (gap == 0) | (gap == 1)
        outer = (gap == -1) | (gap == 2)
        return jnp.where(inner, 7.0, jnp.where(outer, -1.0, 0.0))

    return weight(gap), weight(gap + 1)


def split(table, cells):
    return [table[:, i : i + cells] for i in range(0, table.shape[1], cells)]


def pack_kernel(
    lat_count, tracers, offsets, fraction, courant,
    field, offset, part, north, packed, to_east, to_west, pole, pole_rest, flux, seam_index, seam_part, block_matrix,
    seam_matrix, own_matrix, sems,
):
    depth, row_count, cells = field.shape
    copies = [
        pltpu.make_async_copy(source, target, sems.at[i])
        for i, (source, target) in enumerate(
            ((tracers, field), (offsets, offset), (fraction, part), (courant, north))
        )
    ]
    for copy in copies:
        copy.start()
    for copy in copies[:3]:
        copy.wait()
    shape = (row_count, cells)
    lane = lanes(shape)
    message = jnp.where(
        lane == OFF_LANE,
        rolled(offset[...].astype(f32), OFF_LANE),
        jnp.where(lane == FRAC_LANE, rolled(part[...], FRAC_LANE), 0.0),
    )
    for t in range(depth):
        mine = (lane >= t * SEG) & (lane < (t + 1) * SEG)
        message = jnp.where(mine, rolled(field[t], t * SEG + WEST), message)
    packed[...] = message
    to_east[:row_count] = message
    to_west[...] = for_west(message)
    lat = lax.axis_index("lat")
    south = lat == 0

    @pl.when(south | (lat == lat_count - 1))
    def _():
        base, band, polar, mid = pole_places(south, row_count)
        rows = [field[t, pl.ds(band, BAND)] for t in range(depth)]
        lane = lanes(rows[0].shape)
        half = cells // 2
        for t in range(0, depth - 1, 2):
            value = jnp.where(lane >= half, rows[t], rolled(rows[t + 1], half))
            to_east[pl.ds(pl.multiple_of(base + t // 2 * BAND, 8), BAND)] = value
        rest = rolled(rows[depth - 1], OFF_LANE - cells)
        for t in range(depth):
            mine = (lane >= 3 * t) & (lane < 3 * t + 3)
            rest = jnp.where(mine, rolled(rows[t], 3 * t + 3 - half), rest)
        kept = (lane % SEG < WEST) | (lane >= OFF_LANE)
        for i, value in enumerate((rest, rolled(rest, WEST))):
            at = pl.ds(pl.multiple_of(mid + i * BAND, 8), BAND)
            to_east[at] = jnp.where(kept, to_east[at], value)
        for t in range(depth):
            value = field[t, pl.ds(polar, POLAR)]
            pole[t * POLAR : (t + 1) * POLAR] = value
            if t < WITH_WEST:
                to_east[row_count + t * POLAR : row_count + (t + 1) * POLAR] = value
            else:
                pole_rest[(t - WITH_WEST) * POLAR : (t - WITH_WEST + 1) * POLAR] = value
    pl.when(goes_early())(
        lambda: own_work(
            lat_count, field, offset, part, flux, seam_index, seam_part, block_matrix, seam_matrix, own_matrix
        )
    )
    copies[3].wait()


def pole_places(south, row_count):
    places = (
        jnp.where(south, 0, row_count - POLE),
        jnp.where(south, POLAR, row_count - POLE),
        jnp.where(south, 0, row_count - POLAR),
        jnp.where(south, POLE, 0),
    )
    return [pl.multiple_of(place, 8) for place in places]


def by_place(lat_count, away, south, north):
    lat = lax.axis_index("lat")
    if away is not None:
        pl.when((lat > 0) & (lat < lat_count - 1))(away)
    pl.when(lat == 0)(south)
    pl.when(lat == lat_count - 1)(north)


def pieces(row_count):
    middle = [(POLE, row_count - 2 * POLE)] if row_count > 2 * POLE else []
    return [(0, POLE), *middle, (row_count - POLE, POLE)]


def mid_pieces(row_count):
    return pieces(row_count), pieces(row_count)[1:], pieces(row_count)[:-1]


def own_faces(first_row, count, field, offset, part, own_matrix, flux, seam_index, seam_part):
    depth, _, cells = field.shape
    at = pl.ds(first_row, count)
    shape = (count, cells)
    lane = lanes(shape)
    place = lane % SEG
    offsets = offset[at]
    courant = part[at]
    index = (lane - offsets - 1) & (cells - 1)
    own = field[:, at].reshape(depth * count, cells)
    tables = times(own, own_matrix[...])
    for t in range(depth):
        sums, right, left = split(tables[t * count : (t + 1) * count], cells)
        value = field[t, at]
        flux[t, at] = (
            sums
            - value
            - pick(sums, index)
            + parabola(
                courant, pick(right, index), pick(left, index), pick(value, index)
            )
        )
    first = (place - WEST) & (cells - 1)
    final = jnp.full(shape, cells - 1, i32)
    seam_index[0, at] = (lane - pick(offsets, first) - 1) & (cells - 1)
    seam_index[1, at] = (lane - pick(offsets, final) - 1) & (cells - 1)
    seam_part[0, at] = pick(courant, first)
    seam_part[1, at] = pick(courant, final)


def goes_early():
    lat, lon = lax.axis_index("lat"), lax.axis_index("lon")
    return (lon == 0) & (lat < 2)


def own_kernel(
    lat_count, field, offset, part, flux_given, index_given, part_given, block_given, seam_given,
    flux, seam_index, seam_part, block_matrix, seam_matrix, own_matrix,
):
    del flux_given, index_given, part_given, block_given, seam_given
    pl.when(~goes_early())(
        lambda: own_work(
            lat_count, field, offset, part, flux, seam_index, seam_part, block_matrix, seam_matrix, own_matrix
        )
    )


def own_work(
    lat_count, field, offset, part, flux, seam_index, seam_part, block_matrix, seam_matrix, own_matrix
):
    _, row_count, cells = field.shape
    shape = (cells, cells)
    source = lax.broadcasted_iota(i32, shape, 0)
    target = lax.broadcasted_iota(i32, shape, 1)
    gap = source - target
    upto = jnp.where(gap <= 0, 1.0, 0.0)
    right, left = edge_weights(gap)
    own = jnp.concatenate([upto, right, left, upto - 1.0], axis=1).astype(bf16)
    zeros = jnp.zeros(shape, f32)
    beyond = gap + jnp.where(source < cells // 2, cells, -cells)
    beside = jnp.concatenate([zeros, *edge_weights(beyond), zeros], axis=1).astype(bf16)
    together = source // SEG == target // SEG
    seam = jnp.concatenate([jnp.where(together, upto, 0.0), right, left], axis=1).astype(bf16)
    for i in range(2):
        block_matrix[2 * i * cells : (2 * i + 1) * cells] = own
        block_matrix[(2 * i + 1) * cells : (2 * i + 2) * cells] = beside
        own_matrix[i * cells : (i + 1) * cells] = own[:, : 3 * cells]
        seam_matrix[i * cells : (i + 1) * cells] = seam

    def step(parts):
        for first, count in parts:
            own_faces(first, count, field, offset, part, own_matrix, flux, seam_index, seam_part)

    by_place(lat_count, *(functools.partial(step, parts) for parts in mid_pieces(row_count)))


def rows_after(field, flux, packed, seam_index, seam_part, from_west, from_east, seam_matrix, parts):
    def take(ref, *lead):
        return jnp.concatenate([ref[(*lead, part)] for part in parts], axis=0)

    mine, west = take(packed), take(from_west)
    east = from_east if isinstance(from_east, jax.Array) else take(from_east)
    count, cells = mine.shape
    shape = mine.shape
    lane = lanes(shape)
    place = lane % SEG
    near = place < WEST
    rows = jnp.concatenate([jnp.where(near, west, mine), jnp.where(near, mine, east)], axis=0)
    next_face = place == WEST
    next_offset = pick(east, jnp.full(shape, OFF_LANE, i32)).astype(i32)
    next_part = pick(east, jnp.full(shape, FRAC_LANE, i32))
    next_index = (lane - next_offset - 1) & (cells - 1)
    index = jnp.concatenate(
        [take(seam_index, 0), jnp.where(next_face, next_index, take(seam_index, 1))], axis=0
    )
    courant = jnp.concatenate(
        [take(seam_part, 0), jnp.where(next_face, next_part, take(seam_part, 1))], axis=0
    )
    sums, right, left = split(times(rows, seam_matrix[...]), cells)
    faces = (
        sums
        - rows
        - pick(sums, index)
        + parabola(
            courant, pick(right, index), pick(left, index), pick(rows, index)
        )
    )
    east_faces = faces[count:]
    both = jnp.where(place == WEST - 1, east_faces, faces[:count])
    outside = (lane < FACES) | (lane == cells - 1)
    results = []
    for t in range(field.shape[0]):
        steps = -(t * SEG + WEST)
        face = jnp.where(outside, rolled(both, steps), take(flux, t))
        following = jnp.where(lane == cells - 1, rolled(east_faces, steps - 1), rolled(face, -1))
        results.append(take(field, t) - (following - face))
    return results


def edge_kernel(
    lat_count, field, flux, packed, seam_index, seam_part, seam_matrix, north, from_east, from_west,
    message_a, message_b, wide, east,
):
    depth, row_count, _ = field.shape
    half = row_count // 2
    even = lax.axis_index("lat") % 2 == 0

    def step(parts, beyond):
        return rows_after(
            field, flux, packed, seam_index, seam_part, from_west, beyond, seam_matrix, parts
        )

    def send(t, top, bottom):
        rows = slice(3 * t, 3 * t + 3)
        message_a[rows] = jnp.where(even, top, bottom)
        message_b[rows] = jnp.where(even, bottom, top)

    def away():
        beyond = jnp.concatenate(
            [from_east[:EDGE], rolled(from_east[half - EDGE :], -PAIR)], axis=0
        )
        after = step((pl.ds(0, EDGE), pl.ds(row_count - EDGE, EDGE)), beyond)
        for t in range(depth):
            send(t, after[t][2 * EDGE - 3 :], after[t][:3])

    def polar_device(parts):
        east[:half] = from_east[...]
        east[half:] = rolled(from_east[...], -PAIR)
        for first, count in parts:
            after = step((pl.ds(first, count),), east)
            for t in range(depth):
                wide[t, first : first + count] = after[t]
        for t in range(depth):
            send(t, wide[t, row_count - 3 :], wide[t, :3])

    by_place(
        lat_count, away, *(functools.partial(polar_device, parts) for parts in mid_pieces(row_count)[1:])
    )
    message_a[3 * depth : 3 * depth + 1] = north[:1]
    message_b[3 * depth : 3 * depth + 1] = north[:1]


def rows_between(near, far, near_field, far_field, first, offset, courant, next_offset, next_courant):
    cells = near_field.shape[1]
    lane = lanes(near_field.shape)
    source = lane - offset - 1
    index = source & (cells - 1)
    close = source >= first

    def both(here, there):
        return jnp.where(close, pick(here, index), pick(there, index))

    face = both(near[0], far[3]) - parabola(
        courant, both(near[1], far[1]), both(near[2], far[2]), both(near_field, far_field)
    )
    last = near[0] - parabola(next_courant, near[1], near[2], near_field)
    last = pick(last, (cells - 1 - next_offset) & (cells - 1))
    return rolled(jnp.where(lane == 0, last, face), -1) - face


def merid_flux(wide, t, courant, first, count):
    cell = [wide[t, first + k : first + k + count] for k in (-3, -2, -1, 0, 1)]
    left = 7.0 * (cell[1] + cell[2]) - (cell[0] + cell[3])
    right = 7.0 * (cell[2] + cell[3]) - (cell[1] + cell[4])
    return parabola(courant, right, left, cell[2])


def middle_kernel(
    lat_count, field, offset, part, north, flux, packed, seam_index, seam_part, seam_matrix, block_matrix,
    from_east, from_far, from_west, given_wide, given_east, wide, east, inner, far, faces,
):
    del given_wide, given_east
    depth, row_count, cells = field.shape
    half = row_count // 2
    far[:half] = from_far[...]
    far[half:] = rolled(from_far[...], -PAIR)

    def away():
        east[:half] = from_east[...]
        east[half:] = rolled(from_east[...], -PAIR)
        for first, count in pieces(row_count):
            after = rows_after(
                field, flux, packed, seam_index, seam_part, from_west, east, seam_matrix, (pl.ds(first, count),)
            )
            for t in range(depth):
                wide[t, first : first + count] = after[t]
        inner_rows(wide, north, faces, inner, EDGE, row_count - 2 * EDGE)

    def polar_device(south):
        band_step(south, field, offset, part, east, from_west, block_matrix, wide)
        first, _ = near_pole(south, row_count)
        inner_rows(
            wide, north, faces, inner, first + POLAR if south else EDGE, row_count - 2 * EDGE - POLAR
        )

    by_place(
        lat_count, away, functools.partial(polar_device, True), functools.partial(polar_device, False)
    )


def near_pole(south, row_count):
    return (EDGE, POLAR) if south else (row_count - EDGE - POLAR, POLAR)


def inner_rows(wide, north, faces, result, first, count):
    for t in range(wide.shape[0]):
        faces[t, :count] = merid_flux(wide, t, north[first : first + count], first, count)
        end = first + count
        faces[t, count : count + 1] = merid_flux(wide, t, north[end : end + 1], end, 1)
        result[t, first - EDGE : end - EDGE] = wide[t, first:end] - (
            faces[t, 1 : 1 + count] - faces[t, :count]
        )


def with_sides(west, own, east):
    beside = jnp.where(lanes(own.shape) < own.shape[1] // 2, east, west)
    return jnp.concatenate([own, beside], axis=1)


def unpacked(ref, rows, lane, depth):
    value = ref[rows]
    return jnp.concatenate([rolled(value, lane - t * SEG) for t in range(depth)], axis=0)


def stacked(ref, rows):
    return ref[:, rows, :].reshape(-1, ref.shape[2])


def row_values(offset, part, east, rows):
    beyond = east[rows]
    return (
        offset[rows],
        part[rows],
        pick(beyond, jnp.full(beyond.shape, OFF_LANE, i32)).astype(i32),
        pick(beyond, jnp.full(beyond.shape, FRAC_LANE, i32)),
    )


def band_step(south, field, offset, part, east, from_west, block_matrix, wide):
    depth, row_count, cells = field.shape
    base, band, _, mid = (int(place) for place in static_places(south, row_count))
    rows = pl.ds(band, BAND)
    own = stacked(field, rows)
    half = cells // 2
    pair = from_west[mid : mid + BAND], from_west[mid + BAND : mid + 2 * BAND]
    lane = lanes(pair[0].shape)
    rest = jnp.where(lane % SEG >= WEST, pair[0], rolled(pair[1], -WEST))
    west = []
    for t in range(depth):
        if t < depth - 1:
            value = from_west[base + t // 2 * BAND : base + (t // 2 + 1) * BAND]
            value = rolled(value, half) if t % 2 else value
        else:
            value = rolled(rest, cells - OFF_LANE)
        inner = jnp.where(lane >= half - 3, rolled(rest, half - 3 - 3 * t), 0.0)
        west.append(jnp.where(lane >= half, value, inner))
    west = jnp.concatenate(west, axis=0)
    beyond = unpacked(east, rows, -WEST, depth)
    tables = jnp.concatenate([with_sides(west, own, beyond), with_sides(west, west, own)], axis=0)
    tables = times(tables, block_matrix[...])
    common = row_values(offset, part, east, rows)
    for t in range(depth):
        at = slice(t * BAND, (t + 1) * BAND)
        both = [split(tables[first : first + BAND], cells) for first in (t * BAND, (depth + t) * BAND)]
        wide[t, rows] = rows_between(*both, own[at], west[at], 0, *common)


def static_places(south, row_count):
    return (0, POLAR, 0, POLE) if south else (row_count - POLE, row_count - POLE, row_count - POLAR, 0)


def edge_rows(lat_count, wide, north, message_b, message_a, low, high, result):
    depth, row_count, cells = wide.shape
    lat = lax.axis_index("lat")
    even = lat % 2 == 0
    south, top = lat == 0, lat == lat_count - 1
    end = 3 * depth
    north_courant = jnp.where(even, message_a[end : end + 1], message_b[end : end + 1])
    north_courant = jnp.where(top, 0.0, north_courant)
    first_row = lax.broadcasted_iota(i32, (EDGE, cells), 0)
    low_courant = jnp.where(south & (first_row == 0), 0.0, north[:EDGE])
    high_next = jnp.concatenate([north[row_count - EDGE + 1 :], north_courant], axis=0)
    for t in range(depth):
        rows = slice(3 * t, 3 * t + 3)
        from_a, from_b = message_a[rows], message_b[rows]
        low[t, EDGE - 3 : EDGE] = jnp.where(south, 0.0, jnp.where(even, from_b, from_a))
        low[t, EDGE : 3 * EDGE] = wide[t, : 2 * EDGE]
        high[t, : 2 * EDGE] = wide[t, row_count - 2 * EDGE :]
        high[t, 2 * EDGE : 2 * EDGE + 3] = jnp.where(top, 0.0, jnp.where(even, from_a, from_b))
    for t in range(depth):
        south_face = merid_flux(low, t, low_courant, EDGE, EDGE)
        north_face = merid_flux(low, t, north[1 : EDGE + 1], EDGE + 1, EDGE)
        result[0, t] = low[t, EDGE : 2 * EDGE] - (north_face - south_face)
        south_face = merid_flux(high, t, north[row_count - EDGE :], EDGE, EDGE)
        north_face = merid_flux(high, t, high_next, EDGE + 1, EDGE)
        result[1, t] = high[t, EDGE : 2 * EDGE] - (north_face - south_face)


def copy_edges(result, out, sems):
    row_count = out.shape[1]
    return [
        pltpu.make_async_copy(result.at[i], out.at[:, pl.ds(first, EDGE)], sems.at[i])
        for i, first in enumerate((0, row_count - EDGE))
    ]


def join_kernel(from_west, rest, after, joined):
    del after
    count = joined.shape[0] - rest.shape[0]
    joined[:count] = from_west[from_west.shape[0] - count :]
    joined[count:] = rest[...]


def poles_kernel(
    lat_count, field, offset, part, north, block_matrix, east, far, pole_one, pole_two, message_b, message_a,
    given_wide, given_inner, wide, inner, out, faces, low, high, result, sems,
):
    del given_wide, given_inner

    def polar_device(south):
        depth, row_count, cells = field.shape
        near, beside = near_pole(south, row_count)
        done = near + POLAR if south else EDGE
        count = row_count - 2 * EDGE - POLAR
        copies = [
            pltpu.make_async_copy(
                inner.at[:, pl.ds(first - EDGE, size)], out.at[:, pl.ds(first, size)], sems.at[2 + i]
            )
            for i, (first, size) in enumerate(((done, count), (near, beside)))
        ]
        copies[0].start()
        first = static_places(south, row_count)[2]
        rows = pl.ds(first, POLAR)
        own, west, west_two = stacked(field, rows), pole_one[...], pole_two[...]
        beyond = unpacked(far, rows, cells - WEST, depth)
        tables = jnp.concatenate(
            [with_sides(west_two, west, own), with_sides(beyond, west_two, west)], axis=0
        )
        tables = times(tables, block_matrix[...])
        common = row_values(offset, part, east, rows)
        for t in range(depth):
            at = slice(t * POLAR, (t + 1) * POLAR)
            both = [split(tables[start : start + POLAR], cells) for start in (t * POLAR, (depth + t) * POLAR)]
            wide[t, rows] = rows_between(*both, west[at], west_two[at], -cells, *common)
        inner_rows(wide, north, faces, inner, near, beside)
        copies[1].start()
        edge_rows(lat_count, wide, north, message_b, message_a, low, high, result)
        copies += copy_edges(result, out, sems)
        for copy in copies[2:]:
            copy.start()
        for copy in copies:
            copy.wait()

    by_place(
        lat_count, None, functools.partial(polar_device, True), functools.partial(polar_device, False)
    )


def last_kernel(
    lat_count, wide, inner, north, message_b, message_a, given_out, out, low, high, result, sems
):
    del given_out

    def away():
        count = inner.shape[1]
        inner_copy = pltpu.make_async_copy(inner, out.at[:, pl.ds(EDGE, count)], sems.at[2])
        inner_copy.start()
        edge_rows(lat_count, wide, north, message_b, message_a, low, high, result)
        copies = copy_edges(result, out, sems)
        for copy in copies:
            copy.start()
        for copy in (inner_copy, *copies):
            copy.wait()

    lat = lax.axis_index("lat")
    pl.when((lat > 0) & (lat < lat_count - 1))(away)


def cost(microseconds):
    return pl.CostEstimate(
        flops=int(microseconds * 1e8), bytes_accessed=int(microseconds * 3e6), transcendentals=0
    )


def in_vmem(*values):
    return [pltpu.with_memory_space_constraint(value, VMEM) for value in values]


def whole(count):
    return [pl.BlockSpec(memory_space=VMEM)] * count


def anywhere(count):
    return [pl.BlockSpec(memory_space=pl.ANY)] * count


def on_device(lat_count, lon_count, tracers, offsets, fraction, courant_north):
    tracer_count, level_count, row_count, cells = tracers.shape
    depth = tracer_count * level_count
    shape = (row_count, cells)
    stack = (depth, row_count, cells)
    dma = pltpu.SemaphoreType.DMA

    def along_lon(value, steps, everywhere=True):
        pairs = []
        for l in range(lat_count):
            from_pole = min(l, lat_count - 1 - l)
            for o in range(lon_count):
                if everywhere or from_pole == 0 or lat_count % 2 or lon_count % 2:
                    target = (l, (o + steps) % lon_count)
                else:
                    target = (l, o ^ 1) if from_pole == 1 else (l ^ 1, o)
                pairs.append((l * lon_count + o, target[0] * lon_count + target[1]))
        return lax.ppermute(value, ("lat", "lon"), pairs)

    def along_lat(value, first):
        pairs = []
        last_lat, last_lon = lat_count - 1, lon_count - 1
        for l in range(lat_count):
            other = l + 1 if (l - first) % 2 == 0 else l - 1
            for o in range(lon_count):
                if 0 <= other < lat_count:
                    target = (other, o)
                elif lat_count % 2:
                    target = (l, (o + 1) % lon_count)
                elif l == 0:
                    target = (0, o - 1) if o else (last_lat, 0)
                else:
                    target = (last_lat, o + 1) if o < last_lon else (0, last_lon)
                pairs.append((l * lon_count + o, target[0] * lon_count + target[1]))
        return lax.ppermute(value, ("lat", "lon"), pairs)

    own_shapes = [
        VMEM(stack, f32),
        VMEM((2, *shape), i32),
        VMEM((2, *shape), f32),
        VMEM((4 * cells, 4 * cells), bf16),
        VMEM((2 * cells, 3 * cells), bf16),
    ]
    own_matrix = VMEM((2 * cells, 3 * cells), bf16)
    field, offset, part, north, packed, to_east, to_west, pole, pole_rest, *own = in_vmem(
        *pl.pallas_call(
            functools.partial(pack_kernel, lat_count),
            out_shape=[
                VMEM(stack, f32),
                VMEM(shape, i32),
                VMEM(shape, f32),
                VMEM(shape, f32),
                VMEM(shape, f32),
                VMEM((row_count + WITH_WEST * POLAR, cells), f32),
                VMEM((row_count // 2, cells), f32),
                VMEM((depth * POLAR, cells), f32),
                VMEM(((depth - WITH_WEST) * POLAR, cells), f32),
                *own_shapes,
            ],
            in_specs=anywhere(4),
            out_specs=whole(14),
            scratch_shapes=[own_matrix, dma((4,))],
            cost_estimate=cost(1.0),
            name="pack",
        )(tracers.reshape(stack), offsets, fraction, courant_north)
    )
    from_west = along_lon(to_east, 1)
    from_east = along_lon(to_west, -1)
    from_far = from_east if lon_count == 4 else along_lon(to_west, 3)
    pole_one = along_lon(pole_rest, 1, False)
    pole_two = along_lon(pole, 2, False)

    flux, seam_index, seam_part, block_matrix, seam_matrix = in_vmem(
        *pl.pallas_call(
            functools.partial(own_kernel, lat_count),
            out_shape=own_shapes,
            in_specs=whole(8),
            out_specs=whole(5),
            scratch_shapes=[own_matrix],
            input_output_aliases={3 + i: i for i in range(5)},
            cost_estimate=cost(2.0),
            name="own",
        )(field, offset, part, *own)
    )
    from_west, from_east, from_far, pole_one, pole_two = in_vmem(
        from_west, from_east, from_far, pole_one, pole_two
    )

    message = (3 * depth + 1, cells)
    longer = 24
    message_a, message_b, wide, east = in_vmem(
        *pl.pallas_call(
            functools.partial(edge_kernel, lat_count),
            out_shape=[VMEM(message, f32), VMEM((longer, cells), f32), VMEM(stack, f32), VMEM(shape, f32)],
            in_specs=whole(9),
            out_specs=whole(4),
            cost_estimate=cost(4.0),
            name="edge",
        )(field, flux, packed, seam_index, seam_part, seam_matrix, north, from_east, from_west)
    )
    message_a = along_lat(message_a, 0)
    message_b = along_lat(message_b, 1)

    inner = VMEM((depth, row_count - 2 * EDGE, cells), f32)
    faces = VMEM((depth, row_count - EDGE, cells), f32)
    wide, east, inner_part, far = in_vmem(
        *pl.pallas_call(
            functools.partial(middle_kernel, lat_count),
            out_shape=[VMEM(stack, f32), VMEM(shape, f32), inner, VMEM(shape, f32)],
            in_specs=whole(15),
            out_specs=whole(4),
            scratch_shapes=[faces],
            input_output_aliases={13: 0, 14: 1},
            cost_estimate=cost(0.0),
            name="middle",
        )(
            field, offset, part, north, flux, packed, seam_index, seam_part, seam_matrix, block_matrix,
            from_east, from_far, from_west, wide, east,
        )
    )

    pole_one = pl.pallas_call(
        join_kernel,
        out_shape=VMEM((depth * POLAR, cells), f32),
        in_specs=whole(3),
        out_specs=pl.BlockSpec(memory_space=VMEM),
        cost_estimate=cost(0.8),
        name="join",
    )(from_west, pole_one, far)
    pole_one, message_a, message_b = in_vmem(pole_one, message_a, message_b)
    scratch = [
        VMEM((depth, 3 * EDGE, cells), f32),
        VMEM((depth, 3 * EDGE, cells), f32),
        VMEM((2, depth, EDGE, cells), f32),
        dma((4,)),
    ]
    polar_b = message_b if lat_count % 2 else message_a
    wide, inner, out = pl.pallas_call(
        functools.partial(poles_kernel, lat_count),
        out_shape=[VMEM(stack, f32), inner, jax.ShapeDtypeStruct(stack, f32)],
        in_specs=whole(13),
        out_specs=whole(2) + anywhere(1),
        scratch_shapes=[faces, *scratch],
        input_output_aliases={11: 0, 12: 1},
        cost_estimate=cost(0.0),
        name="poles",
    )(
        field, offset, part, north, block_matrix, east, far, pole_one, pole_two, polar_b, message_a,
        wide, inner_part,
    )

    out = pl.pallas_call(
        functools.partial(last_kernel, lat_count),
        out_shape=jax.ShapeDtypeStruct(stack, f32),
        in_specs=whole(5) + anywhere(1),
        out_specs=pl.BlockSpec(memory_space=pl.ANY),
        scratch_shapes=scratch,
        input_output_aliases={5: 0},
        cost_estimate=cost(0.7),
        name="last",
    )(*in_vmem(wide, inner), north, message_b, message_a, out)
    return out.reshape(tracers.shape)


def solution(mesh):
    placed = (P(None, None, "lat", "lon"), P("lat", "lon"), P("lat", "lon"), P("lat", "lon"))
    return jax.shard_map(
        functools.partial(on_device, mesh.shape["lat"], mesh.shape["lon"]),
        mesh=mesh,
        in_specs=placed,
        out_specs=P(None, None, "lat", "lon"),
        check_vma=False,
    )
```

```python
import functools

import jax
import jax.numpy as jnp
from jax import lax
from jax.experimental import pallas as pl
from jax.experimental.pallas import tpu as pltpu
from jax.sharding import PartitionSpec as P

POLAR = 24
BAND = 24
POLE = POLAR + BAND
WEST = 12
SEG = 24
FACES = 11
OFF_LANE = 120
FRAC_LANE = 121
PAIR = 4
WITH_WEST = 2
EDGE = 8

f32 = jnp.float32
bf16 = jnp.bfloat16
i32 = jnp.int32
VMEM = pltpu.VMEM


def lanes(shape):
    return lax.broadcasted_iota(i32, shape, 1)


def rolled(value, steps):
    steps = steps % value.shape[1]
    return pltpu.roll(value, steps, 1) if steps else value


def pick(table, index):
    return jnp.take_along_axis(table, index, axis=1, mode="promise_in_bounds")


def parabola(c, right, left, centre):
    jump = right - left
    curve = 72.0 * centre - 3.0 * (left + right)
    return c * (1 / 12) * (right - 0.5 * c * (jump - (1.0 - (2.0 / 3.0) * c) * curve))


def times(value, matrix):
    high = value.astype(bf16)
    low = (value - high.astype(f32)).astype(bf16)
    return jnp.dot(jnp.concatenate([high, low], axis=1), matrix, preferred_element_type=f32)


def for_west(packed):
    half, cells = packed.shape[0] // 2, packed.shape[1]
    lane = lanes((half, cells))
    place = lane % SEG
    first = (lane >= OFF_LANE) & (lane < OFF_LANE + 2)
    first = first | ((lane < OFF_LANE) & (place >= WEST - 2) & (place < WEST + 2))
    return jnp.where(first, packed[:half], rolled(packed[half:], PAIR))


def edge_weights(gap):
    def weight(gap):
        inner = (gap == 0) | (gap == 1)
        outer = (gap == -1) | (gap == 2)
        return jnp.where(inner, 7.0, jnp.where(outer, -1.0, 0.0))

    return weight(gap), weight(gap + 1)


def split(table, cells):
    return [table[:, i : i + cells] for i in range(0, table.shape[1], cells)]


def pack_kernel(
    lat_count, tracers, offsets, fraction, courant,
    field, offset, part, north, packed, to_east, to_west, pole, pole_rest, flux, seam_index, seam_part, block_matrix,
    seam_matrix, own_matrix, sems,
):
    depth, row_count, cells = field.shape
    copies = [
        pltpu.make_async_copy(source, target, sems.at[i])
        for i, (source, target) in enumerate(
            ((tracers, field), (offsets, offset), (fraction, part), (courant, north))
        )
    ]
    for copy in copies:
        copy.start()
    for copy in copies[:3]:
        copy.wait()
    shape = (row_count, cells)
    lane = lanes(shape)
    message = jnp.where(
        lane == OFF_LANE,
        rolled(offset[...].astype(f32), OFF_LANE),
        jnp.where(lane == FRAC_LANE, rolled(part[...], FRAC_LANE), 0.0),
    )
    for t in range(depth):
        mine = (lane >= t * SEG) & (lane < (t + 1) * SEG)
        message = jnp.where(mine, rolled(field[t], t * SEG + WEST), message)
    packed[...] = message
    to_east[:row_count] = message
    to_west[...] = for_west(message)
    lat = lax.axis_index("lat")
    south = lat == 0

    @pl.when(south | (lat == lat_count - 1))
    def _():
        base, band, polar, mid = pole_places(south, row_count)
        rows = [field[t, pl.ds(band, BAND)] for t in range(depth)]
        lane = lanes(rows[0].shape)
        half = cells // 2
        for t in range(0, depth - 1, 2):
            value = jnp.where(lane >= half, rows[t], rolled(rows[t + 1], half))
            to_east[pl.ds(pl.multiple_of(base + t // 2 * BAND, 8), BAND)] = value
        rest = rolled(rows[depth - 1], OFF_LANE - cells)
        for t in range(depth):
            mine = (lane >= 3 * t) & (lane < 3 * t + 3)
            rest = jnp.where(mine, rolled(rows[t], 3 * t + 3 - half), rest)
        kept = (lane % SEG < WEST) | (lane >= OFF_LANE)
        for i, value in enumerate((rest, rolled(rest, WEST))):
            at = pl.ds(pl.multiple_of(mid + i * BAND, 8), BAND)
            to_east[at] = jnp.where(kept, to_east[at], value)
        for t in range(depth):
            value = field[t, pl.ds(polar, POLAR)]
            pole[t * POLAR : (t + 1) * POLAR] = value
            if t < WITH_WEST:
                to_east[row_count + t * POLAR : row_count + (t + 1) * POLAR] = value
            else:
                pole_rest[(t - WITH_WEST) * POLAR : (t - WITH_WEST + 1) * POLAR] = value
    pl.when(goes_early())(
        lambda: own_work(
            lat_count, field, offset, part, flux, seam_index, seam_part, block_matrix, seam_matrix, own_matrix
        )
    )
    copies[3].wait()


def pole_places(south, row_count):
    places = (
        jnp.where(south, 0, row_count - POLE),
        jnp.where(south, POLAR, row_count - POLE),
        jnp.where(south, 0, row_count - POLAR),
        jnp.where(south, POLE, 0),
    )
    return [pl.multiple_of(place, 8) for place in places]


def by_place(lat_count, away, south, north):
    lat = lax.axis_index("lat")
    if away is not None:
        pl.when((lat > 0) & (lat < lat_count - 1))(away)
    pl.when(lat == 0)(south)
    pl.when(lat == lat_count - 1)(north)


def pieces(row_count):
    middle = [(POLE, row_count - 2 * POLE)] if row_count > 2 * POLE else []
    return [(0, POLE), *middle, (row_count - POLE, POLE)]


def mid_pieces(row_count):
    return pieces(row_count), pieces(row_count)[1:], pieces(row_count)[:-1]


def own_faces(first_row, count, field, offset, part, own_matrix, flux, seam_index, seam_part):
    depth, _, cells = field.shape
    at = pl.ds(first_row, count)
    shape = (count, cells)
    lane = lanes(shape)
    place = lane % SEG
    offsets = offset[at]
    courant = part[at]
    index = (lane - offsets - 1) & (cells - 1)
    own = field[:, at].reshape(depth * count, cells)
    tables = times(own, own_matrix[...])
    for t in range(depth):
        sums, right, left = split(tables[t * count : (t + 1) * count], cells)
        value = field[t, at]
        flux[t, at] = (
            sums
            - value
            - pick(sums, index)
            + parabola(
                courant, pick(right, index), pick(left, index), pick(value, index)
            )
        )
    first = (place - WEST) & (cells - 1)
    final = jnp.full(shape, cells - 1, i32)
    seam_index[0, at] = (lane - pick(offsets, first) - 1) & (cells - 1)
    seam_index[1, at] = (lane - pick(offsets, final) - 1) & (cells - 1)
    seam_part[0, at] = pick(courant, first)
    seam_part[1, at] = pick(courant, final)


def goes_early():
    lat, lon = lax.axis_index("lat"), lax.axis_index("lon")
    return (lon == 0) & (lat < 2)


def own_kernel(
    lat_count, field, offset, part, flux_given, index_given, part_given, block_given, seam_given,
    flux, seam_index, seam_part, block_matrix, seam_matrix, own_matrix,
):
    del flux_given, index_given, part_given, block_given, seam_given
    pl.when(~goes_early())(
        lambda: own_work(
            lat_count, field, offset, part, flux, seam_index, seam_part, block_matrix, seam_matrix, own_matrix
        )
    )


def own_work(
    lat_count, field, offset, part, flux, seam_index, seam_part, block_matrix, seam_matrix, own_matrix
):
    _, row_count, cells = field.shape
    shape = (cells, cells)
    source = lax.broadcasted_iota(i32, shape, 0)
    target = lax.broadcasted_iota(i32, shape, 1)
    gap = source - target
    upto = jnp.where(gap <= 0, 1.0, 0.0)
    right, left = edge_weights(gap)
    own = jnp.concatenate([upto, right, left, upto - 1.0], axis=1).astype(bf16)
    zeros = jnp.zeros(shape, f32)
    beyond = gap + jnp.where(source < cells // 2, cells, -cells)
    beside = jnp.concatenate([zeros, *edge_weights(beyond), zeros], axis=1).astype(bf16)
    together = source // SEG == target // SEG
    seam = jnp.concatenate([jnp.where(together, upto, 0.0), right, left], axis=1).astype(bf16)
    for i in range(2):
        block_matrix[2 * i * cells : (2 * i + 1) * cells] = own
        block_matrix[(2 * i + 1) * cells : (2 * i + 2) * cells] = beside
        own_matrix[i * cells : (i + 1) * cells] = own[:, : 3 * cells]
        seam_matrix[i * cells : (i + 1) * cells] = seam

    def step(parts):
        for first, count in parts:
            own_faces(first, count, field, offset, part, own_matrix, flux, seam_index, seam_part)

    by_place(lat_count, *(functools.partial(step, parts) for parts in mid_pieces(row_count)))


def rows_after(field, flux, packed, seam_index, seam_part, from_west, from_east, seam_matrix, parts):
    def take(ref, *lead):
        return jnp.concatenate([ref[(*lead, part)] for part in parts], axis=0)

    mine, west = take(packed), take(from_west)
    east = from_east if isinstance(from_east, jax.Array) else take(from_east)
    count, cells = mine.shape
    shape = mine.shape
    lane = lanes(shape)
    place = lane % SEG
    near = place < WEST
    rows = jnp.concatenate([jnp.where(near, west, mine), jnp.where(near, mine, east)], axis=0)
    next_face = place == WEST
    next_offset = pick(east, jnp.full(shape, OFF_LANE, i32)).astype(i32)
    next_part = pick(east, jnp.full(shape, FRAC_LANE, i32))
    next_index = (lane - next_offset - 1) & (cells - 1)
    index = jnp.concatenate(
        [take(seam_index, 0), jnp.where(next_face, next_index, take(seam_index, 1))], axis=0
    )
    courant = jnp.concatenate(
        [take(seam_part, 0), jnp.where(next_face, next_part, take(seam_part, 1))], axis=0
    )
    sums, right, left = split(times(rows, seam_matrix[...]), cells)
    faces = (
        sums
        - rows
        - pick(sums, index)
        + parabola(
            courant, pick(right, index), pick(left, index), pick(rows, index)
        )
    )
    east_faces = faces[count:]
    both = jnp.where(place == WEST - 1, east_faces, faces[:count])
    outside = (lane < FACES) | (lane == cells - 1)
    results = []
    for t in range(field.shape[0]):
        steps = -(t * SEG + WEST)
        face = jnp.where(outside, rolled(both, steps), take(flux, t))
        following = jnp.where(lane == cells - 1, rolled(east_faces, steps - 1), rolled(face, -1))
        results.append(take(field, t) - (following - face))
    return results


def edge_kernel(
    lat_count, field, flux, packed, seam_index, seam_part, seam_matrix, north, from_east, from_west,
    message_a, message_b, wide, east,
):
    depth, row_count, _ = field.shape
    half = row_count // 2
    even = lax.axis_index("lat") % 2 == 0

    def step(parts, beyond):
        return rows_after(
            field, flux, packed, seam_index, seam_part, from_west, beyond, seam_matrix, parts
        )

    def send(t, top, bottom):
        rows = slice(3 * t, 3 * t + 3)
        message_a[rows] = jnp.where(even, top, bottom)
        message_b[rows] = jnp.where(even, bottom, top)

    def away():
        beyond = jnp.concatenate(
            [from_east[:EDGE], rolled(from_east[half - EDGE :], -PAIR)], axis=0
        )
        after = step((pl.ds(0, EDGE), pl.ds(row_count - EDGE, EDGE)), beyond)
        for t in range(depth):
            send(t, after[t][2 * EDGE - 3 :], after[t][:3])

    def polar_device(parts):
        east[:half] = from_east[...]
        east[half:] = rolled(from_east[...], -PAIR)
        for first, count in parts:
            after = step((pl.ds(first, count),), east)
            for t in range(depth):
                wide[t, first : first + count] = after[t]
        for t in range(depth):
            send(t, wide[t, row_count - 3 :], wide[t, :3])

    by_place(
        lat_count, away, *(functools.partial(polar_device, parts) for parts in mid_pieces(row_count)[1:])
    )
    message_a[3 * depth : 3 * depth + 1] = north[:1]
    message_b[3 * depth : 3 * depth + 1] = north[:1]


def rows_between(near, far, near_field, far_field, first, offset, courant, next_offset, next_courant):
    cells = near_field.shape[1]
    lane = lanes(near_field.shape)
    source = lane - offset - 1
    index = source & (cells - 1)
    close = source >= first

    def both(here, there):
        return jnp.where(close, pick(here, index), pick(there, index))

    face = both(near[0], far[3]) - parabola(
        courant, both(near[1], far[1]), both(near[2], far[2]), both(near_field, far_field)
    )
    last = near[0] - parabola(next_courant, near[1], near[2], near_field)
    last = pick(last, (cells - 1 - next_offset) & (cells - 1))
    return rolled(jnp.where(lane == 0, last, face), -1) - face


def merid_flux(wide, t, courant, first, count):
    cell = [wide[t, first + k : first + k + count] for k in (-3, -2, -1, 0, 1)]
    left = 7.0 * (cell[1] + cell[2]) - (cell[0] + cell[3])
    right = 7.0 * (cell[2] + cell[3]) - (cell[1] + cell[4])
    return parabola(courant, right, left, cell[2])


def middle_kernel(
    lat_count, field, offset, part, north, flux, packed, seam_index, seam_part, seam_matrix, block_matrix,
    from_east, from_far, from_west, given_wide, given_east, wide, east, inner, far, faces,
):
    del given_wide, given_east
    depth, row_count, cells = field.shape
    half = row_count // 2
    far[:half] = from_far[...]
    far[half:] = rolled(from_far[...], -PAIR)

    def away():
        east[:half] = from_east[...]
        east[half:] = rolled(from_east[...], -PAIR)
        for first, count in pieces(row_count):
            after = rows_after(
                field, flux, packed, seam_index, seam_part, from_west, east, seam_matrix, (pl.ds(first, count),)
            )
            for t in range(depth):
                wide[t, first : first + count] = after[t]
        inner_rows(wide, north, faces, inner, EDGE, row_count - 2 * EDGE)

    def polar_device(south):
        band_step(south, field, offset, part, east, from_west, block_matrix, wide)
        first, _ = near_pole(south, row_count)
        inner_rows(
            wide, north, faces, inner, first + POLAR if south else EDGE, row_count - 2 * EDGE - POLAR
        )

    by_place(
        lat_count, away, functools.partial(polar_device, True), functools.partial(polar_device, False)
    )


def near_pole(south, row_count):
    return (EDGE, POLAR) if south else (row_count - EDGE - POLAR, POLAR)


def inner_rows(wide, north, faces, result, first, count):
    for t in range(wide.shape[0]):
        faces[t, :count] = merid_flux(wide, t, north[first : first + count], first, count)
        end = first + count
        faces[t, count : count + 1] = merid_flux(wide, t, north[end : end + 1], end, 1)
        result[t, first - EDGE : end - EDGE] = wide[t, first:end] - (
            faces[t, 1 : 1 + count] - faces[t, :count]
        )


def with_sides(west, own, east):
    beside = jnp.where(lanes(own.shape) < own.shape[1] // 2, east, west)
    return jnp.concatenate([own, beside], axis=1)


def unpacked(ref, rows, lane, depth):
    value = ref[rows]
    return jnp.concatenate([rolled(value, lane - t * SEG) for t in range(depth)], axis=0)


def stacked(ref, rows):
    return ref[:, rows, :].reshape(-1, ref.shape[2])


def row_values(offset, part, east, rows):
    beyond = east[rows]
    return (
        offset[rows],
        part[rows],
        pick(beyond, jnp.full(beyond.shape, OFF_LANE, i32)).astype(i32),
        pick(beyond, jnp.full(beyond.shape, FRAC_LANE, i32)),
    )


def band_step(south, field, offset, part, east, from_west, block_matrix, wide):
    depth, row_count, cells = field.shape
    base, band, _, mid = (int(place) for place in static_places(south, row_count))
    rows = pl.ds(band, BAND)
    own = stacked(field, rows)
    half = cells // 2
    pair = from_west[mid : mid + BAND], from_west[mid + BAND : mid + 2 * BAND]
    lane = lanes(pair[0].shape)
    rest = jnp.where(lane % SEG >= WEST, pair[0], rolled(pair[1], -WEST))
    west = []
    for t in range(depth):
        if t < depth - 1:
            value = from_west[base + t // 2 * BAND : base + (t // 2 + 1) * BAND]
            value = rolled(value, half) if t % 2 else value
        else:
            value = rolled(rest, cells - OFF_LANE)
        inner = jnp.where(lane >= half - 3, rolled(rest, half - 3 - 3 * t), 0.0)
        west.append(jnp.where(lane >= half, value, inner))
    west = jnp.concatenate(west, axis=0)
    beyond = unpacked(east, rows, -WEST, depth)
    tables = jnp.concatenate([with_sides(west, own, beyond), with_sides(west, west, own)], axis=0)
    tables = times(tables, block_matrix[...])
    common = row_values(offset, part, east, rows)
    for t in range(depth):
        at = slice(t * BAND, (t + 1) * BAND)
        both = [split(tables[first : first + BAND], cells) for first in (t * BAND, (depth + t) * BAND)]
        wide[t, rows] = rows_between(*both, own[at], west[at], 0, *common)


def static_places(south, row_count):
    return (0, POLAR, 0, POLE) if south else (row_count - POLE, row_count - POLE, row_count - POLAR, 0)


def edge_rows(lat_count, wide, north, message_b, message_a, low, high, result):
    depth, row_count, cells = wide.shape
    lat = lax.axis_index("lat")
    even = lat % 2 == 0
    south, top = lat == 0, lat == lat_count - 1
    end = 3 * depth
    north_courant = jnp.where(even, message_a[end : end + 1], message_b[end : end + 1])
    north_courant = jnp.where(top, 0.0, north_courant)
    first_row = lax.broadcasted_iota(i32, (EDGE, cells), 0)
    low_courant = jnp.where(south & (first_row == 0), 0.0, north[:EDGE])
    high_next = jnp.concatenate([north[row_count - EDGE + 1 :], north_courant], axis=0)
    for t in range(depth):
        rows = slice(3 * t, 3 * t + 3)
        from_a, from_b = message_a[rows], message_b[rows]
        low[t, EDGE - 3 : EDGE] = jnp.where(south, 0.0, jnp.where(even, from_b, from_a))
        low[t, EDGE : 3 * EDGE] = wide[t, : 2 * EDGE]
        high[t, : 2 * EDGE] = wide[t, row_count - 2 * EDGE :]
        high[t, 2 * EDGE : 2 * EDGE + 3] = jnp.where(top, 0.0, jnp.where(even, from_a, from_b))
    for t in range(depth):
        south_face = merid_flux(low, t, low_courant, EDGE, EDGE)
        north_face = merid_flux(low, t, north[1 : EDGE + 1], EDGE + 1, EDGE)
        result[0, t] = low[t, EDGE : 2 * EDGE] - (north_face - south_face)
        south_face = merid_flux(high, t, north[row_count - EDGE :], EDGE, EDGE)
        north_face = merid_flux(high, t, high_next, EDGE + 1, EDGE)
        result[1, t] = high[t, EDGE : 2 * EDGE] - (north_face - south_face)


def copy_edges(result, out, sems):
    row_count = out.shape[1]
    return [
        pltpu.make_async_copy(result.at[i], out.at[:, pl.ds(first, EDGE)], sems.at[i])
        for i, first in enumerate((0, row_count - EDGE))
    ]


def join_kernel(from_west, rest, after, joined):
    del after
    count = joined.shape[0] - rest.shape[0]
    joined[:count] = from_west[from_west.shape[0] - count :]
    joined[count:] = rest[...]


def poles_kernel(
    lat_count, field, offset, part, north, block_matrix, east, far, pole_one, pole_two, given_wide, given_inner,
    wide, inner, faces,
):
    del given_wide, given_inner

    def polar_device(south):
        depth, row_count, cells = field.shape
        rows = pl.ds(static_places(south, row_count)[2], POLAR)
        own, west, west_two = stacked(field, rows), pole_one[...], pole_two[...]
        beyond = unpacked(far, rows, cells - WEST, depth)
        tables = jnp.concatenate(
            [with_sides(west_two, west, own), with_sides(beyond, west_two, west)], axis=0
        )
        tables = times(tables, block_matrix[...])
        common = row_values(offset, part, east, rows)
        for t in range(depth):
            at = slice(t * POLAR, (t + 1) * POLAR)
            both = [split(tables[start : start + POLAR], cells) for start in (t * POLAR, (depth + t) * POLAR)]
            wide[t, rows] = rows_between(*both, west[at], west_two[at], -cells, *common)
        inner_rows(wide, north, faces, inner, *near_pole(south, row_count))

    by_place(
        lat_count, None, functools.partial(polar_device, True), functools.partial(polar_device, False)
    )


def last_kernel(
    lat_count, at_poles, wide, inner, north, message_b, message_a, given_out, out, low, high, result, sems
):
    del given_out

    def finish():
        count = inner.shape[1]
        inner_copy = pltpu.make_async_copy(inner, out.at[:, pl.ds(EDGE, count)], sems.at[2])
        inner_copy.start()
        edge_rows(lat_count, wide, north, message_b, message_a, low, high, result)
        copies = copy_edges(result, out, sems)
        for copy in copies:
            copy.start()
        for copy in (inner_copy, *copies):
            copy.wait()

    lat = lax.axis_index("lat")
    polar = (lat == 0) | (lat == lat_count - 1)
    pl.when(polar if at_poles else ~polar)(finish)


def poles_output_kernel(lat_count, wide, inner, north, message_b, message_a, out, *scratch):
    last_kernel(lat_count, True, wide, inner, north, message_b, message_a, None, out, *scratch)


def cost(microseconds):
    return pl.CostEstimate(
        flops=int(microseconds * 1e8), bytes_accessed=int(microseconds * 3e6), transcendentals=0
    )


def in_vmem(*values):
    return [pltpu.with_memory_space_constraint(value, VMEM) for value in values]


def whole(count):
    return [pl.BlockSpec(memory_space=VMEM)] * count


def anywhere(count):
    return [pl.BlockSpec(memory_space=pl.ANY)] * count


def on_device(lat_count, lon_count, tracers, offsets, fraction, courant_north):
    tracer_count, level_count, row_count, cells = tracers.shape
    depth = tracer_count * level_count
    shape = (row_count, cells)
    stack = (depth, row_count, cells)
    dma = pltpu.SemaphoreType.DMA

    def along_lon(value, steps, everywhere=True):
        pairs = []
        for l in range(lat_count):
            from_pole = min(l, lat_count - 1 - l)
            for o in range(lon_count):
                if everywhere or from_pole == 0 or lat_count % 2 or lon_count % 2:
                    target = (l, (o + steps) % lon_count)
                else:
                    target = (l, o ^ 1) if from_pole == 1 else (l ^ 1, o)
                pairs.append((l * lon_count + o, target[0] * lon_count + target[1]))
        return lax.ppermute(value, ("lat", "lon"), pairs)

    def along_lat(value, first):
        pairs = []
        last_lat, last_lon = lat_count - 1, lon_count - 1
        for l in range(lat_count):
            other = l + 1 if (l - first) % 2 == 0 else l - 1
            for o in range(lon_count):
                if 0 <= other < lat_count:
                    target = (other, o)
                elif lat_count % 2:
                    target = (l, (o + 1) % lon_count)
                elif l == 0:
                    target = (0, o - 1) if o else (last_lat, 0)
                else:
                    target = (last_lat, o + 1) if o < last_lon else (0, last_lon)
                pairs.append((l * lon_count + o, target[0] * lon_count + target[1]))
        return lax.ppermute(value, ("lat", "lon"), pairs)

    own_shapes = [
        VMEM(stack, f32),
        VMEM((2, *shape), i32),
        VMEM((2, *shape), f32),
        VMEM((4 * cells, 4 * cells), bf16),
        VMEM((2 * cells, 3 * cells), bf16),
    ]
    own_matrix = VMEM((2 * cells, 3 * cells), bf16)
    field, offset, part, north, packed, to_east, to_west, pole, pole_rest, *own = in_vmem(
        *pl.pallas_call(
            functools.partial(pack_kernel, lat_count),
            out_shape=[
                VMEM(stack, f32),
                VMEM(shape, i32),
                VMEM(shape, f32),
                VMEM(shape, f32),
                VMEM(shape, f32),
                VMEM((row_count + WITH_WEST * POLAR, cells), f32),
                VMEM((row_count // 2, cells), f32),
                VMEM((depth * POLAR, cells), f32),
                VMEM(((depth - WITH_WEST) * POLAR, cells), f32),
                *own_shapes,
            ],
            in_specs=anywhere(4),
            out_specs=whole(14),
            scratch_shapes=[own_matrix, dma((4,))],
            cost_estimate=cost(1.0),
            name="pack",
        )(tracers.reshape(stack), offsets, fraction, courant_north)
    )
    from_west = along_lon(to_east, 1)
    from_east = along_lon(to_west, -1)
    from_far = from_east if lon_count == 4 else along_lon(to_west, 3)
    pole_one = along_lon(pole_rest, 1, False)
    pole_two = along_lon(pole, 2, False)

    flux, seam_index, seam_part, block_matrix, seam_matrix = in_vmem(
        *pl.pallas_call(
            functools.partial(own_kernel, lat_count),
            out_shape=own_shapes,
            in_specs=whole(8),
            out_specs=whole(5),
            scratch_shapes=[own_matrix],
            input_output_aliases={3 + i: i for i in range(5)},
            cost_estimate=cost(2.0),
            name="own",
        )(field, offset, part, *own)
    )
    from_west, from_east, from_far, pole_one, pole_two = in_vmem(
        from_west, from_east, from_far, pole_one, pole_two
    )

    message = (3 * depth + 1, cells)
    longer = 24
    message_a, message_b, wide, east = in_vmem(
        *pl.pallas_call(
            functools.partial(edge_kernel, lat_count),
            out_shape=[VMEM(message, f32), VMEM((longer, cells), f32), VMEM(stack, f32), VMEM(shape, f32)],
            in_specs=whole(9),
            out_specs=whole(4),
            cost_estimate=cost(4.0),
            name="edge",
        )(field, flux, packed, seam_index, seam_part, seam_matrix, north, from_east, from_west)
    )
    message_a = along_lat(message_a, 0)
    message_b = along_lat(message_b, 1)

    inner = VMEM((depth, row_count - 2 * EDGE, cells), f32)
    faces = VMEM((depth, row_count - EDGE, cells), f32)
    wide, east, inner_part, far = in_vmem(
        *pl.pallas_call(
            functools.partial(middle_kernel, lat_count),
            out_shape=[VMEM(stack, f32), VMEM(shape, f32), inner, VMEM(shape, f32)],
            in_specs=whole(15),
            out_specs=whole(4),
            scratch_shapes=[faces],
            input_output_aliases={13: 0, 14: 1},
            cost_estimate=cost(0.0),
            name="middle",
        )(
            field, offset, part, north, flux, packed, seam_index, seam_part, seam_matrix, block_matrix,
            from_east, from_far, from_west, wide, east,
        )
    )

    pole_one = pl.pallas_call(
        join_kernel,
        out_shape=VMEM((depth * POLAR, cells), f32),
        in_specs=whole(3),
        out_specs=pl.BlockSpec(memory_space=VMEM),
        cost_estimate=cost(0.3),
        name="join",
    )(from_west, pole_one, far)
    (pole_one,) = in_vmem(pole_one)
    wide, inner = in_vmem(
        *pl.pallas_call(
            functools.partial(poles_kernel, lat_count),
            out_shape=[VMEM(stack, f32), inner],
            in_specs=whole(11),
            out_specs=whole(2),
            scratch_shapes=[faces],
            input_output_aliases={9: 0, 10: 1},
            cost_estimate=cost(0.0),
            name="poles",
        )(field, offset, part, north, block_matrix, east, far, pole_one, pole_two, wide, inner_part)
    )

    message_a, message_b = in_vmem(message_a, message_b)
    finish = dict(
        out_shape=jax.ShapeDtypeStruct(stack, f32),
        out_specs=pl.BlockSpec(memory_space=pl.ANY),
        scratch_shapes=[
            VMEM((depth, 3 * EDGE, cells), f32),
            VMEM((depth, 3 * EDGE, cells), f32),
            VMEM((2, depth, EDGE, cells), f32),
            dma((3,)),
        ],
    )
    polar_b = message_b if lat_count % 2 else message_a
    out = pl.pallas_call(
        functools.partial(poles_output_kernel, lat_count),
        in_specs=whole(5),
        cost_estimate=cost(0.0),
        name="poles_output",
        **finish,
    )(wide, inner, north, polar_b, message_a)
    out = pl.pallas_call(
        functools.partial(last_kernel, lat_count, False),
        in_specs=whole(5) + anywhere(1),
        input_output_aliases={5: 0},
        cost_estimate=cost(0.7),
        name="last",
        **finish,
    )(wide, inner, north, message_b, message_a, out)
    return out.reshape(tracers.shape)


def solution(mesh):
    placed = (P(None, None, "lat", "lon"), P("lat", "lon"), P("lat", "lon"), P("lat", "lon"))
    return jax.shard_map(
        functools.partial(on_device, mesh.shape["lat"], mesh.shape["lon"]),
        mesh=mesh,
        in_specs=placed,
        out_specs=P(None, None, "lat", "lon"),
        check_vma=False,
    )
```
